128 devices in a mesh: dp: 8 (over x, core), expert: 16 (over y, z).
Axes of the slice: x: 4, y: 4, z: 4, core: 2. Of those that a mesh axis runs over, the one named last changes fastest.
Arguments:
- upper_half: bfloat16 [16384, 2048], P(('dp', 'expert')), may hold values from -6 to 6
- lower_half: bfloat16 [16384, 2048], P(('dp', 'expert')), may hold values from -6 to 6
- upper_grad: bfloat16 [16384, 2048], P(('dp', 'expert')), may hold values from -6 to 6
- lower_grad: bfloat16 [16384, 2048], P(('dp', 'expert')), may hold values from -3 to 3
- expert_ids: int32 [16384, 6], P(('dp', 'expert')), may hold values from 0 to 31, as said below
- gate_weights: int32 [16384, 6], P(('dp', 'expert')), may hold values from 64 to 383
- route_slots: int32 [16384, 6], P(('dp', 'expert')), may hold values from 0 to 30, as said below
- expert_weight: bfloat16 [32, 2048, 2304], P('expert'), may hold values from -0.15625 to 0.15625
Outputs:
- upper_input: bfloat16 [16384, 2048], P(('dp', 'expert'))
- lower_input_grad: bfloat16 [16384, 2048], P(('dp', 'expert'))
- weight_grad: float32 [32, 2048, 2304], P('expert', 'dp')
The draws below stay inside these ranges and needn't reach their ends.
Inputs may be any that keep to these rules, and one draw needn't show every extreme that they name: `expert_ids`: each row names 6 different experts. `route_slots`: A route is live when its slot is below 30; a slot of 30 marks a route dropped for lack of room. Among the rows of one device, the live routes to one expert hold distinct slots. In every draw some expert has all 30 slots live from every device, and some route is dropped.
All inputs are finite; a program needn't handle non-finite values.
Results may differ from the reference program's by a relative error of at most 0.015.
Values may be sent and summed in bfloat16 or wider, within the bound.
A program may use at most 192 MiB of HBM per device.

```python
import jax
import jax.numpy as jnp
from jax import lax

D = 2048
H = 768
TOPK = 6
GATE_DENOM = 1024
TOK_DEV = 128
EXPERTS = 32
TOKENS = 16384
CAP = 30
N_DP = 8
N_EXPERT = 16


def route_table(key):
    folded = jax.random.fold_in(key, 11)
    subkeys = jax.random.split(folded, 5)
    blocks = TOKENS // TOK_DEV
    positions = jnp.arange(TOKENS, dtype=jnp.int32)
    experts_iota = jnp.arange(EXPERTS, dtype=jnp.int32)
    levels = jax.random.randint(subkeys[0], (EXPERTS,), 0, 4, dtype=jnp.int32) * 1024
    scores = jax.random.randint(subkeys[1], (TOKENS, EXPERTS), 0, 4096, dtype=jnp.int32) + levels[None, :]
    favored = jax.random.randint(subkeys[2], (), 0, EXPERTS, dtype=jnp.int32)
    shifts = jax.random.randint(subkeys[3], (blocks,), 0, TOK_DEV, dtype=jnp.int32)
    block_of = positions // TOK_DEV
    forced = (positions % TOK_DEV + shifts[block_of]) % TOK_DEV < CAP + 2
    boosted = jnp.where(forced[:, None] & (experts_iota[None, :] == favored), 1048576, 0)
    ranked = (scores + boosted) * EXPERTS + experts_iota[None, :]
    chosen = lax.top_k(ranked, TOPK)[1].astype(jnp.int32)
    flat_ids = chosen.reshape(blocks, TOK_DEV * TOPK)
    onehot = (flat_ids[:, :, None] == experts_iota[None, None, :]).astype(jnp.int32)
    ranking = jnp.sum((jnp.cumsum(onehot, axis=1) - 1) * onehot, axis=2)
    offsets = jax.random.randint(subkeys[4], (blocks, EXPERTS), 0, CAP, dtype=jnp.int32)
    offset_of = jnp.take_along_axis(offsets, flat_ids, axis=1)
    slot_table = jnp.where(ranking < CAP, (ranking + offset_of) % CAP, CAP)
    return (chosen, slot_table.reshape(TOKENS, TOPK).astype(jnp.int32))


def draw_expert_ids(key, part):
    return route_table(key)[0]


def draw_route_slots(key, part):
    return route_table(key)[1]


def plant(result, stream_key, least, largest):
    spot = [jax.random.randint(jax.random.fold_in(stream_key, axis), (), 0, length) for axis, length in enumerate(result.shape)]
    main_axis = result.shape.index(max(result.shape))
    neighbour = spot[:main_axis] + [(spot[main_axis] + 1) % result.shape[main_axis]] + spot[main_axis + 1:]
    return result.at[tuple(spot)].set(least).at[tuple(neighbour)].set(largest)


def block_scale(rng, shape, pieces, smallest, high):
    def one(axis_at, shards_of):
        draws = jax.random.uniform(jax.random.fold_in(jax.random.fold_in(rng, 6), axis_at), (shards_of,), jnp.float32, smallest / len(pieces), high / len(pieces))
        return jnp.repeat(jnp.exp(draws), shape[axis_at] // shards_of).reshape((-1,) + (1,) * (len(shape) - axis_at - 1))

    loudness = one(*pieces[0])
    for cut in pieces[1:]:
        loudness = loudness * one(*cut)
    return loudness


def normal_values(stream_key, dims, scale, limit, shards=(), kind=jnp.bfloat16):
    values = scale * jax.random.normal(stream_key, dims, jnp.float32)
    if shards:
        values = values * block_scale(stream_key, dims, shards, -0.22, 0.18)
    return jnp.clip(values, -limit, limit).astype(kind)


def setup_inputs(seed: int = 0) -> dict:
    key_of = jax.random.split(jax.random.key(seed), 9)
    upper_half = normal_values(key_of[0], (TOKENS, D), 1.0, 6.0, ((0, 128),))
    lower_half = normal_values(key_of[1], (TOKENS, D), 1.0, 6.0, ((0, 128),))
    upper_grad = normal_values(key_of[2], (TOKENS, D), 1.0, 6.0, ((0, 128),))
    lower_grad = normal_values(key_of[3], (TOKENS, D), 0.5, 3.0, ((0, 128),))
    expert_ids = draw_expert_ids(jax.random.fold_in(key_of[8], 71), 0)
    gate_weights = plant(jax.random.randint(key_of[5], (TOKENS, TOPK), 64, 384), jax.random.fold_in(key_of[5], 1), 64, 383).astype(jnp.int32)
    route_slots = draw_route_slots(jax.random.fold_in(key_of[8], 71), 0)
    expert_weight = normal_values(key_of[7], (EXPERTS, D, 3 * H), ((D + H) // 2) ** -0.5, 0.15625, ((0, 16),))
    return {"upper_half": upper_half, "lower_half": lower_half, "upper_grad": upper_grad, "lower_grad": lower_grad, "expert_ids": expert_ids, "gate_weights": gate_weights, "route_slots": route_slots, "expert_weight": expert_weight}


norm_eps = 1e-06

def reference(upper_half, lower_half, upper_grad, lower_grad, expert_ids, gate_weights, route_slots, expert_weight):
    blocks = N_DP * N_EXPERT
    slots_total = blocks * EXPERTS * CAP
    group_rows = N_EXPERT * CAP
    block_of = (jnp.arange(TOKENS, dtype=jnp.int32) // TOK_DEV).astype(jnp.int32)
    kept_routes = route_slots < CAP
    flat_index = jnp.where(kept_routes, (block_of[:, None] * EXPERTS + expert_ids) * CAP + route_slots, slots_total).astype(jnp.int32)
    lower_float = lower_half.astype(jnp.float32)
    upper_float = upper_grad.astype(jnp.float32)
    norm_scale = lax.rsqrt(lax.optimization_barrier(jnp.mean(lower_float * lower_float, axis=1, keepdims=True)) + norm_eps)
    normed = (lower_float * norm_scale).astype(jnp.bfloat16)
    shares = gate_weights.astype(jnp.float32) / GATE_DENOM
    normed_buffer = jnp.zeros((slots_total, D), jnp.bfloat16)
    scaled_buffer = jnp.zeros((slots_total, D), jnp.bfloat16)
    for column in range(TOPK):
        normed_buffer = normed_buffer.at[flat_index[:, column]].set(normed, mode='drop')
        scaled_rows = (shares[:, column:column + 1] * upper_float).astype(jnp.bfloat16)
        scaled_buffer = scaled_buffer.at[flat_index[:, column]].set(scaled_rows, mode='drop')

    def by_expert(buffer):
        return buffer.reshape(N_DP, N_EXPERT, EXPERTS, CAP, D).transpose(2, 0, 1, 3, 4).reshape(EXPERTS, N_DP, group_rows, D)

    def by_slot(stacked):
        return stacked.reshape(EXPERTS, N_DP, N_EXPERT, CAP, D).transpose(1, 2, 0, 3, 4).reshape(slots_total, D)

    def one_expert(packed):
        normed_rows, scaled_rows, weight = packed
        flat_normed = normed_rows.reshape(N_DP * group_rows, D)
        flat_scaled = scaled_rows.reshape(N_DP * group_rows, D)
        gate_up = jnp.dot(flat_normed, weight[:, :2 * H], preferred_element_type=jnp.float32)
        gate_part = gate_up[:, :H]
        up_part = gate_up[:, H:]
        sigmoid_gate = jax.nn.sigmoid(gate_part)
        hidden = (gate_part * sigmoid_gate * up_part).astype(jnp.bfloat16)
        output = jnp.dot(hidden, weight[:, 2 * H:].T, preferred_element_type=jnp.float32).astype(jnp.bfloat16)
        grad_hidden = jnp.dot(flat_scaled, weight[:, 2 * H:], preferred_element_type=jnp.float32)
        grad_gate = grad_hidden * up_part * sigmoid_gate * (1.0 + gate_part * (1.0 - sigmoid_gate))
        grad_up = grad_hidden * gate_part * sigmoid_gate
        grad_gate_up = jnp.concatenate([grad_gate, grad_up], axis=1).astype(jnp.bfloat16)
        grad_input = jnp.dot(grad_gate_up, weight[:, :2 * H].T, preferred_element_type=jnp.float32).astype(jnp.bfloat16)
        upper_part = jnp.einsum('pmd,pmf->pdf', normed_rows.astype(jnp.float32), grad_gate_up.reshape(N_DP, group_rows, 2 * H).astype(jnp.float32))
        lower_part = jnp.einsum('pmd,pmh->pdh', scaled_rows.astype(jnp.float32), hidden.reshape(N_DP, group_rows, H).astype(jnp.float32))
        partial_value = jnp.concatenate([upper_part, lower_part], axis=2)
        rounded = lax.optimization_barrier(partial_value.astype(jnp.bfloat16))
        weight_grad = lax.optimization_barrier(jnp.sum(rounded.astype(jnp.float32), axis=0))
        return (output.reshape(N_DP, group_rows, D), grad_input.reshape(N_DP, group_rows, D), weight_grad)
    outputs, grad_inputs, weight_grad = lax.map(one_expert, (by_expert(normed_buffer), by_expert(scaled_buffer), expert_weight))
    output_flat = by_slot(outputs)
    input_flat = by_slot(grad_inputs)
    mixture = jnp.zeros((TOKENS, D), jnp.float32)
    grad_normed = jnp.zeros((TOKENS, D), jnp.float32)
    for column in range(TOPK):
        taken = jnp.take(output_flat, flat_index[:, column], axis=0, mode='fill', fill_value=0)
        mixture = mixture + shares[:, column:column + 1] * taken.astype(jnp.float32)
        grad_taken = jnp.take(input_flat, flat_index[:, column], axis=0, mode='fill', fill_value=0)
        grad_normed = grad_normed + grad_taken.astype(jnp.float32)
    upper_input = (upper_half.astype(jnp.float32) - mixture).astype(jnp.bfloat16)
    inner_mean = lax.optimization_barrier(jnp.mean(lower_float * grad_normed, axis=1, keepdims=True))
    cubed = norm_scale * norm_scale * norm_scale
    lower_input_grad = (lower_grad.astype(jnp.float32) + norm_scale * grad_normed - lower_float * cubed * inner_mean).astype(jnp.bfloat16)
    return (upper_input, lower_input_grad, weight_grad)
```

```python
import functools

import jax
import jax.numpy as jnp
from jax import lax
from jax.experimental import pallas as pl
from jax.experimental.pallas import tpu as pltpu
from jax.sharding import PartitionSpec as P

MESH = pl.DeviceIdType.MESH
F32 = jnp.float32
BF16 = jnp.bfloat16

GATE_DENOM = 1024
NORM_EPS = 1e-06
T = 128
D = 2048
H = 768
F = 3 * H
TOPK = 6
CAP = 30
S = 32
M = 16 * S
RING = 4
SHARE = D // 8


def dot_nt(a, b):
    return lax.dot_general(a, b, (((1,), (1,)), ((), ())), preferred_element_type=F32)


def dot_tn(a, b):
    return lax.dot_general(a, b, (((0,), (0,)), ((), ())), preferred_element_type=F32)


def dot_nn(a, b):
    return lax.dot_general(a, b, (((1,), (0,)), ((), ())), preferred_element_type=F32)


def kernel(
    uh, lh, ug, lg, rt, w_hbm,
    o_up, o_lo, o_own, o_left, o_right,
    AG, RT, SD, R, O1, W, G, PX, PG, OWN, TMP, FL, FR, FT,
    ag_s, ag_r, agf_s, agf_r, rt_s, rt_r, s2_s, s2_r, rb_s, rb_r,
    px_s, px_r, pg_s, pg_r, x_s, x_r, fn_s, fn_r, loc, w_sem, credit, pcredit,
):
    dp = lax.axis_index("dp")
    ex = lax.axis_index("expert")
    x, c = dp // 2, dp % 2
    y, z = ex // RING, ex % RING
    a_me = (y, z)
    b_me = (z, y)

    def ydev(k):
        return (dp, ((y + k) % RING) * RING + z)

    def zdev(k):
        return (dp, y * RING + (z + k) % RING)

    def xdev(k):
        return (((x + k) % RING) * 2 + c, ex)

    a_dev = (ydev, zdev)
    b_dev = (zdev, ydev)
    partner = (x * 2 + 1 - c, ex)

    def rcopy(src, dst, ss, rs, dev):
        return pltpu.make_async_remote_copy(
            src_ref=src, dst_ref=dst, send_sem=ss, recv_sem=rs, device_id=dev, device_id_type=MESH
        )

    def load_w(j):
        return pltpu.make_async_copy(w_hbm.at[j], W, w_sem)

    load_w(0).start()

    barrier = pltpu.get_barrier_semaphore()
    peers = [ydev(k) for k in (1, 2, 3)] + [zdev(k) for k in (1, 2, 3)] + [xdev(1), xdev(3), partner]
    for dev in peers:
        pl.semaphore_signal(barrier, inc=1, device_id=dev, device_id_type=MESH)

    for p in (0, 1):
        RT[p, a_me[p]] = rt[...]
    AG[1, z] = ug[...]
    low = lh[...].astype(F32)
    scale = lax.rsqrt(jnp.mean(low * low, axis=1, keepdims=True) + NORM_EPS)
    AG[0, y] = (low * scale).astype(BF16)

    pl.semaphore_wait(barrier, len(peers))

    HALF = T // 2

    def rows(h):
        return pl.ds(h * HALF, HALF)

    def rt_copy(p, k):
        me = a_me[p]
        return rcopy(RT.at[p, me], RT.at[p, me], rt_s.at[p, k], rt_r.at[p, k], a_dev[p](k))

    def ag_copy(p, d, h):
        me = a_me[p]
        blk = AG.at[p, me, rows(h)]
        return rcopy(blk, blk, ag_s.at[p, d, h], ag_r.at[p, d, h], a_dev[p](1 if d == 0 else 3))

    def agf_copy(p, d):
        frm = (a_me[p] + (3 if d == 0 else 1)) % RING
        blk = AG.at[p, frm, rows(d)]
        return rcopy(blk, blk, agf_s.at[p, d], agf_r.at[p, d], a_dev[p](1 if d == 0 else 3))

    for p in (1, 0):
        for k in (1, 2, 3):
            rt_copy(p, k).start()
    for p in (1, 0):
        ag_copy(p, 0, 0).start()
        ag_copy(p, 1, 1).start()
    for p in (1, 0):
        ag_copy(p, 0, 1).start()
        ag_copy(p, 1, 0).start()

    row = lax.broadcasted_iota(jnp.int32, (T, T), 0)

    def codes_of(p, j):
        b, s = row >> 5, row & 31
        if p == 0:
            return 64 * (4 * y + b) + 32 * j + s
        return 64 * (4 * b + z) + 32 * j + s

    def onehot(p, j, a):
        val = codes_of(p, j)
        hot = jnp.zeros((T, T), F32)
        share = jnp.zeros((T, T), F32)
        for k in range(TOPK):
            m = RT[p, a, k : k + 1, :] == val
            hot = jnp.where(m, 1.0, hot)
            gate = RT[p, a, 8 + k : 9 + k, :].astype(F32) * (1.0 / GATE_DENOM)
            share = jnp.where(m, gate, share)
        return hot, share

    def gather(p, j, a):
        hot, share = onehot(p, j, a)
        hot = hot.astype(BF16)
        for n in range(4):
            cols = pl.ds(n * 512, 512)
            picked = dot_nn(hot, AG[p, a, :, cols])
            if p == 1:
                picked = picked * jnp.sum(share, axis=1, keepdims=True)
            SD[p, j, a, :, cols] = picked.astype(BF16)

    def r_rows(p, a):
        block = a * RING + z if p == 0 else y * RING + a
        return pl.ds(pl.multiple_of(block * S, S), S)

    def r_rows_of(p, a, b):
        block = a * RING + b if p == 0 else b * RING + a
        return pl.ds(pl.multiple_of(block * S, S), S)

    def slots(b):
        return pl.ds(pl.multiple_of(b * S, S), S)

    def s2_send(p, j, a):
        for k in (1, 2, 3):
            b = (b_me[p] + k) % RING
            rcopy(
                SD.at[p, j, a, slots(b)], R.at[p, j, r_rows(p, a)],
                s2_s.at[p, j, k], s2_r.at[p, j, k], b_dev[p](k),
            ).start()
        pltpu.make_async_copy(
            SD.at[p, j, a, slots(b_me[p])], R.at[p, j, r_rows(p, a)], loc.at[p, j]
        ).start()

    def s2_whole(p, j, k):
        return rcopy(SD.at[p, j, 0], R.at[p, j, pl.ds(0, T)], s2_s.at[p, j, k], s2_r.at[p, j, k], b_dev[p](k))

    def loc_whole(p, j):
        return pltpu.make_async_copy(SD.at[p, j, 0], R.at[p, j, pl.ds(0, T)], loc.at[p, j])

    for p in (1, 0):
        gather(p, 0, a_me[p])
        s2_send(p, 0, a_me[p])
    for p in (1, 0):
        ag_copy(p, 0, 0).wait_recv()
        agf_copy(p, 0).start()
        ag_copy(p, 1, 1).wait_recv()
        agf_copy(p, 1).start()
    for p in (1, 0):
        for k in (1, 2, 3):
            rt_copy(p, k).wait_recv()
    for p in (1, 0):
        ag_copy(p, 0, 1).wait_recv()
        gather(p, 0, (a_me[p] + 3) % RING)
        s2_send(p, 0, (a_me[p] + 3) % RING)
        ag_copy(p, 1, 0).wait_recv()
        gather(p, 0, (a_me[p] + 1) % RING)
        s2_send(p, 0, (a_me[p] + 1) % RING)
    for p in (1, 0):
        agf_copy(p, 0).wait_recv()
        agf_copy(p, 1).wait_recv()
        gather(p, 0, (a_me[p] + 2) % RING)
        s2_send(p, 0, (a_me[p] + 2) % RING)

    def gather_later(a, carry):
        for p in (1, 0):
            gather(p, 1, a)
        return carry

    lax.fori_loop(0, RING, gather_later, 0)
    for p in (1, 0):
        for k in (1, 2, 3):
            rt_copy(p, k).wait_send()
        for d in (0, 1):
            for h in (0, 1):
                ag_copy(p, d, h).wait_send()
            agf_copy(p, d).wait_send()

    def s2_sent(j):
        for p in (0, 1):
            for k in (1, 2, 3):
                s2_whole(p, j, k).wait_send()
            loc_whole(p, j).wait()
        for p in (0, 1):
            for k in (1, 2, 3):
                pl.semaphore_signal(credit.at[j], inc=1, device_id=b_dev[p](k), device_id_type=MESH)

    s2_sent(0)

    def send_later(a, carry):
        for p in (1, 0):
            s2_send(p, 1, a)
        return carry

    lax.fori_loop(0, RING, send_later, 0)

    def px_copy(p, j, b):
        src = R.at[p, j, :, pl.ds(pl.multiple_of(b * 512 + (1 - c) * SHARE, SHARE), SHARE)]
        return rcopy(src, PX.at[p, :, pl.ds(b * SHARE, SHARE)], px_s.at[p], px_r.at[p], partner)

    def px_whole(p):
        half = R.at[p, 0, :, pl.ds(0, 4 * SHARE)]
        return rcopy(half, PX.at[p], px_s.at[p], px_r.at[p], partner)

    def pg_copy(cols):
        return rcopy(G.at[:, cols], PG.at[:, cols], pg_s, pg_r, partner)

    pg_whole = rcopy(G, PG, pg_s, pg_r, partner)

    def hidden_part(j):
        for p in (0, 1):
            for k in (1, 2, 3):
                s2_whole(p, j, k).wait_recv()
        if j == 1:
            pl.semaphore_wait(pcredit, 1)
        for p in (0, 1):
            for b in range(RING):
                px_copy(p, j, b).start()
        load_w(j).wait()

        def tile(n, carry):
            at = [pl.ds(pl.multiple_of(i * H + n * 256, 256), 256) for i in range(3)]
            gate = dot_nn(R[0, j], W[:, at[0]])
            up = dot_nn(R[0, j], W[:, at[1]])
            grad = dot_nn(R[1, j], W[:, at[2]])
            sig = jax.nn.sigmoid(gate)
            act = gate * sig
            G[:, at[2]] = (act * up).astype(BF16)
            G[:, at[0]] = (grad * up * sig * (1.0 + gate * (1.0 - sig))).astype(BF16)
            G[:, at[1]] = (grad * act).astype(BF16)
            for i in range(3):
                pg_copy(at[i]).start()
            return carry

        lax.fori_loop(0, 3, tile, 0)

    def outputs_part(j, out, route):
        def tile(n, carry):
            at = pl.ds(pl.multiple_of(n * 256, 256), 256)
            out[:, at] = dot_nt(G[:, 2 * H :], W[at, 2 * H :]).astype(BF16)
            route[:, at] = dot_nt(G[:, : 2 * H], W[at, : 2 * H]).astype(BF16)
            return carry

        lax.fori_loop(0, D // 256, tile, 0)

    def weight_block(j, b, dst):
        mine = pl.ds(pl.multiple_of(b * 512 + c * SHARE, SHARE), SHARE)
        theirs = pl.ds(pl.multiple_of(b * SHARE, SHARE), SHARE)

        def tile(p, first, count):
            def body(n, carry):
                at = pl.ds(pl.multiple_of(first + n * 256, 256), 256)
                acc = dot_tn(R[p, j, :, mine], G[:, at])
                acc = acc + dot_tn(PX[p, :, theirs], PG[:, at])
                dst[:, at] = acc.astype(BF16)
                return carry

            lax.fori_loop(0, count, body, 0)

        tile(0, 0, 6)
        tile(1, 2 * H, 3)

    AH = pl.ds(0, SHARE // 2)
    BH = pl.ds(SHARE // 2, SHARE // 2)

    def x_copy(j, own, d, i):
        to = xdev(1 if d == 0 else 3)
        near = own((x + (1 if d == 0 else 3)) % RING)
        far = own((x + 2) % RING)
        fin = o_left if d == 0 else o_right
        early, late = (AH, BH) if d == 0 else (BH, AH)
        if i == 0:
            src, dst = far.at[early], TMP.at[j, d]
        elif i == 1:
            src, dst = near.at[late], fin.at[j, late]
        else:
            src, dst = near.at[early], fin.at[j, early]
        return rcopy(src, dst, x_s.at[j, d, i], x_r.at[j, d, i], to)

    def own_copy(j, own):
        return pltpu.make_async_copy(own(x), o_own.at[j], w_sem)

    def weight_part(j, own):
        for p in (0, 1):
            px_whole(p).wait_recv()
        pg_whole.wait_recv()
        weight_block(j, (x + 2) % RING, own((x + 2) % RING))
        x_copy(j, own, 0, 0).start()
        x_copy(j, own, 1, 0).start()
        weight_block(j, (x + 1) % RING, own((x + 1) % RING))
        x_copy(j, own, 0, 1).start()
        weight_block(j, (x + 3) % RING, own((x + 3) % RING))
        x_copy(j, own, 1, 1).start()
        weight_block(j, x, own(x))
        if j == 0:
            pl.semaphore_signal(pcredit, inc=1, device_id=partner, device_id_type=MESH)

    def partner_sent():
        for p in (0, 1):
            px_whole(p).wait_send()
        pg_whole.wait_send()

    def x_add(j, own):
        for d in (0, 1):
            early = AH if d == 0 else BH
            near = own((x + (1 if d == 0 else 3)) % RING)
            x_copy(j, own, d, 0).wait_recv()
            near[early, :] = (near[early, :].astype(F32) + TMP[j, d].astype(F32)).astype(BF16)
            x_copy(j, own, d, 2).start()

    def x_done(j, own):
        for d in (0, 1):
            for i in (1, 2):
                x_copy(j, own, d, i).wait_recv()
            for i in range(3):
                x_copy(j, own, d, i).wait_send()

    def own0(b):
        return OWN.at[b]

    def own1(b):
        return W.at[pl.ds(pl.multiple_of(b * SHARE, SHARE), SHARE)]

    def back(j, bufs):
        pl.semaphore_wait(credit.at[j], 6)
        for p in (0, 1):
            for k in (1, 2, 3):
                b = (b_me[p] + k) % RING
                for a in range(RING):
                    rcopy(
                        bufs[p].at[r_rows_of(p, a, b)], SD.at[p, j, a, slots(b_me[p])],
                        rb_s.at[p, j, k], rb_r.at[p, j, k], b_dev[p](k),
                    ).start()
            for a in range(RING):
                pltpu.make_async_copy(
                    bufs[p].at[r_rows(p, a)], SD.at[p, j, a, slots(b_me[p])], loc.at[p, j]
                ).start()

    def back_whole(p, j, k, bufs):
        return rcopy(
            bufs[p].at[pl.ds(0, T)], SD.at[p, j, 0], rb_s.at[p, j, k], rb_r.at[p, j, k], b_dev[p](k)
        )

    bufs0 = (R.at[0, 0], R.at[1, 0])
    bufs1 = (O1.at[0], O1.at[1])

    hidden_part(0)
    weight_part(0, own0)
    partner_sent()
    outputs_part(0, bufs0[0], bufs0[1])
    load_w(1).start()
    back(0, bufs0)
    s2_sent(1)
    hidden_part(1)
    x_add(0, own0)
    outputs_part(1, bufs1[0], bufs1[1])
    back(1, bufs1)
    weight_part(1, own1)
    partner_sent()
    own_copy(0, own0).start()
    own_copy(0, own0).wait()
    own_copy(1, own1).start()

    def fn_copy(p, d, i):
        to = a_dev[p](1 if d == 0 else 3)
        near = (a_me[p] + (1 if d == 0 else 3)) % RING
        far = (a_me[p] + 2) % RING
        fin = FL if d == 0 else FR
        early, late = rows(d), rows(1 - d)
        if i == 0:
            src, dst = AG.at[p, far, early], FT.at[p, d]
        elif i == 1:
            src, dst = AG.at[p, near, late], fin.at[p, late]
        else:
            src, dst = AG.at[p, near, early], fin.at[p, early]
        return rcopy(src, dst, fn_s.at[p, d, i], fn_r.at[p, d, i], to)

    def combine(p, a):
        parts = []
        for j in (0, 1):
            hot, share = onehot(p, j, a)
            if p == 0:
                top = share.astype(BF16)
                parts.append((j, top))
                parts.append((j, (share - top.astype(F32)).astype(BF16)))
            else:
                parts.append((j, hot.astype(BF16)))
        for n in range(4):
            cols = pl.ds(n * 512, 512)
            total = jnp.zeros((T, 512), F32)
            for j, weights in parts:
                total = total + dot_tn(weights, SD[p, j, a, :, cols])
            AG[p, a, :, cols] = total.astype(BF16)

    for p in (0, 1):
        for j, bufs in ((0, bufs0), (1, bufs1)):
            for k in (1, 2, 3):
                back_whole(p, j, k, bufs).wait_recv()
            loc_whole(p, j).wait()
        combine(p, (a_me[p] + 2) % RING)
        fn_copy(p, 0, 0).start()
        fn_copy(p, 1, 0).start()
        combine(p, (a_me[p] + 1) % RING)
        fn_copy(p, 0, 1).start()
        combine(p, (a_me[p] + 3) % RING)
        fn_copy(p, 1, 1).start()
    for p in (0, 1):
        combine(p, a_me[p])
    for p in (0, 1):
        for d in (0, 1):
            near = (a_me[p] + (1 if d == 0 else 3)) % RING
            early = rows(d)
            fn_copy(p, d, 0).wait_recv()
            AG[p, near, early, :] = (
                AG[p, near, early, :].astype(F32) + FT[p, d].astype(F32)
            ).astype(BF16)
            fn_copy(p, d, 2).start()

    x_add(1, own1)

    for p in (0, 1):
        for d in (0, 1):
            for i in (1, 2):
                fn_copy(p, d, i).wait_recv()
    mixture = AG[0, y].astype(F32) + FL[0].astype(F32) + FR[0].astype(F32)
    o_up[...] = (uh[...].astype(F32) - mixture).astype(BF16)
    grad_normed = AG[1, z].astype(F32) + FL[1].astype(F32) + FR[1].astype(F32)
    low = lh[...].astype(F32)
    scale = lax.rsqrt(jnp.mean(low * low, axis=1, keepdims=True) + NORM_EPS)
    inner = jnp.mean(low * grad_normed, axis=1, keepdims=True)
    o_lo[...] = (
        lg[...].astype(F32) + scale * grad_normed - low * (scale * scale * scale) * inner
    ).astype(BF16)

    for p in (0, 1):
        for d in (0, 1):
            for i in range(3):
                fn_copy(p, d, i).wait_send()
        for j, bufs in ((0, bufs0), (1, bufs1)):
            for k in (1, 2, 3):
                back_whole(p, j, k, bufs).wait_send()
    own_copy(1, own1).wait()
    x_done(0, own0)
    x_done(1, own1)


def run(upper_half, lower_half, upper_grad, lower_grad, routes, expert_weight):
    vm = pl.BlockSpec(memory_space=pltpu.VMEM)
    hbm = pl.BlockSpec(memory_space=pl.ANY)
    dma = pltpu.SemaphoreType.DMA
    half = jax.ShapeDtypeStruct((2, SHARE, F), BF16)
    rows = jax.ShapeDtypeStruct((T, D), BF16)
    return pl.pallas_call(
        kernel,
        out_shape=(rows, rows, half, half, half),
        in_specs=[vm, vm, vm, vm, vm, hbm],
        out_specs=(vm, vm, hbm, hbm, hbm),
        scratch_shapes=[
            pltpu.VMEM((2, RING, T, D), BF16),
            pltpu.VMEM((2, RING, 16, T), jnp.int32),
            pltpu.VMEM((2, 2, RING, T, D), BF16),
            pltpu.VMEM((2, 2, M, D), BF16),
            pltpu.VMEM((2, M, D), BF16),
            pltpu.VMEM((D, F), BF16),
            pltpu.VMEM((M, F), BF16),
            pltpu.VMEM((2, M, 4 * SHARE), BF16),
            pltpu.VMEM((M, F), BF16),
            pltpu.VMEM((RING, SHARE, F), BF16),
            pltpu.VMEM((2, 2, SHARE // 2, F), BF16),
            pltpu.VMEM((2, T, D), BF16),
            pltpu.VMEM((2, T, D), BF16),
            pltpu.VMEM((2, 2, T // 2, D), BF16),
            dma((2, 2, 2)), dma((2, 2, 2)),
            dma((2, 2)), dma((2, 2)),
            dma((2, 4)), dma((2, 4)),
            dma((2, 2, 4)), dma((2, 2, 4)),
            dma((2, 2, 4)), dma((2, 2, 4)),
            dma((2,)), dma((2,)),
            dma, dma,
            dma((2, 2, 3)), dma((2, 2, 3)),
            dma((2, 2, 3)), dma((2, 2, 3)),
            dma((2, 2)),
            dma,
            pltpu.SemaphoreType.REGULAR((2,)),
            pltpu.SemaphoreType.REGULAR,
        ],
        compiler_params=pltpu.CompilerParams(
            collective_id=0, has_side_effects=True, vmem_limit_bytes=61 * 1024 * 1024
        ),
        cost_estimate=pl.CostEstimate(
            flops=29_000_000_000, bytes_accessed=30_000_000, transcendentals=800_000
        ),
    )(upper_half, lower_half, upper_grad, lower_grad, routes, expert_weight)


def shards(
    upper_half, lower_half, upper_grad, lower_grad, expert_ids, gate_weights, route_slots, expert_weight
):
    code = jnp.where(route_slots < CAP, expert_ids * S + route_slots, -1)
    pad = ((0, 0), (0, 8 - TOPK))
    routes = jnp.concatenate(
        [jnp.pad(code, pad, constant_values=-1), jnp.pad(gate_weights, pad)], axis=1
    ).T
    up, lo, own, left, right = run(
        upper_half, lower_half, upper_grad, lower_grad, routes, expert_weight
    )
    weight_grad = own.astype(F32) + left.astype(F32) + right.astype(F32)
    return up, lo, weight_grad


def solution(mesh):
    tok = P(("dp", "expert"), None)
    return jax.shard_map(
        shards,
        mesh=mesh,
        in_specs=(tok,) * 7 + (P("expert", None, None),),
        out_specs=(tok, tok, P("expert", "dp", None)),
        check_vma=False,
    )
```

```python
import functools

import jax
import jax.numpy as jnp
from jax import lax
from jax.experimental import pallas as pl
from jax.experimental.pallas import tpu as pltpu
from jax.sharding import PartitionSpec as P

MESH = pl.DeviceIdType.MESH
F32 = jnp.float32
BF16 = jnp.bfloat16

GATE_DENOM = 1024
NORM_EPS = 1e-06
T = 128
D = 2048
H = 768
F = 3 * H
TOPK = 6
CAP = 30
S = 32
M = 16 * S
RING = 4
SHARE = D // 8


def dot_nt(a, b):
    return lax.dot_general(a, b, (((1,), (1,)), ((), ())), preferred_element_type=F32)


def dot_tn(a, b):
    return lax.dot_general(a, b, (((0,), (0,)), ((), ())), preferred_element_type=F32)


def dot_nn(a, b):
    return lax.dot_general(a, b, (((1,), (0,)), ((), ())), preferred_element_type=F32)


def kernel(
    uh_in, lh_in, ug_in, lg_in, ids_in, gates_in, slots_in, w_hbm,
    o_up, o_lo, o_own, o_left, o_right,
    uh, lh, lg, ids, gates, slots_of, AG, RT, SD, R, O, W, G, PX, PG, OWN, TMP, FL, FR, FT,
    ag_s, ag_r, agf_s, agf_r, rt_s, rt_r, s2_s, s2_r, rb_s, rb_r,
    px_s, px_r, pg_s, pg_r, x_s, x_r, fn_s, fn_r, loc, loc_b, w_sem, in_sem, credit, pcredit,
):
    dp = lax.axis_index("dp")
    ex = lax.axis_index("expert")
    x, c = dp // 2, dp % 2
    y, z = ex // RING, ex % RING
    a_me = (y, z)
    b_me = (z, y)

    def ydev(k):
        return (dp, ((y + k) % RING) * RING + z)

    def zdev(k):
        return (dp, y * RING + (z + k) % RING)

    def xdev(k):
        return (((x + k) % RING) * 2 + c, ex)

    a_dev = (ydev, zdev)
    b_dev = (zdev, ydev)
    partner = (x * 2 + 1 - c, ex)

    def rcopy(src, dst, ss, rs, dev):
        return pltpu.make_async_remote_copy(
            src_ref=src, dst_ref=dst, send_sem=ss, recv_sem=rs, device_id=dev, device_id_type=MESH
        )

    def load_w(j):
        return pltpu.make_async_copy(w_hbm.at[j], W, w_sem)

    barrier = pltpu.get_barrier_semaphore()
    peers = [ydev(k) for k in (1, 2, 3)] + [zdev(k) for k in (1, 2, 3)] + [xdev(1), xdev(3), partner]
    for dev in peers:
        pl.semaphore_signal(barrier, inc=1, device_id=dev, device_id_type=MESH)

    pairs = (
        (lh_in, lh), (ug_in, AG.at[1, z]), (ids_in, ids), (gates_in, gates), (slots_in, slots_of),
        (uh_in, uh), (lg_in, lg),
    )
    loads = [pltpu.make_async_copy(src, dst, in_sem.at[i]) for i, (src, dst) in enumerate(pairs)]
    for load in loads:
        load.start()
    load_w(0).start()
    for i in (2, 3, 4):
        loads[i].wait()
    for p in (0, 1):
        RT[p, a_me[p], 0:TOPK, :] = jnp.where(slots_of[...] < CAP, ids[...] * S + slots_of[...], -1)
        RT[p, a_me[p], 8 : 8 + TOPK, :] = gates[...]
    loads[0].wait()
    low = lh[...].astype(F32)
    scale = lax.rsqrt(jnp.mean(low * low, axis=1, keepdims=True) + NORM_EPS)
    AG[0, y] = (low * scale).astype(BF16)
    loads[1].wait()

    pl.semaphore_wait(barrier, len(peers))

    HALF = T // 2

    def rows(h):
        return pl.ds(h * HALF, HALF)

    def rt_copy(p, k):
        me = a_me[p]
        return rcopy(RT.at[p, me], RT.at[p, me], rt_s.at[p, k], rt_r.at[p, k], a_dev[p](k))

    def ag_copy(p, d, h):
        me = a_me[p]
        blk = AG.at[p, me, rows(h)]
        return rcopy(blk, blk, ag_s.at[p, d, h], ag_r.at[p, d, h], a_dev[p](1 if d == 0 else 3))

    def agf_copy(p, d):
        frm = (a_me[p] + (3 if d == 0 else 1)) % RING
        blk = AG.at[p, frm, rows(d)]
        return rcopy(blk, blk, agf_s.at[p, d], agf_r.at[p, d], a_dev[p](1 if d == 0 else 3))

    for p in (1, 0):
        for k in (1, 2, 3):
            rt_copy(p, k).start()
    for p in (1, 0):
        ag_copy(p, 0, 0).start()
        ag_copy(p, 1, 1).start()
    for p in (1, 0):
        ag_copy(p, 0, 1).start()
        ag_copy(p, 1, 0).start()

    row = lax.broadcasted_iota(jnp.int32, (T, T), 0)

    def codes_of(p, j):
        b, s = row >> 5, row & 31
        if p == 0:
            return 64 * (4 * y + b) + 32 * j + s
        return 64 * (4 * b + z) + 32 * j + s

    def onehot(p, j, a):
        val = codes_of(p, j)
        hot = jnp.zeros((T, T), F32)
        share = jnp.zeros((T, T), F32)
        for k in range(TOPK):
            m = RT[p, a, k : k + 1, :] == val
            hot = jnp.where(m, 1.0, hot)
            gate = RT[p, a, 8 + k : 9 + k, :].astype(F32) * (1.0 / GATE_DENOM)
            share = jnp.where(m, gate, share)
        return hot, share

    def gather(p, j, a):
        hot, share = onehot(p, j, a)
        hot = hot.astype(BF16)
        for n in range(4):
            cols = pl.ds(n * 512, 512)
            picked = dot_nn(hot, AG[p, a, :, cols])
            if p == 1:
                picked = picked * jnp.sum(share, axis=1, keepdims=True)
            SD[p, j, a, :, cols] = picked.astype(BF16)

    def r_rows(p, a):
        block = a * RING + z if p == 0 else y * RING + a
        return pl.ds(pl.multiple_of(block * S, S), S)

    def r_rows_of(p, a, b):
        block = a * RING + b if p == 0 else b * RING + a
        return pl.ds(pl.multiple_of(block * S, S), S)

    def slots(b):
        return pl.ds(pl.multiple_of(b * S, S), S)

    def s2_send(p, j, a):
        for k in (1, 2, 3):
            b = (b_me[p] + k) % RING
            rcopy(
                SD.at[p, j, a, slots(b)], R.at[p, j, r_rows(p, a)],
                s2_s.at[p, j, k], s2_r.at[p, j, k], b_dev[p](k),
            ).start()
        pltpu.make_async_copy(
            SD.at[p, j, a, slots(b_me[p])], R.at[p, j, r_rows(p, a)], loc.at[p, j]
        ).start()

    def s2_whole(p, j, k):
        return rcopy(SD.at[p, j, 0], R.at[p, j, pl.ds(0, T)], s2_s.at[p, j, k], s2_r.at[p, j, k], b_dev[p](k))

    def loc_whole(p, j):
        return pltpu.make_async_copy(SD.at[p, j, 0], R.at[p, j, pl.ds(0, T)], loc.at[p, j])

    for p in (1, 0):
        gather(p, 0, a_me[p])
        s2_send(p, 0, a_me[p])
    for p in (1, 0):
        ag_copy(p, 0, 0).wait_recv()
        agf_copy(p, 0).start()
        ag_copy(p, 1, 1).wait_recv()
        agf_copy(p, 1).start()
    for p in (1, 0):
        for k in (1, 2, 3):
            rt_copy(p, k).wait_recv()
    for p in (1, 0):
        ag_copy(p, 0, 1).wait_recv()
        gather(p, 0, (a_me[p] + 3) % RING)
        s2_send(p, 0, (a_me[p] + 3) % RING)
        ag_copy(p, 1, 0).wait_recv()
        gather(p, 0, (a_me[p] + 1) % RING)
        s2_send(p, 0, (a_me[p] + 1) % RING)
    for p in (1, 0):
        agf_copy(p, 0).wait_recv()
        agf_copy(p, 1).wait_recv()
        gather(p, 0, (a_me[p] + 2) % RING)
        s2_send(p, 0, (a_me[p] + 2) % RING)

    def gather_later(a, carry):
        for p in (1, 0):
            gather(p, 1, a)
        return carry

    lax.fori_loop(0, RING, gather_later, 0)
    for p in (1, 0):
        for k in (1, 2, 3):
            rt_copy(p, k).wait_send()
        for d in (0, 1):
            for h in (0, 1):
                ag_copy(p, d, h).wait_send()
            agf_copy(p, d).wait_send()

    def s2_sent(j):
        for p in (0, 1):
            for k in (1, 2, 3):
                s2_whole(p, j, k).wait_send()
            loc_whole(p, j).wait()
        for p in (0, 1):
            for k in (1, 2, 3):
                pl.semaphore_signal(credit.at[j], inc=1, device_id=b_dev[p](k), device_id_type=MESH)

    s2_sent(0)

    def send_later(a, carry):
        for p in (1, 0):
            s2_send(p, 1, a)
        return carry

    lax.fori_loop(0, RING, send_later, 0)

    def px_copy(p, j, b):
        src = R.at[p, j, :, pl.ds(pl.multiple_of(b * 512 + (1 - c) * SHARE, SHARE), SHARE)]
        return rcopy(src, PX.at[p, :, pl.ds(b * SHARE, SHARE)], px_s.at[p], px_r.at[p], partner)

    def px_whole(p):
        half = R.at[p, 0, :, pl.ds(0, 4 * SHARE)]
        return rcopy(half, PX.at[p], px_s.at[p], px_r.at[p], partner)

    def pg_copy(cols):
        return rcopy(G.at[:, cols], PG.at[:, cols], pg_s, pg_r, partner)

    pg_whole = rcopy(G, PG, pg_s, pg_r, partner)

    def hidden_part(j):
        for p in (0, 1):
            for k in (1, 2, 3):
                s2_whole(p, j, k).wait_recv()
        if j == 1:
            pl.semaphore_wait(pcredit, 1)
        for p in (0, 1):
            for b in range(RING):
                px_copy(p, j, b).start()
        load_w(j).wait()

        def tile(n, carry):
            at = [pl.ds(pl.multiple_of(i * H + n * 256, 256), 256) for i in range(3)]
            gate = dot_nn(R[0, j], W[:, at[0]])
            up = dot_nn(R[0, j], W[:, at[1]])
            grad = dot_nn(R[1, j], W[:, at[2]])
            sig = jax.nn.sigmoid(gate)
            act = gate * sig
            G[:, at[2]] = (act * up).astype(BF16)
            G[:, at[0]] = (grad * up * sig * (1.0 + gate * (1.0 - sig))).astype(BF16)
            G[:, at[1]] = (grad * act).astype(BF16)
            for i in range(3):
                pg_copy(at[i]).start()
            return carry

        lax.fori_loop(0, 3, tile, 0)

    def outputs_part(j, out, route):
        def tile(n, carry):
            at = pl.ds(pl.multiple_of(n * 256, 256), 256)
            out[:, at] = dot_nt(G[:, 2 * H :], W[at, 2 * H :]).astype(BF16)
            route[:, at] = dot_nt(G[:, : 2 * H], W[at, : 2 * H]).astype(BF16)
            return carry

        lax.fori_loop(0, D // 256, tile, 0)

    def weight_block(j, b, dst):
        mine = pl.ds(pl.multiple_of(b * 512 + c * SHARE, SHARE), SHARE)
        theirs = pl.ds(pl.multiple_of(b * SHARE, SHARE), SHARE)

        def tile(p, first, count):
            def body(n, carry):
                at = pl.ds(pl.multiple_of(first + n * 256, 256), 256)
                acc = dot_tn(R[p, j, :, mine], G[:, at])
                acc = acc + dot_tn(PX[p, :, theirs], PG[:, at])
                dst[:, at] = acc.astype(BF16)
                return carry

            lax.fori_loop(0, count, body, 0)

        tile(0, 0, 6)
        tile(1, 2 * H, 3)

    AH = pl.ds(0, SHARE // 2)
    BH = pl.ds(SHARE // 2, SHARE // 2)

    def x_copy(j, own, d, i):
        to = xdev(1 if d == 0 else 3)
        near = own((x + (1 if d == 0 else 3)) % RING)
        far = own((x + 2) % RING)
        fin = o_left if d == 0 else o_right
        early, late = (AH, BH) if d == 0 else (BH, AH)
        if i == 0:
            src, dst = far.at[early], TMP.at[j, d]
        elif i == 1:
            src, dst = near.at[late], fin.at[j, late]
        else:
            src, dst = near.at[early], fin.at[j, early]
        return rcopy(src, dst, x_s.at[j, d, i], x_r.at[j, d, i], to)

    def weight_far(j, own):
        for p in (0, 1):
            px_whole(p).wait_recv()
        pg_whole.wait_recv()
        weight_block(j, (x + 2) % RING, own((x + 2) % RING))
        x_copy(j, own, 0, 0).start()
        x_copy(j, own, 1, 0).start()

    def weight_near(j, own, d):
        b = (x + (1 if d == 0 else 3)) % RING
        weight_block(j, b, own(b))
        x_copy(j, own, d, 1).start()

    def weight_own(j, own):
        weight_block(j, x, own(x))

    def partner_sent():
        for p in (0, 1):
            px_whole(p).wait_send()
        pg_whole.wait_send()

    def x_add(j, own):
        for d in (0, 1):
            early = AH if d == 0 else BH
            near = own((x + (1 if d == 0 else 3)) % RING)
            x_copy(j, own, d, 0).wait_recv()
            near[early, :] = (near[early, :].astype(F32) + TMP[j, d].astype(F32)).astype(BF16)
            x_copy(j, own, d, 2).start()

    def x_done(j, own):
        for d in (0, 1):
            for i in (1, 2):
                x_copy(j, own, d, i).wait_recv()
            for i in range(3):
                x_copy(j, own, d, i).wait_send()

    def own0(b):
        return OWN.at[b]

    def own1(b):
        return W.at[pl.ds(pl.multiple_of(b * SHARE, SHARE), SHARE)]

    OFFS = (2, 1, 3, 0)

    def back(j, i):
        for p in (0, 1):
            a = (a_me[p] + OFFS[i]) % RING
            for k in (1, 2, 3):
                b = (b_me[p] + k) % RING
                rcopy(
                    O.at[p, j, r_rows_of(p, a, b)], SD.at[p, j, a, slots(b_me[p])],
                    rb_s.at[p, j, k], rb_r.at[p, j, i], b_dev[p](k),
                ).start()
            pltpu.make_async_copy(
                O.at[p, j, r_rows(p, a)], SD.at[p, j, a, slots(b_me[p])], loc_b.at[p, j, i]
            ).start()

    def back_arrived(p, j, i):
        rcopy(
            O.at[p, j, pl.ds(0, 3 * S)], SD.at[p, j, 0, pl.ds(0, 3 * S)],
            rb_s.at[p, j, 1], rb_r.at[p, j, i], b_dev[p](1),
        ).wait_recv()
        pltpu.make_async_copy(
            O.at[p, j, pl.ds(0, S)], SD.at[p, j, 0, pl.ds(0, S)], loc_b.at[p, j, i]
        ).wait()

    def back_sent(p, j, k):
        rcopy(
            O.at[p, j, pl.ds(0, T)], SD.at[p, j, 0], rb_s.at[p, j, k], rb_r.at[p, j, 0], b_dev[p](k)
        ).wait_send()

    hidden_part(0)
    weight_far(0, own0)
    outputs_part(0, O.at[0, 0], O.at[1, 0])
    load_w(1).start()
    pl.semaphore_wait(credit.at[0], 6)
    for i in range(RING):
        back(0, i)
    weight_near(0, own0, 0)
    weight_near(0, own0, 1)
    weight_own(0, own0)
    pl.semaphore_signal(pcredit, inc=1, device_id=partner, device_id_type=MESH)
    partner_sent()
    s2_sent(1)
    hidden_part(1)
    x_add(0, own0)
    outputs_part(1, O.at[0, 1], O.at[1, 1])
    pl.semaphore_wait(credit.at[1], 6)
    back(1, 0)
    weight_far(1, own1)
    back(1, 1)
    weight_near(1, own1, 0)
    back(1, 2)
    weight_near(1, own1, 1)
    back(1, 3)
    weight_own(1, own1)
    partner_sent()
    own_copies = [pltpu.make_async_copy(own(x), o_own.at[j], w_sem) for j, own in enumerate((own0, own1))]
    own_copies[0].start()
    own_copies[0].wait()
    own_copies[1].start()

    def fn_copy(p, d, i):
        to = a_dev[p](1 if d == 0 else 3)
        near = (a_me[p] + (1 if d == 0 else 3)) % RING
        far = (a_me[p] + 2) % RING
        fin = FL if d == 0 else FR
        early, late = rows(d), rows(1 - d)
        if i == 0:
            src, dst = AG.at[p, far, early], FT.at[p, d]
        elif i == 1:
            src, dst = AG.at[p, near, late], fin.at[p, late]
        else:
            src, dst = AG.at[p, near, early], fin.at[p, early]
        return rcopy(src, dst, fn_s.at[p, d, i], fn_r.at[p, d, i], to)

    def combine(p, a):
        parts = []
        for j in (0, 1):
            hot, share = onehot(p, j, a)
            if p == 0:
                top = share.astype(BF16)
                parts.append((j, top))
                parts.append((j, (share - top.astype(F32)).astype(BF16)))
            else:
                parts.append((j, hot.astype(BF16)))
        for n in range(4):
            cols = pl.ds(n * 512, 512)
            total = jnp.zeros((T, 512), F32)
            for j, weights in parts:
                total = total + dot_tn(weights, SD[p, j, a, :, cols])
            AG[p, a, :, cols] = total.astype(BF16)

    for i in range(RING):
        if i == 3:
            for p in (0, 1):
                for d in (0, 1):
                    near = (a_me[p] + (1 if d == 0 else 3)) % RING
                    early = rows(d)
                    fn_copy(p, d, 0).wait_recv()
                    AG[p, near, early, :] = (
                        AG[p, near, early, :].astype(F32) + FT[p, d].astype(F32)
                    ).astype(BF16)
                    fn_copy(p, d, 2).start()
            x_add(1, own1)
        for p in (0, 1):
            for j in (0, 1):
                back_arrived(p, j, i)
            combine(p, (a_me[p] + OFFS[i]) % RING)
            if i == 0:
                fn_copy(p, 0, 0).start()
                fn_copy(p, 1, 0).start()
            elif i < 3:
                fn_copy(p, i - 1, 1).start()

    for p in (0, 1):
        for d in (0, 1):
            for i in (1, 2):
                fn_copy(p, d, i).wait_recv()
    loads[5].wait()
    loads[6].wait()
    mixture = AG[0, y].astype(F32) + FL[0].astype(F32) + FR[0].astype(F32)
    o_up[...] = (uh[...].astype(F32) - mixture).astype(BF16)
    grad_normed = AG[1, z].astype(F32) + FL[1].astype(F32) + FR[1].astype(F32)
    low = lh[...].astype(F32)
    scale = lax.rsqrt(jnp.mean(low * low, axis=1, keepdims=True) + NORM_EPS)
    inner = jnp.mean(low * grad_normed, axis=1, keepdims=True)
    o_lo[...] = (
        lg[...].astype(F32) + scale * grad_normed - low * (scale * scale * scale) * inner
    ).astype(BF16)

    for p in (0, 1):
        for d in (0, 1):
            for i in range(3):
                fn_copy(p, d, i).wait_send()
        for j in (0, 1):
            for k in (1, 2, 3):
                back_sent(p, j, k)
    own_copies[1].wait()
    x_done(0, own0)
    x_done(1, own1)


def run(*arrays):
    vm = pl.BlockSpec(memory_space=pltpu.VMEM)
    hbm = pl.BlockSpec(memory_space=pl.ANY)
    dma = pltpu.SemaphoreType.DMA
    half = jax.ShapeDtypeStruct((2, SHARE, F), BF16)
    rows = jax.ShapeDtypeStruct((T, D), BF16)
    return pl.pallas_call(
        kernel,
        out_shape=(rows, rows, half, half, half),
        in_specs=[hbm] * 8,
        out_specs=(vm, vm, hbm, hbm, hbm),
        scratch_shapes=[
            pltpu.VMEM((T, D), BF16),
            pltpu.VMEM((T, D), BF16),
            pltpu.VMEM((T, D), BF16),
            pltpu.VMEM((TOPK, T), jnp.int32),
            pltpu.VMEM((TOPK, T), jnp.int32),
            pltpu.VMEM((TOPK, T), jnp.int32),
            pltpu.VMEM((2, RING, T, D), BF16),
            pltpu.VMEM((2, RING, 16, T), jnp.int32),
            pltpu.VMEM((2, 2, RING, T, D), BF16),
            pltpu.VMEM((2, 2, M, D), BF16),
            pltpu.VMEM((2, 2, M, D), BF16),
            pltpu.VMEM((D, F), BF16),
            pltpu.VMEM((M, F), BF16),
            pltpu.VMEM((2, M, 4 * SHARE), BF16),
            pltpu.VMEM((M, F), BF16),
            pltpu.VMEM((RING, SHARE, F), BF16),
            pltpu.VMEM((2, 2, SHARE // 2, F), BF16),
            pltpu.VMEM((2, T, D), BF16),
            pltpu.VMEM((2, T, D), BF16),
            pltpu.VMEM((2, 2, T // 2, D), BF16),
            dma((2, 2, 2)), dma((2, 2, 2)),
            dma((2, 2)), dma((2, 2)),
            dma((2, 4)), dma((2, 4)),
            dma((2, 2, 4)), dma((2, 2, 4)),
            dma((2, 2, 4)), dma((2, 2, 4)),
            dma((2,)), dma((2,)),
            dma, dma,
            dma((2, 2, 3)), dma((2, 2, 3)),
            dma((2, 2, 3)), dma((2, 2, 3)),
            dma((2, 2)),
            dma((2, 2, 4)),
            dma,
            dma((7,)),
            pltpu.SemaphoreType.REGULAR((2,)),
            pltpu.SemaphoreType.REGULAR,
        ],
        compiler_params=pltpu.CompilerParams(
            collective_id=0, has_side_effects=True, vmem_limit_bytes=63 * 1024 * 1024
        ),
        cost_estimate=pl.CostEstimate(
            flops=29_000_000_000, bytes_accessed=30_000_000, transcendentals=800_000
        ),
    )(*arrays)


def shards(
    upper_half, lower_half, upper_grad, lower_grad, expert_ids, gate_weights, route_slots, expert_weight
):
    up, lo, own, left, right = run(
        upper_half, lower_half, upper_grad, lower_grad,
        expert_ids.T, gate_weights.T, route_slots.T, expert_weight,
    )
    weight_grad = own.astype(F32) + left.astype(F32) + right.astype(F32)
    return up, lo, weight_grad


def solution(mesh):
    tok = P(("dp", "expert"), None)
    return jax.shard_map(
        shards,
        mesh=mesh,
        in_specs=(tok,) * 7 + (P("expert", None, None),),
        out_specs=(tok, tok, P("expert", "dp", None)),
        check_vma=False,
    )
```

```python
import functools

import jax
import jax.numpy as jnp
from jax import lax
from jax.experimental import pallas as pl
from jax.experimental.pallas import tpu as pltpu
from jax.sharding import PartitionSpec as P

MESH = pl.DeviceIdType.MESH
F32 = jnp.float32
BF16 = jnp.bfloat16

GATE_DENOM = 1024
NORM_EPS = 1e-06
T = 128
D = 2048
H = 768
F = 3 * H
TOPK = 6
CAP = 30
S = 32
M = 16 * S
RING = 4
SHARE = D // 8


def dot_nt(a, b):
    return lax.dot_general(a, b, (((1,), (1,)), ((), ())), preferred_element_type=F32)


def dot_tn(a, b):
    return lax.dot_general(a, b, (((0,), (0,)), ((), ())), preferred_element_type=F32)


def dot_nn(a, b):
    return lax.dot_general(a, b, (((1,), (0,)), ((), ())), preferred_element_type=F32)


def kernel(
    uh_in, lh_in, ug_in, lg_in, ids_in, gates_in, slots_in, w_hbm,
    o_up, o_lo, o_sum, o_left, o_right,
    uh, lh, lg, ids, gates, slots_of, AG, RT, SD, R, O, W, G, PX, PG, OWN, TMP, FL, FR, FT,
    ag_s, ag_r, agf_s, agf_r, rt_s, rt_r, s2_s, s2_r, rb_s, rb_r,
    px_s, px_r, pg_s, pg_r, x_s, x_r, fn_s, fn_r, loc, loc_b, w_sem, in_sem, out_sem, credit, pcredit, xcredit,
):
    dp = lax.axis_index("dp")
    ex = lax.axis_index("expert")
    x, c = dp // 2, dp % 2
    y, z = ex // RING, ex % RING
    a_me = (y, z)
    b_me = (z, y)

    def ydev(k):
        return (dp, ((y + k) % RING) * RING + z)

    def zdev(k):
        return (dp, y * RING + (z + k) % RING)

    def xdev(k):
        return (((x + k) % RING) * 2 + c, ex)

    a_dev = (ydev, zdev)
    b_dev = (zdev, ydev)
    partner = (x * 2 + 1 - c, ex)

    def rcopy(src, dst, ss, rs, dev):
        return pltpu.make_async_remote_copy(
            src_ref=src, dst_ref=dst, send_sem=ss, recv_sem=rs, device_id=dev, device_id_type=MESH
        )

    def load_w(j):
        return pltpu.make_async_copy(w_hbm.at[j], W, w_sem.at[0])

    barrier = pltpu.get_barrier_semaphore()
    peers = [ydev(k) for k in (1, 2, 3)] + [zdev(k) for k in (1, 2, 3)] + [xdev(1), xdev(3), partner]
    for dev in peers:
        pl.semaphore_signal(barrier, inc=1, device_id=dev, device_id_type=MESH)

    pairs = (
        (lh_in, lh), (ug_in, AG.at[1, z]), (ids_in, ids), (gates_in, gates), (slots_in, slots_of),
        (uh_in, uh), (lg_in, lg),
    )
    loads = [pltpu.make_async_copy(src, dst, in_sem.at[i]) for i, (src, dst) in enumerate(pairs)]
    for load in loads:
        load.start()
    load_w(0).start()
    for i in (2, 3, 4):
        loads[i].wait()
    for p in (0, 1):
        RT[p, a_me[p], 0:TOPK, :] = jnp.where(slots_of[...] < CAP, ids[...] * S + slots_of[...], -1)
        RT[p, a_me[p], 8 : 8 + TOPK, :] = gates[...]
    loads[0].wait()
    low = lh[...].astype(F32)
    scale = lax.rsqrt(jnp.mean(low * low, axis=1, keepdims=True) + NORM_EPS)
    AG[0, y] = (low * scale).astype(BF16)
    loads[1].wait()

    pl.semaphore_wait(barrier, len(peers))

    HALF = T // 2

    def rows(h):
        return pl.ds(h * HALF, HALF)

    def rt_copy(p, k):
        me = a_me[p]
        return rcopy(RT.at[p, me], RT.at[p, me], rt_s.at[p, k], rt_r.at[p, k], a_dev[p](k))

    def ag_copy(p, d, h):
        me = a_me[p]
        blk = AG.at[p, me, rows(h)]
        return rcopy(blk, blk, ag_s.at[p, d, h], ag_r.at[p, d, h], a_dev[p](1 if d == 0 else 3))

    def agf_copy(p, d):
        frm = (a_me[p] + (3 if d == 0 else 1)) % RING
        blk = AG.at[p, frm, rows(d)]
        return rcopy(blk, blk, agf_s.at[p, d], agf_r.at[p, d], a_dev[p](1 if d == 0 else 3))

    for p in (1, 0):
        for k in (1, 2, 3):
            rt_copy(p, k).start()
    for p in (1, 0):
        ag_copy(p, 0, 0).start()
        ag_copy(p, 1, 1).start()
    for p in (1, 0):
        ag_copy(p, 0, 1).start()
        ag_copy(p, 1, 0).start()

    row = lax.broadcasted_iota(jnp.int32, (T, T), 0)

    def codes_of(p, j):
        b, s = row >> 5, row & 31
        if p == 0:
            return 64 * (4 * y + b) + 32 * j + s
        return 64 * (4 * b + z) + 32 * j + s

    def onehot(p, j, a):
        val = codes_of(p, j)
        hot = jnp.zeros((T, T), F32)
        share = jnp.zeros((T, T), F32)
        for k in range(TOPK):
            m = RT[p, a, k : k + 1, :] == val
            hot = jnp.where(m, 1.0, hot)
            gate = RT[p, a, 8 + k : 9 + k, :].astype(F32) * (1.0 / GATE_DENOM)
            share = jnp.where(m, gate, share)
        return hot, share

    def gather(p, j, a):
        hot, share = onehot(p, j, a)
        hot = hot.astype(BF16)
        for n in range(4):
            cols = pl.ds(n * 512, 512)
            picked = dot_nn(hot, AG[p, a, :, cols])
            if p == 1:
                picked = picked * jnp.sum(share, axis=1, keepdims=True)
            SD[p, j, a, :, cols] = picked.astype(BF16)

    def r_rows(p, a):
        block = a * RING + z if p == 0 else y * RING + a
        return pl.ds(pl.multiple_of(block * S, S), S)

    def r_rows_of(p, a, b):
        block = a * RING + b if p == 0 else b * RING + a
        return pl.ds(pl.multiple_of(block * S, S), S)

    def slots(b):
        return pl.ds(pl.multiple_of(b * S, S), S)

    def s2_send(p, j, a):
        for k in (1, 2, 3):
            b = (b_me[p] + k) % RING
            rcopy(
                SD.at[p, j, a, slots(b)], R.at[p, j, r_rows(p, a)],
                s2_s.at[p, j, k], s2_r.at[p, j, k], b_dev[p](k),
            ).start()
        pltpu.make_async_copy(
            SD.at[p, j, a, slots(b_me[p])], R.at[p, j, r_rows(p, a)], loc.at[p, j]
        ).start()

    def s2_whole(p, j, k):
        return rcopy(SD.at[p, j, 0], R.at[p, j, pl.ds(0, T)], s2_s.at[p, j, k], s2_r.at[p, j, k], b_dev[p](k))

    def loc_whole(p, j):
        return pltpu.make_async_copy(SD.at[p, j, 0], R.at[p, j, pl.ds(0, T)], loc.at[p, j])

    for p in (1, 0):
        gather(p, 0, a_me[p])
        s2_send(p, 0, a_me[p])
    for p in (1, 0):
        ag_copy(p, 0, 0).wait_recv()
        agf_copy(p, 0).start()
        ag_copy(p, 1, 1).wait_recv()
        agf_copy(p, 1).start()
    for p in (1, 0):
        for k in (1, 2, 3):
            rt_copy(p, k).wait_recv()
    for p in (1, 0):
        ag_copy(p, 0, 1).wait_recv()
        gather(p, 0, (a_me[p] + 3) % RING)
        s2_send(p, 0, (a_me[p] + 3) % RING)
        ag_copy(p, 1, 0).wait_recv()
        gather(p, 0, (a_me[p] + 1) % RING)
        s2_send(p, 0, (a_me[p] + 1) % RING)
    for p in (1, 0):
        agf_copy(p, 0).wait_recv()
        agf_copy(p, 1).wait_recv()
        gather(p, 0, (a_me[p] + 2) % RING)
        s2_send(p, 0, (a_me[p] + 2) % RING)

    def gather_later(a, carry):
        for p in (1, 0):
            gather(p, 1, a)
        return carry

    lax.fori_loop(0, RING, gather_later, 0)
    for p in (1, 0):
        for k in (1, 2, 3):
            rt_copy(p, k).wait_send()
        for d in (0, 1):
            for h in (0, 1):
                ag_copy(p, d, h).wait_send()
            agf_copy(p, d).wait_send()

    def s2_sent(j):
        for p in (0, 1):
            for k in (1, 2, 3):
                s2_whole(p, j, k).wait_send()
            loc_whole(p, j).wait()
        for p in (0, 1):
            for k in (1, 2, 3):
                pl.semaphore_signal(credit.at[j], inc=1, device_id=b_dev[p](k), device_id_type=MESH)

    s2_sent(0)

    def send_later(a, carry):
        for p in (1, 0):
            s2_send(p, 1, a)
        return carry

    lax.fori_loop(0, RING, send_later, 0)

    def px_copy(p, j, b):
        src = R.at[p, j, :, pl.ds(pl.multiple_of(b * 512 + (1 - c) * SHARE, SHARE), SHARE)]
        return rcopy(src, PX.at[p, :, pl.ds(b * SHARE, SHARE)], px_s.at[p], px_r.at[p], partner)

    def px_whole(p):
        half = R.at[p, 0, :, pl.ds(0, 4 * SHARE)]
        return rcopy(half, PX.at[p], px_s.at[p], px_r.at[p], partner)

    def pg_copy(cols):
        return rcopy(G.at[:, cols], PG.at[:, cols], pg_s, pg_r, partner)

    pg_whole = rcopy(G, PG, pg_s, pg_r, partner)

    def hidden_part(j):
        for p in (0, 1):
            for k in (1, 2, 3):
                s2_whole(p, j, k).wait_recv()
        if j == 1:
            pl.semaphore_wait(pcredit, 1)
        for p in (0, 1):
            for b in range(RING):
                px_copy(p, j, b).start()
        load_w(j).wait()

        def tile(n, carry):
            at = [pl.ds(pl.multiple_of(i * H + n * 256, 256), 256) for i in range(3)]
            gate = dot_nn(R[0, j], W[:, at[0]])
            up = dot_nn(R[0, j], W[:, at[1]])
            grad = dot_nn(R[1, j], W[:, at[2]])
            sig = jax.nn.sigmoid(gate)
            act = gate * sig
            G[:, at[2]] = (act * up).astype(BF16)
            G[:, at[0]] = (grad * up * sig * (1.0 + gate * (1.0 - sig))).astype(BF16)
            G[:, at[1]] = (grad * act).astype(BF16)
            for i in range(3):
                pg_copy(at[i]).start()
            return carry

        lax.fori_loop(0, 3, tile, 0)

    def outputs_part(j, out, route):
        def tile(n, carry):
            at = pl.ds(pl.multiple_of(n * 512, 512), 512)
            out[:, at] = dot_nt(G[:, 2 * H :], W[at, 2 * H :]).astype(BF16)
            route[:, at] = dot_nt(G[:, : 2 * H], W[at, : 2 * H]).astype(BF16)
            return carry

        lax.fori_loop(0, D // 512, tile, 0)

    def weight_block(j, b, dst):
        mine = pl.ds(pl.multiple_of(b * 512 + c * SHARE, SHARE), SHARE)
        theirs = pl.ds(pl.multiple_of(b * SHARE, SHARE), SHARE)

        def tile(p, first, count):
            def body(n, carry):
                at = pl.ds(pl.multiple_of(first + n * H, H), H)
                acc = dot_tn(R[p, j, :, mine], G[:, at])
                acc = acc + dot_tn(PX[p, :, theirs], PG[:, at])
                dst[:, at] = acc.astype(BF16)
                return carry

            lax.fori_loop(0, count, body, 0)

        tile(0, 0, 2)
        tile(1, 2 * H, 1)

    AH = pl.ds(0, SHARE // 2)
    BH = pl.ds(SHARE // 2, SHARE // 2)

    def x_copy(j, own, d, i):
        to = xdev(1 if d == 0 else 3)
        near = own((x + (1 if d == 0 else 3)) % RING)
        far = own((x + 2) % RING)
        early, late = (AH, BH) if d == 0 else (BH, AH)
        fin = (o_left, o_right)[d] if j == 0 else W.at[pl.ds((4 + d) * SHARE, SHARE)]
        if i == 0:
            src, dst = far.at[early], TMP.at[j, d]
        elif i == 1:
            src, dst = near.at[late], fin.at[late]
        else:
            src, dst = near.at[early], fin.at[early]
        return rcopy(src, dst, x_s.at[j, d, i], x_r.at[j, d, i], to)

    def weight_far(j, own):
        for p in (0, 1):
            px_whole(p).wait_recv()
        pg_whole.wait_recv()
        weight_block(j, (x + 2) % RING, own((x + 2) % RING))
        x_copy(j, own, 0, 0).start()
        x_copy(j, own, 1, 0).start()

    def weight_near(j, own, d):
        b = (x + (1 if d == 0 else 3)) % RING
        weight_block(j, b, own(b))
        x_copy(j, own, d, 1).start()

    def weight_own(j, own):
        weight_block(j, x, own(x))

    def partner_sent():
        for p in (0, 1):
            px_whole(p).wait_send()
        pg_whole.wait_send()

    def x_add(j, own):
        for d in (0, 1):
            early = AH if d == 0 else BH
            near = own((x + (1 if d == 0 else 3)) % RING)
            x_copy(j, own, d, 0).wait_recv()
            near[early, :] = (near[early, :].astype(F32) + TMP[j, d].astype(F32)).astype(BF16)
            x_copy(j, own, d, 2).start()

    def x_arrived(j, own):
        for d in (0, 1):
            for i in (1, 2):
                x_copy(j, own, d, i).wait_recv()

    def x_sent(j, own):
        for d in (0, 1):
            for i in range(3):
                x_copy(j, own, d, i).wait_send()

    def own0(b):
        return OWN.at[b]

    def own1(b):
        return W.at[pl.ds(pl.multiple_of(b * SHARE, SHARE), SHARE)]

    OFFS = (2, 1, 3, 0)

    def back(j, i):
        for p in (0, 1):
            a = (a_me[p] + OFFS[i]) % RING
            for k in (1, 2, 3):
                b = (b_me[p] + k) % RING
                rcopy(
                    O.at[p, j, r_rows_of(p, a, b)], SD.at[p, j, a, slots(b_me[p])],
                    rb_s.at[p, j, k], rb_r.at[p, j, i], b_dev[p](k),
                ).start()
            pltpu.make_async_copy(
                O.at[p, j, r_rows(p, a)], SD.at[p, j, a, slots(b_me[p])], loc_b.at[p, j, i]
            ).start()

    def back_arrived(p, j, i):
        rcopy(
            O.at[p, j, pl.ds(0, 3 * S)], SD.at[p, j, 0, pl.ds(0, 3 * S)],
            rb_s.at[p, j, 1], rb_r.at[p, j, i], b_dev[p](1),
        ).wait_recv()
        pltpu.make_async_copy(
            O.at[p, j, pl.ds(0, S)], SD.at[p, j, 0, pl.ds(0, S)], loc_b.at[p, j, i]
        ).wait()

    def back_sent(p, j, k):
        rcopy(
            O.at[p, j, pl.ds(0, T)], SD.at[p, j, 0], rb_s.at[p, j, k], rb_r.at[p, j, 0], b_dev[p](k)
        ).wait_send()

    hidden_part(0)
    weight_far(0, own0)
    outputs_part(0, O.at[0, 0], O.at[1, 0])
    load_w(1).start()
    pl.semaphore_wait(credit.at[0], 6)
    for i in range(RING):
        back(0, i)
    weight_near(0, own0, 0)
    weight_near(0, own0, 1)
    weight_own(0, own0)
    pl.semaphore_signal(pcredit, inc=1, device_id=partner, device_id_type=MESH)
    partner_sent()
    s2_sent(1)
    hidden_part(1)
    x_add(0, own0)
    outputs_part(1, O.at[0, 1], O.at[1, 1])
    for k in (1, 3):
        pl.semaphore_signal(xcredit, inc=1, device_id=xdev(k), device_id_type=MESH)
    pl.semaphore_wait(credit.at[1], 6)
    back(1, 0)
    weight_far(1, own1)
    back(1, 1)
    pl.semaphore_wait(xcredit, 2)
    weight_near(1, own1, 0)
    back(1, 2)
    weight_near(1, own1, 1)
    back(1, 3)
    weight_own(1, own1)
    partner_sent()

    pieces = [
        pltpu.make_async_copy(src, G.at[pl.ds(d * SHARE, SHARE)], w_sem.at[1 + d])
        for d, src in enumerate((o_left, o_right))
    ]
    sums = [
        pltpu.make_async_copy(buf.at[pl.ds(0, SHARE)], o_sum.at[j], out_sem.at[j])
        for j, buf in enumerate((G, PG))
    ]

    def fetch_pieces():
        x_arrived(0, own0)
        for piece in pieces:
            piece.start()

    def sum0():
        for piece in pieces:
            piece.wait()
        G[0:SHARE, :] = (
            own0(x)[...].astype(F32)
            + G[0:SHARE, :].astype(F32)
            + G[SHARE : 2 * SHARE, :].astype(F32)
        ).astype(BF16)
        sums[0].start()

    def sum1():
        x_arrived(1, own1)
        PG[0:SHARE, :] = (
            own1(x)[...].astype(F32)
            + W[4 * SHARE : 5 * SHARE, :].astype(F32)
            + W[5 * SHARE : 6 * SHARE, :].astype(F32)
        ).astype(BF16)
        sums[1].start()

    def fn_copy(p, d, i):
        to = a_dev[p](1 if d == 0 else 3)
        near = (a_me[p] + (1 if d == 0 else 3)) % RING
        far = (a_me[p] + 2) % RING
        fin = FL if d == 0 else FR
        early, late = rows(d), rows(1 - d)
        if i == 0:
            src, dst = AG.at[p, far, early], FT.at[p, d]
        elif i == 1:
            src, dst = AG.at[p, near, late], fin.at[p, late]
        else:
            src, dst = AG.at[p, near, early], fin.at[p, early]
        return rcopy(src, dst, fn_s.at[p, d, i], fn_r.at[p, d, i], to)

    def combine(p, a):
        parts = []
        for j in (0, 1):
            hot, share = onehot(p, j, a)
            if p == 0:
                top = share.astype(BF16)
                parts.append((j, top))
                parts.append((j, (share - top.astype(F32)).astype(BF16)))
            else:
                parts.append((j, hot.astype(BF16)))
        for n in range(4):
            cols = pl.ds(n * 512, 512)
            total = jnp.zeros((T, 512), F32)
            for j, weights in parts:
                total = total + dot_tn(weights, SD[p, j, a, :, cols])
            AG[p, a, :, cols] = total.astype(BF16)

    for i in range(RING):
        if i == 3:
            for p in (0, 1):
                for d in (0, 1):
                    near = (a_me[p] + (1 if d == 0 else 3)) % RING
                    early = rows(d)
                    fn_copy(p, d, 0).wait_recv()
                    AG[p, near, early, :] = (
                        AG[p, near, early, :].astype(F32) + FT[p, d].astype(F32)
                    ).astype(BF16)
                    fn_copy(p, d, 2).start()
            x_add(1, own1)
        for p in (0, 1):
            for j in (0, 1):
                back_arrived(p, j, i)
            combine(p, (a_me[p] + OFFS[i]) % RING)
            if i == 0:
                fn_copy(p, 0, 0).start()
                fn_copy(p, 1, 0).start()
            elif i < 3:
                fn_copy(p, i - 1, 1).start()
        if i == 0:
            fetch_pieces()
        if i == 1:
            sum0()

    def fn_arrived(p):
        for d in (0, 1):
            for i in (1, 2):
                fn_copy(p, d, i).wait_recv()

    results = [
        pltpu.make_async_copy(src, dst, out_sem.at[2 + p]) for p, (src, dst) in enumerate(((uh, o_up), (lg, o_lo)))
    ]
    loads[5].wait()
    loads[6].wait()
    low = lh[...].astype(F32)
    scale = lax.rsqrt(jnp.mean(low * low, axis=1, keepdims=True) + NORM_EPS)
    fn_arrived(0)
    mixture = AG[0, y].astype(F32) + FL[0].astype(F32) + FR[0].astype(F32)
    uh[...] = (uh[...].astype(F32) - mixture).astype(BF16)
    results[0].start()
    fn_arrived(1)
    grad_normed = AG[1, z].astype(F32) + FL[1].astype(F32) + FR[1].astype(F32)
    low = lh[...].astype(F32)
    inner = jnp.mean(low * grad_normed, axis=1, keepdims=True)
    lg[...] = (
        lg[...].astype(F32) + scale * grad_normed - low * (scale * scale * scale) * inner
    ).astype(BF16)
    results[1].start()
    sum1()

    for p in (0, 1):
        for d in (0, 1):
            for i in range(3):
                fn_copy(p, d, i).wait_send()
        for j in (0, 1):
            for k in (1, 2, 3):
                back_sent(p, j, k)
    x_sent(0, own0)
    x_sent(1, own1)
    for copy in results + sums:
        copy.wait()


def run(*arrays):
    hbm = pl.BlockSpec(memory_space=pl.ANY)
    dma = pltpu.SemaphoreType.DMA
    half = jax.ShapeDtypeStruct((SHARE, F), BF16)
    both = jax.ShapeDtypeStruct((2, SHARE, F), BF16)
    rows = jax.ShapeDtypeStruct((T, D), BF16)
    return pl.pallas_call(
        kernel,
        out_shape=(rows, rows, both, half, half),
        in_specs=[hbm] * 8,
        out_specs=(hbm,) * 5,
        scratch_shapes=[
            pltpu.VMEM((T, D), BF16),
            pltpu.VMEM((T, D), BF16),
            pltpu.VMEM((T, D), BF16),
            pltpu.VMEM((TOPK, T), jnp.int32),
            pltpu.VMEM((TOPK, T), jnp.int32),
            pltpu.VMEM((TOPK, T), jnp.int32),
            pltpu.VMEM((2, RING, T, D), BF16),
            pltpu.VMEM((2, RING, 16, T), jnp.int32),
            pltpu.VMEM((2, 2, RING, T, D), BF16),
            pltpu.VMEM((2, 2, M, D), BF16),
            pltpu.VMEM((2, 2, M, D), BF16),
            pltpu.VMEM((D, F), BF16),
            pltpu.VMEM((M, F), BF16),
            pltpu.VMEM((2, M, 4 * SHARE), BF16),
            pltpu.VMEM((M, F), BF16),
            pltpu.VMEM((RING, SHARE, F), BF16),
            pltpu.VMEM((2, 2, SHARE // 2, F), BF16),
            pltpu.VMEM((2, T, D), BF16),
            pltpu.VMEM((2, T, D), BF16),
            pltpu.VMEM((2, 2, T // 2, D), BF16),
            dma((2, 2, 2)), dma((2, 2, 2)),
            dma((2, 2)), dma((2, 2)),
            dma((2, 4)), dma((2, 4)),
            dma((2, 2, 4)), dma((2, 2, 4)),
            dma((2, 2, 4)), dma((2, 2, 4)),
            dma((2,)), dma((2,)),
            dma, dma,
            dma((2, 2, 3)), dma((2, 2, 3)),
            dma((2, 2, 3)), dma((2, 2, 3)),
            dma((2, 2)),
            dma((2, 2, 4)),
            dma((3,)),
            dma((7,)),
            dma((4,)),
            pltpu.SemaphoreType.REGULAR((2,)),
            pltpu.SemaphoreType.REGULAR,
            pltpu.SemaphoreType.REGULAR,
        ],
        compiler_params=pltpu.CompilerParams(
            collective_id=0, has_side_effects=True, vmem_limit_bytes=63 * 1024 * 1024
        ),
        cost_estimate=pl.CostEstimate(
            flops=29_000_000_000, bytes_accessed=30_000_000, transcendentals=800_000
        ),
    )(*arrays)


def shards(
    upper_half, lower_half, upper_grad, lower_grad, expert_ids, gate_weights, route_slots, expert_weight
):
    up, lo, total, _, _ = run(
        upper_half, lower_half, upper_grad, lower_grad,
        expert_ids.T, gate_weights.T, route_slots.T, expert_weight,
    )
    return up, lo, total.astype(F32)


def solution(mesh):
    tok = P(("dp", "expert"), None)
    return jax.shard_map(
        shards,
        mesh=mesh,
        in_specs=(tok,) * 7 + (P("expert", None, None),),
        out_specs=(tok, tok, P("expert", "dp", None)),
        check_vma=False,
    )
```

```python
import functools

import jax
import jax.numpy as jnp
from jax import lax
from jax.experimental import pallas as pl
from jax.experimental.pallas import tpu as pltpu
from jax.sharding import PartitionSpec as P

MESH = pl.DeviceIdType.MESH
F32 = jnp.float32
BF16 = jnp.bfloat16

GATE_DENOM = 1024
NORM_EPS = 1e-06
T = 128
D = 2048
H = 768
F = 3 * H
TOPK = 6
CAP = 30
S = 32
M = 16 * S
RING = 4
SHARE = D // 8


def dot_nt(a, b):
    return lax.dot_general(a, b, (((1,), (1,)), ((), ())), preferred_element_type=F32)


def dot_tn(a, b):
    return lax.dot_general(a, b, (((0,), (0,)), ((), ())), preferred_element_type=F32)


def dot_nn(a, b):
    return lax.dot_general(a, b, (((1,), (0,)), ((), ())), preferred_element_type=F32)


def kernel(
    uh_in, lh_in, ug_in, lg_in, ids_in, gates_in, slots_in, w_hbm,
    o_up, o_lo, o_sum, o_own, o_left, o_right,
    uh, lh, lg, ids, gates, slots_of, AG, RT, SD, R, O, W, G, PX, PG, OWN, TMP, FL, FR, FT,
    ag_s, ag_r, agf_s, agf_r, rt_s, rt_r, s2_s, s2_r, rb_s, rb_r,
    px_s, px_r, pg_s, pg_r, x_s, x_r, fn_s, fn_r, loc, loc_b, w_sem, in_sem, out_sem, credit, pcredit,
):
    dp = lax.axis_index("dp")
    ex = lax.axis_index("expert")
    x, c = dp // 2, dp % 2
    y, z = ex // RING, ex % RING
    a_me = (y, z)
    b_me = (z, y)

    def ydev(k):
        return (dp, ((y + k) % RING) * RING + z)

    def zdev(k):
        return (dp, y * RING + (z + k) % RING)

    def xdev(k):
        return (((x + k) % RING) * 2 + c, ex)

    a_dev = (ydev, zdev)
    b_dev = (zdev, ydev)
    partner = (x * 2 + 1 - c, ex)

    def rcopy(src, dst, ss, rs, dev):
        return pltpu.make_async_remote_copy(
            src_ref=src, dst_ref=dst, send_sem=ss, recv_sem=rs, device_id=dev, device_id_type=MESH
        )

    def load_w(j):
        return pltpu.make_async_copy(w_hbm.at[j], W, w_sem.at[0])

    barrier = pltpu.get_barrier_semaphore()
    peers = [ydev(k) for k in (1, 2, 3)] + [zdev(k) for k in (1, 2, 3)] + [xdev(1), xdev(3), partner]
    for dev in peers:
        pl.semaphore_signal(barrier, inc=1, device_id=dev, device_id_type=MESH)

    pairs = (
        (lh_in, lh), (ug_in, AG.at[1, z]), (ids_in, ids), (gates_in, gates), (slots_in, slots_of),
        (uh_in, uh), (lg_in, lg),
    )
    loads = [pltpu.make_async_copy(src, dst, in_sem.at[i]) for i, (src, dst) in enumerate(pairs)]
    for load in loads:
        load.start()
    load_w(0).start()
    for i in (2, 3, 4):
        loads[i].wait()
    for p in (0, 1):
        RT[p, a_me[p], 0:TOPK, :] = jnp.where(slots_of[...] < CAP, ids[...] * S + slots_of[...], -1)
        RT[p, a_me[p], 8 : 8 + TOPK, :] = gates[...]
    loads[0].wait()
    low = lh[...].astype(F32)
    scale = lax.rsqrt(jnp.mean(low * low, axis=1, keepdims=True) + NORM_EPS)
    AG[0, y] = (low * scale).astype(BF16)
    loads[1].wait()

    pl.semaphore_wait(barrier, len(peers))

    HALF = T // 2

    def rows(h):
        return pl.ds(h * HALF, HALF)

    def rt_copy(p, k):
        me = a_me[p]
        return rcopy(RT.at[p, me], RT.at[p, me], rt_s.at[p, k], rt_r.at[p, k], a_dev[p](k))

    def ag_copy(p, d, h):
        me = a_me[p]
        blk = AG.at[p, me, rows(h)]
        return rcopy(blk, blk, ag_s.at[p, d, h], ag_r.at[p, d, h], a_dev[p](1 if d == 0 else 3))

    def agf_copy(p, d):
        frm = (a_me[p] + (3 if d == 0 else 1)) % RING
        blk = AG.at[p, frm, rows(d)]
        return rcopy(blk, blk, agf_s.at[p, d], agf_r.at[p, d], a_dev[p](1 if d == 0 else 3))

    for p in (1, 0):
        for k in (1, 2, 3):
            rt_copy(p, k).start()
    for p in (1, 0):
        ag_copy(p, 0, 0).start()
        ag_copy(p, 1, 1).start()
    for p in (1, 0):
        ag_copy(p, 0, 1).start()
        ag_copy(p, 1, 0).start()

    row = lax.broadcasted_iota(jnp.int32, (T, T), 0)

    def codes_of(p, j):
        b, s = row >> 5, row & 31
        if p == 0:
            return 64 * (4 * y + b) + 32 * j + s
        return 64 * (4 * b + z) + 32 * j + s

    def onehot(p, j, a):
        val = codes_of(p, j)
        hot = jnp.zeros((T, T), F32)
        share = jnp.zeros((T, T), F32)
        for k in range(TOPK):
            m = RT[p, a, k : k + 1, :] == val
            hot = jnp.where(m, 1.0, hot)
            gate = RT[p, a, 8 + k : 9 + k, :].astype(F32) * (1.0 / GATE_DENOM)
            share = jnp.where(m, gate, share)
        return hot, share

    def gather(p, j, a):
        hot, share = onehot(p, j, a)
        hot = hot.astype(BF16)
        for n in range(4):
            cols = pl.ds(n * 512, 512)
            picked = dot_nn(hot, AG[p, a, :, cols])
            if p == 1:
                picked = picked * jnp.sum(share, axis=1, keepdims=True)
            SD[p, j, a, :, cols] = picked.astype(BF16)

    def r_rows(p, a):
        block = a * RING + z if p == 0 else y * RING + a
        return pl.ds(pl.multiple_of(block * S, S), S)

    def r_rows_of(p, a, b):
        block = a * RING + b if p == 0 else b * RING + a
        return pl.ds(pl.multiple_of(block * S, S), S)

    def slots(b):
        return pl.ds(pl.multiple_of(b * S, S), S)

    def s2_send(p, j, a):
        for k in (1, 2, 3):
            b = (b_me[p] + k) % RING
            rcopy(
                SD.at[p, j, a, slots(b)], R.at[p, j, r_rows(p, a)],
                s2_s.at[p, j, k], s2_r.at[p, j, k], b_dev[p](k),
            ).start()
        pltpu.make_async_copy(
            SD.at[p, j, a, slots(b_me[p])], R.at[p, j, r_rows(p, a)], loc.at[p, j]
        ).start()

    def s2_whole(p, j, k):
        return rcopy(SD.at[p, j, 0], R.at[p, j, pl.ds(0, T)], s2_s.at[p, j, k], s2_r.at[p, j, k], b_dev[p](k))

    def loc_whole(p, j):
        return pltpu.make_async_copy(SD.at[p, j, 0], R.at[p, j, pl.ds(0, T)], loc.at[p, j])

    for p in (1, 0):
        gather(p, 0, a_me[p])
        s2_send(p, 0, a_me[p])
    for p in (1, 0):
        ag_copy(p, 0, 0).wait_recv()
        agf_copy(p, 0).start()
        ag_copy(p, 1, 1).wait_recv()
        agf_copy(p, 1).start()
    for p in (1, 0):
        for k in (1, 2, 3):
            rt_copy(p, k).wait_recv()
    for p in (1, 0):
        ag_copy(p, 0, 1).wait_recv()
        gather(p, 0, (a_me[p] + 3) % RING)
        s2_send(p, 0, (a_me[p] + 3) % RING)
        ag_copy(p, 1, 0).wait_recv()
        gather(p, 0, (a_me[p] + 1) % RING)
        s2_send(p, 0, (a_me[p] + 1) % RING)
    for p in (1, 0):
        agf_copy(p, 0).wait_recv()
        agf_copy(p, 1).wait_recv()
        gather(p, 0, (a_me[p] + 2) % RING)
        s2_send(p, 0, (a_me[p] + 2) % RING)

    def gather_later(a, carry):
        for p in (1, 0):
            gather(p, 1, a)
        return carry

    lax.fori_loop(0, RING, gather_later, 0)
    for p in (1, 0):
        for k in (1, 2, 3):
            rt_copy(p, k).wait_send()
        for d in (0, 1):
            for h in (0, 1):
                ag_copy(p, d, h).wait_send()
            agf_copy(p, d).wait_send()

    def s2_sent(j):
        for p in (0, 1):
            for k in (1, 2, 3):
                s2_whole(p, j, k).wait_send()
            loc_whole(p, j).wait()
        for p in (0, 1):
            for k in (1, 2, 3):
                pl.semaphore_signal(credit.at[j], inc=1, device_id=b_dev[p](k), device_id_type=MESH)

    s2_sent(0)

    def send_later(a, carry):
        for p in (1, 0):
            s2_send(p, 1, a)
        return carry

    lax.fori_loop(0, RING, send_later, 0)

    def px_copy(p, j, b):
        src = R.at[p, j, :, pl.ds(pl.multiple_of(b * 512 + (1 - c) * SHARE, SHARE), SHARE)]
        return rcopy(src, PX.at[p, :, pl.ds(b * SHARE, SHARE)], px_s.at[p], px_r.at[p], partner)

    def px_whole(p):
        half = R.at[p, 0, :, pl.ds(0, 4 * SHARE)]
        return rcopy(half, PX.at[p], px_s.at[p], px_r.at[p], partner)

    def pg_copy(cols):
        return rcopy(G.at[:, cols], PG.at[:, cols], pg_s, pg_r, partner)

    pg_whole = rcopy(G, PG, pg_s, pg_r, partner)

    def hidden_part(j):
        for p in (0, 1):
            for k in (1, 2, 3):
                s2_whole(p, j, k).wait_recv()
        if j == 1:
            pl.semaphore_wait(pcredit, 1)
        for p in (0, 1):
            for b in range(RING):
                px_copy(p, j, b).start()
        load_w(j).wait()

        def tile(n, carry):
            at = [pl.ds(pl.multiple_of(i * H + n * 256, 256), 256) for i in range(3)]
            gate = dot_nn(R[0, j], W[:, at[0]])
            up = dot_nn(R[0, j], W[:, at[1]])
            grad = dot_nn(R[1, j], W[:, at[2]])
            sig = jax.nn.sigmoid(gate)
            act = gate * sig
            G[:, at[2]] = (act * up).astype(BF16)
            G[:, at[0]] = (grad * up * sig * (1.0 + gate * (1.0 - sig))).astype(BF16)
            G[:, at[1]] = (grad * act).astype(BF16)
            for i in range(3):
                pg_copy(at[i]).start()
            return carry

        lax.fori_loop(0, 3, tile, 0)

    def outputs_part(j, out, route):
        def tile(n, carry):
            at = pl.ds(pl.multiple_of(n * 512, 512), 512)
            out[:, at] = dot_nt(G[:, 2 * H :], W[at, 2 * H :]).astype(BF16)
            route[:, at] = dot_nt(G[:, : 2 * H], W[at, : 2 * H]).astype(BF16)
            return carry

        lax.fori_loop(0, D // 512, tile, 0)

    def weight_block(j, b, dst):
        mine = pl.ds(pl.multiple_of(b * 512 + c * SHARE, SHARE), SHARE)
        theirs = pl.ds(pl.multiple_of(b * SHARE, SHARE), SHARE)

        def tile(p, first, count):
            def body(n, carry):
                at = pl.ds(pl.multiple_of(first + n * H, H), H)
                acc = dot_tn(R[p, j, :, mine], G[:, at])
                acc = acc + dot_tn(PX[p, :, theirs], PG[:, at])
                dst[:, at] = acc.astype(BF16)
                return carry

            lax.fori_loop(0, count, body, 0)

        tile(0, 0, 2)
        tile(1, 2 * H, 1)

    AH = pl.ds(0, SHARE // 2)
    BH = pl.ds(SHARE // 2, SHARE // 2)

    def x_copy(j, own, d, i):
        to = xdev(1 if d == 0 else 3)
        near = own((x + (1 if d == 0 else 3)) % RING)
        far = own((x + 2) % RING)
        early, late = (AH, BH) if d == 0 else (BH, AH)
        fin = (o_left, o_right)[d].at[j]
        if i == 0:
            src, dst = far.at[early], TMP.at[j, d]
        elif i == 1:
            src, dst = near.at[late], fin.at[late]
        else:
            src, dst = near.at[early], fin.at[early]
        return rcopy(src, dst, x_s.at[j, d, i], x_r.at[j, d, i], to)

    def weight_far(j, own):
        for p in (0, 1):
            px_whole(p).wait_recv()
        pg_whole.wait_recv()
        weight_block(j, (x + 2) % RING, own((x + 2) % RING))
        x_copy(j, own, 0, 0).start()
        x_copy(j, own, 1, 0).start()

    def weight_near(j, own, d):
        b = (x + (1 if d == 0 else 3)) % RING
        weight_block(j, b, own(b))
        x_copy(j, own, d, 1).start()

    def weight_own(j, own):
        weight_block(j, x, own(x))

    def partner_sent():
        for p in (0, 1):
            px_whole(p).wait_send()
        pg_whole.wait_send()

    def x_add(j, own):
        for d in (0, 1):
            early = AH if d == 0 else BH
            near = own((x + (1 if d == 0 else 3)) % RING)
            x_copy(j, own, d, 0).wait_recv()
            near[early, :] = (near[early, :].astype(F32) + TMP[j, d].astype(F32)).astype(BF16)
            x_copy(j, own, d, 2).start()

    def x_arrived(j, own):
        for d in (0, 1):
            for i in (1, 2):
                x_copy(j, own, d, i).wait_recv()

    def x_sent(j, own):
        for d in (0, 1):
            for i in range(3):
                x_copy(j, own, d, i).wait_send()

    def own0(b):
        return OWN.at[b]

    def own1(b):
        return W.at[pl.ds(pl.multiple_of(b * SHARE, SHARE), SHARE)]

    OFFS = (2, 1, 3, 0)

    def back(j, i):
        for p in (0, 1):
            a = (a_me[p] + OFFS[i]) % RING
            for k in (1, 2, 3):
                b = (b_me[p] + k) % RING
                rcopy(
                    O.at[p, j, r_rows_of(p, a, b)], SD.at[p, j, a, slots(b_me[p])],
                    rb_s.at[p, j, k], rb_r.at[p, j, i], b_dev[p](k),
                ).start()
            pltpu.make_async_copy(
                O.at[p, j, r_rows(p, a)], SD.at[p, j, a, slots(b_me[p])], loc_b.at[p, j, i]
            ).start()

    def back_arrived(p, j, i):
        rcopy(
            O.at[p, j, pl.ds(0, 3 * S)], SD.at[p, j, 0, pl.ds(0, 3 * S)],
            rb_s.at[p, j, 1], rb_r.at[p, j, i], b_dev[p](1),
        ).wait_recv()
        pltpu.make_async_copy(
            O.at[p, j, pl.ds(0, S)], SD.at[p, j, 0, pl.ds(0, S)], loc_b.at[p, j, i]
        ).wait()

    def back_sent(p, j, k):
        rcopy(
            O.at[p, j, pl.ds(0, T)], SD.at[p, j, 0], rb_s.at[p, j, k], rb_r.at[p, j, 0], b_dev[p](k)
        ).wait_send()

    hidden_part(0)
    weight_far(0, own0)
    outputs_part(0, O.at[0, 0], O.at[1, 0])
    load_w(1).start()
    pl.semaphore_wait(credit.at[0], 6)
    for i in range(RING):
        back(0, i)
    weight_near(0, own0, 0)
    weight_near(0, own0, 1)
    weight_own(0, own0)
    pl.semaphore_signal(pcredit, inc=1, device_id=partner, device_id_type=MESH)
    partner_sent()
    s2_sent(1)
    hidden_part(1)
    x_add(0, own0)
    outputs_part(1, O.at[0, 1], O.at[1, 1])
    pl.semaphore_wait(credit.at[1], 6)
    back(1, 0)
    weight_far(1, own1)
    back(1, 1)
    weight_near(1, own1, 0)
    back(1, 2)
    weight_near(1, own1, 1)
    back(1, 3)
    weight_own(1, own1)
    partner_sent()

    own_out = pltpu.make_async_copy(own1(x), o_own, out_sem.at[1])
    own_out.start()
    pieces = [
        pltpu.make_async_copy(src.at[0], G.at[pl.ds(d * SHARE, SHARE)], w_sem.at[1 + d])
        for d, src in enumerate((o_left, o_right))
    ]
    sum_out = pltpu.make_async_copy(G.at[pl.ds(0, SHARE)], o_sum, out_sem.at[0])

    def fetch_pieces():
        x_arrived(0, own0)
        for piece in pieces:
            piece.start()

    def sum0():
        for piece in pieces:
            piece.wait()
        G[0:SHARE, :] = (
            own0(x)[...].astype(F32)
            + G[0:SHARE, :].astype(F32)
            + G[SHARE : 2 * SHARE, :].astype(F32)
        ).astype(BF16)
        sum_out.start()

    def fn_copy(p, d, i):
        to = a_dev[p](1 if d == 0 else 3)
        near = (a_me[p] + (1 if d == 0 else 3)) % RING
        far = (a_me[p] + 2) % RING
        fin = FL if d == 0 else FR
        early, late = rows(d), rows(1 - d)
        if i == 0:
            src, dst = AG.at[p, far, early], FT.at[p, d]
        elif i == 1:
            src, dst = AG.at[p, near, late], fin.at[p, late]
        else:
            src, dst = AG.at[p, near, early], fin.at[p, early]
        return rcopy(src, dst, fn_s.at[p, d, i], fn_r.at[p, d, i], to)

    def combine(p, a):
        parts = []
        for j in (0, 1):
            hot, share = onehot(p, j, a)
            if p == 0:
                top = share.astype(BF16)
                parts.append((j, top))
                parts.append((j, (share - top.astype(F32)).astype(BF16)))
            else:
                parts.append((j, hot.astype(BF16)))
        for n in range(4):
            cols = pl.ds(n * 512, 512)
            total = jnp.zeros((T, 512), F32)
            for j, weights in parts:
                total = total + dot_tn(weights, SD[p, j, a, :, cols])
            AG[p, a, :, cols] = total.astype(BF16)

    for i in range(RING):
        if i == 3:
            for p in (0, 1):
                for d in (0, 1):
                    near = (a_me[p] + (1 if d == 0 else 3)) % RING
                    early = rows(d)
                    fn_copy(p, d, 0).wait_recv()
                    AG[p, near, early, :] = (
                        AG[p, near, early, :].astype(F32) + FT[p, d].astype(F32)
                    ).astype(BF16)
                    fn_copy(p, d, 2).start()
            x_add(1, own1)
        for p in (0, 1):
            for j in (0, 1):
                back_arrived(p, j, i)
            combine(p, (a_me[p] + OFFS[i]) % RING)
            if i == 0:
                fn_copy(p, 0, 0).start()
                fn_copy(p, 1, 0).start()
            elif i < 3:
                fn_copy(p, i - 1, 1).start()
        if i == 0:
            fetch_pieces()
        if i == 1:
            sum0()

    def fn_arrived(p):
        for d in (0, 1):
            for i in (1, 2):
                fn_copy(p, d, i).wait_recv()

    results = [
        pltpu.make_async_copy(src, dst, out_sem.at[2 + p]) for p, (src, dst) in enumerate(((uh, o_up), (lg, o_lo)))
    ]
    loads[5].wait()
    loads[6].wait()
    low = lh[...].astype(F32)
    scale = lax.rsqrt(jnp.mean(low * low, axis=1, keepdims=True) + NORM_EPS)
    fn_arrived(0)
    mixture = AG[0, y].astype(F32) + FL[0].astype(F32) + FR[0].astype(F32)
    uh[...] = (uh[...].astype(F32) - mixture).astype(BF16)
    results[0].start()
    fn_arrived(1)
    grad_normed = AG[1, z].astype(F32) + FL[1].astype(F32) + FR[1].astype(F32)
    low = lh[...].astype(F32)
    inner = jnp.mean(low * grad_normed, axis=1, keepdims=True)
    lg[...] = (
        lg[...].astype(F32) + scale * grad_normed - low * (scale * scale * scale) * inner
    ).astype(BF16)
    results[1].start()
    x_arrived(1, own1)

    for p in (0, 1):
        for d in (0, 1):
            for i in range(3):
                fn_copy(p, d, i).wait_send()
        for j in (0, 1):
            for k in (1, 2, 3):
                back_sent(p, j, k)
    x_sent(0, own0)
    x_sent(1, own1)
    for copy in results + [own_out, sum_out]:
        copy.wait()


def run(*arrays):
    hbm = pl.BlockSpec(memory_space=pl.ANY)
    dma = pltpu.SemaphoreType.DMA
    half = jax.ShapeDtypeStruct((SHARE, F), BF16)
    both = jax.ShapeDtypeStruct((2, SHARE, F), BF16)
    rows = jax.ShapeDtypeStruct((T, D), BF16)
    return pl.pallas_call(
        kernel,
        out_shape=(rows, rows, half, half, both, both),
        in_specs=[hbm] * 8,
        out_specs=(hbm,) * 6,
        scratch_shapes=[
            pltpu.VMEM((T, D), BF16),
            pltpu.VMEM((T, D), BF16),
            pltpu.VMEM((T, D), BF16),
            pltpu.VMEM((TOPK, T), jnp.int32),
            pltpu.VMEM((TOPK, T), jnp.int32),
            pltpu.VMEM((TOPK, T), jnp.int32),
            pltpu.VMEM((2, RING, T, D), BF16),
            pltpu.VMEM((2, RING, 16, T), jnp.int32),
            pltpu.VMEM((2, 2, RING, T, D), BF16),
            pltpu.VMEM((2, 2, M, D), BF16),
            pltpu.VMEM((2, 2, M, D), BF16),
            pltpu.VMEM((D, F), BF16),
            pltpu.VMEM((M, F), BF16),
            pltpu.VMEM((2, M, 4 * SHARE), BF16),
            pltpu.VMEM((M, F), BF16),
            pltpu.VMEM((RING, SHARE, F), BF16),
            pltpu.VMEM((2, 2, SHARE // 2, F), BF16),
            pltpu.VMEM((2, T, D), BF16),
            pltpu.VMEM((2, T, D), BF16),
            pltpu.VMEM((2, 2, T // 2, D), BF16),
            dma((2, 2, 2)), dma((2, 2, 2)),
            dma((2, 2)), dma((2, 2)),
            dma((2, 4)), dma((2, 4)),
            dma((2, 2, 4)), dma((2, 2, 4)),
            dma((2, 2, 4)), dma((2, 2, 4)),
            dma((2,)), dma((2,)),
            dma, dma,
            dma((2, 2, 3)), dma((2, 2, 3)),
            dma((2, 2, 3)), dma((2, 2, 3)),
            dma((2, 2)),
            dma((2, 2, 4)),
            dma((3,)),
            dma((7,)),
            dma((4,)),
            pltpu.SemaphoreType.REGULAR((2,)),
            pltpu.SemaphoreType.REGULAR,
        ],
        compiler_params=pltpu.CompilerParams(
            collective_id=0, has_side_effects=True, vmem_limit_bytes=63 * 1024 * 1024
        ),
        cost_estimate=pl.CostEstimate(
            flops=29_000_000_000, bytes_accessed=30_000_000, transcendentals=800_000
        ),
    )(*arrays)


STEPS = 8


def finish_kernel(up, lo, total, own, left, right, o_up, o_lo, o_weight):
    o_up[...] = up[...]
    o_lo[...] = lo[...]
    i = pl.program_id(0)

    @pl.when(i < STEPS // 2)
    def _():
        o_weight[0] = total[...].astype(F32)

    @pl.when(i >= STEPS // 2)
    def _():
        o_weight[0] = own[...].astype(F32) + left[0].astype(F32) + right[0].astype(F32)


def finish(*arrays):
    per = STEPS // 2
    tall = 2 * SHARE // STEPS
    row = pl.BlockSpec((T // STEPS, D), lambda i: (i, 0))
    first = pl.BlockSpec((tall, F), lambda i: (jnp.minimum(i, per - 1), 0))
    second = pl.BlockSpec((tall, F), lambda i: (jnp.maximum(i - per, 0), 0))
    piece = pl.BlockSpec((1, tall, F), lambda i: (1, jnp.maximum(i - per, 0), 0))
    return pl.pallas_call(
        finish_kernel,
        out_shape=(
            jax.ShapeDtypeStruct((T, D), BF16),
            jax.ShapeDtypeStruct((T, D), BF16),
            jax.ShapeDtypeStruct((2, SHARE, F), F32),
        ),
        grid=(STEPS,),
        in_specs=[row, row, first, second, piece, piece],
        out_specs=(row, row, pl.BlockSpec((1, tall, F), lambda i: (i // per, i % per, 0))),
        cost_estimate=pl.CostEstimate(flops=3_000_000, bytes_accessed=11_500_000, transcendentals=0),
    )(*arrays)


def shards(
    upper_half, lower_half, upper_grad, lower_grad, expert_ids, gate_weights, route_slots, expert_weight
):
    return finish(*run(
        upper_half, lower_half, upper_grad, lower_grad,
        expert_ids.T, gate_weights.T, route_slots.T, expert_weight,
    ))


def solution(mesh):
    tok = P(("dp", "expert"), None)
    return jax.shard_map(
        shards,
        mesh=mesh,
        in_specs=(tok,) * 7 + (P("expert", None, None),),
        out_specs=(tok, tok, P("expert", "dp", None)),
        check_vma=False,
    )
```

```python
import functools

import jax
import jax.numpy as jnp
from jax import lax
from jax.experimental import pallas as pl
from jax.experimental.pallas import tpu as pltpu
from jax.sharding import PartitionSpec as P

MESH = pl.DeviceIdType.MESH
F32 = jnp.float32
BF16 = jnp.bfloat16

GATE_DENOM = 1024
NORM_EPS = 1e-06
T = 128
D = 2048
H = 768
F = 3 * H
TOPK = 6
CAP = 30
S = 32
M = 16 * S
RING = 4
SHARE = D // 8


def dot_nt(a, b):
    return lax.dot_general(a, b, (((1,), (1,)), ((), ())), preferred_element_type=F32)


def dot_tn(a, b):
    return lax.dot_general(a, b, (((0,), (0,)), ((), ())), preferred_element_type=F32)


def dot_nn(a, b):
    return lax.dot_general(a, b, (((1,), (0,)), ((), ())), preferred_element_type=F32)


def kernel(
    uh_in, lh_in, ug_in, lg_in, ids_in, gates_in, slots_in, w_hbm,
    o_up, o_lo, o_sum, o_own, o_left, o_right,
    uh, lh, lg, ids, gates, slots_of, AG, RT, SD, R, O, W, G, PX, PG, OWN, TMP, FL, FR, FT,
    ag_s, ag_r, agf_s, agf_r, rt_s, rt_r, s2_s, s2_r, rb_s, rb_r,
    px_s, px_r, pg_s, pg_r, x_s, x_r, fn_s, fn_r, loc, loc_b, w_sem, in_sem, out_sem, credit, pcredit,
):
    dp = lax.axis_index("dp")
    ex = lax.axis_index("expert")
    x, c = dp // 2, dp % 2
    y, z = ex // RING, ex % RING
    a_me = (y, z)
    b_me = (z, y)

    def ydev(k):
        return (dp, ((y + k) % RING) * RING + z)

    def zdev(k):
        return (dp, y * RING + (z + k) % RING)

    def xdev(k):
        return (((x + k) % RING) * 2 + c, ex)

    a_dev = (ydev, zdev)
    b_dev = (zdev, ydev)
    partner = (x * 2 + 1 - c, ex)

    def rcopy(src, dst, ss, rs, dev):
        return pltpu.make_async_remote_copy(
            src_ref=src, dst_ref=dst, send_sem=ss, recv_sem=rs, device_id=dev, device_id_type=MESH
        )

    def load_w(j):
        return pltpu.make_async_copy(w_hbm.at[j], W, w_sem.at[0])

    barrier = pltpu.get_barrier_semaphore()
    peers = [ydev(k) for k in (1, 2, 3)] + [zdev(k) for k in (1, 2, 3)] + [xdev(1), xdev(3), partner]
    for dev in peers:
        pl.semaphore_signal(barrier, inc=1, device_id=dev, device_id_type=MESH)

    pairs = (
        (lh_in, lh), (ug_in, AG.at[1, z]), (ids_in, ids), (gates_in, gates), (slots_in, slots_of),
        (uh_in, uh), (lg_in, lg),
    )
    loads = [pltpu.make_async_copy(src, dst, in_sem.at[i]) for i, (src, dst) in enumerate(pairs)]
    for load in loads:
        load.start()
    load_w(0).start()
    for i in (2, 3, 4):
        loads[i].wait()
    for p in (0, 1):
        RT[p, a_me[p], 0:TOPK, :] = jnp.where(slots_of[...] < CAP, ids[...] * S + slots_of[...], -1)
        RT[p, a_me[p], 8 : 8 + TOPK, :] = gates[...]
    loads[0].wait()
    low = lh[...].astype(F32)
    scale = lax.rsqrt(jnp.mean(low * low, axis=1, keepdims=True) + NORM_EPS)
    AG[0, y] = (low * scale).astype(BF16)
    loads[1].wait()

    pl.semaphore_wait(barrier, len(peers))

    HALF = T // 2

    def rows(h):
        return pl.ds(h * HALF, HALF)

    def rt_copy(p, k):
        me = a_me[p]
        return rcopy(RT.at[p, me], RT.at[p, me], rt_s.at[p, k], rt_r.at[p, k], a_dev[p](k))

    def ag_copy(p, d, h):
        me = a_me[p]
        blk = AG.at[p, me, rows(h)]
        return rcopy(blk, blk, ag_s.at[p, d, h], ag_r.at[p, d, h], a_dev[p](1 if d == 0 else 3))

    def agf_copy(p, d):
        frm = (a_me[p] + (3 if d == 0 else 1)) % RING
        blk = AG.at[p, frm, rows(d)]
        return rcopy(blk, blk, agf_s.at[p, d], agf_r.at[p, d], a_dev[p](1 if d == 0 else 3))

    for p in (1, 0):
        for k in (1, 2, 3):
            rt_copy(p, k).start()
    for p in (1, 0):
        ag_copy(p, 0, 0).start()
        ag_copy(p, 1, 1).start()
    for p in (1, 0):
        ag_copy(p, 0, 1).start()
        ag_copy(p, 1, 0).start()

    row = lax.broadcasted_iota(jnp.int32, (T, T), 0)

    def codes_of(p, j):
        b, s = row >> 5, row & 31
        if p == 0:
            return 64 * (4 * y + b) + 32 * j + s
        return 64 * (4 * b + z) + 32 * j + s

    def onehot(p, j, a):
        val = codes_of(p, j)
        hot = jnp.zeros((T, T), F32)
        share = jnp.zeros((T, T), F32)
        for k in range(TOPK):
            m = RT[p, a, k : k + 1, :] == val
            hot = jnp.where(m, 1.0, hot)
            gate = RT[p, a, 8 + k : 9 + k, :].astype(F32) * (1.0 / GATE_DENOM)
            share = jnp.where(m, gate, share)
        return hot, share

    def gather(p, j, a):
        hot, share = onehot(p, j, a)
        hot = hot.astype(BF16)
        for n in range(4):
            cols = pl.ds(n * 512, 512)
            picked = dot_nn(hot, AG[p, a, :, cols])
            if p == 1:
                picked = picked * jnp.sum(share, axis=1, keepdims=True)
            SD[p, j, a, :, cols] = picked.astype(BF16)

    def r_rows(p, a):
        block = a * RING + z if p == 0 else y * RING + a
        return pl.ds(pl.multiple_of(block * S, S), S)

    def r_rows_of(p, a, b):
        block = a * RING + b if p == 0 else b * RING + a
        return pl.ds(pl.multiple_of(block * S, S), S)

    def slots(b):
        return pl.ds(pl.multiple_of(b * S, S), S)

    def s2_send(p, j, a):
        for k in (1, 2, 3):
            b = (b_me[p] + k) % RING
            rcopy(
                SD.at[p, j, a, slots(b)], R.at[p, j, r_rows(p, a)],
                s2_s.at[p, j, k], s2_r.at[p, j, k], b_dev[p](k),
            ).start()
        pltpu.make_async_copy(
            SD.at[p, j, a, slots(b_me[p])], R.at[p, j, r_rows(p, a)], loc.at[p, j]
        ).start()

    def s2_whole(p, j, k):
        return rcopy(SD.at[p, j, 0], R.at[p, j, pl.ds(0, T)], s2_s.at[p, j, k], s2_r.at[p, j, k], b_dev[p](k))

    def loc_whole(p, j):
        return pltpu.make_async_copy(SD.at[p, j, 0], R.at[p, j, pl.ds(0, T)], loc.at[p, j])

    for p in (1, 0):
        gather(p, 0, a_me[p])
        s2_send(p, 0, a_me[p])
    for p in (1, 0):
        ag_copy(p, 0, 0).wait_recv()
        agf_copy(p, 0).start()
        ag_copy(p, 1, 1).wait_recv()
        agf_copy(p, 1).start()
    for p in (1, 0):
        for k in (1, 2, 3):
            rt_copy(p, k).wait_recv()
    for p in (1, 0):
        ag_copy(p, 0, 1).wait_recv()
        gather(p, 0, (a_me[p] + 3) % RING)
        s2_send(p, 0, (a_me[p] + 3) % RING)
        ag_copy(p, 1, 0).wait_recv()
        gather(p, 0, (a_me[p] + 1) % RING)
        s2_send(p, 0, (a_me[p] + 1) % RING)
    for p in (1, 0):
        agf_copy(p, 0).wait_recv()
        agf_copy(p, 1).wait_recv()
        gather(p, 0, (a_me[p] + 2) % RING)
        s2_send(p, 0, (a_me[p] + 2) % RING)

    def gather_later(a, carry):
        for p in (1, 0):
            gather(p, 1, a)
        return carry

    lax.fori_loop(0, RING, gather_later, 0)
    for p in (1, 0):
        for k in (1, 2, 3):
            rt_copy(p, k).wait_send()
        for d in (0, 1):
            for h in (0, 1):
                ag_copy(p, d, h).wait_send()
            agf_copy(p, d).wait_send()

    def s2_sent(j):
        for p in (0, 1):
            for k in (1, 2, 3):
                s2_whole(p, j, k).wait_send()
            loc_whole(p, j).wait()
        for p in (0, 1):
            for k in (1, 2, 3):
                pl.semaphore_signal(credit.at[j], inc=1, device_id=b_dev[p](k), device_id_type=MESH)

    s2_sent(0)

    def send_later(a, carry):
        for p in (1, 0):
            s2_send(p, 1, a)
        return carry

    lax.fori_loop(0, RING, send_later, 0)

    def px_copy(p, j, b):
        src = R.at[p, j, :, pl.ds(pl.multiple_of(b * 512 + (1 - c) * SHARE, SHARE), SHARE)]
        return rcopy(src, PX.at[p, :, pl.ds(b * SHARE, SHARE)], px_s.at[p], px_r.at[p], partner)

    def px_whole(p):
        half = R.at[p, 0, :, pl.ds(0, 4 * SHARE)]
        return rcopy(half, PX.at[p], px_s.at[p], px_r.at[p], partner)

    def pg_copy(cols):
        return rcopy(G.at[:, cols], PG.at[:, cols], pg_s, pg_r, partner)

    pg_whole = rcopy(G, PG, pg_s, pg_r, partner)

    def hidden_part(j):
        for p in (0, 1):
            for k in (1, 2, 3):
                s2_whole(p, j, k).wait_recv()
        if j == 1:
            pl.semaphore_wait(pcredit, 1)
        for p in (0, 1):
            for b in range(RING):
                px_copy(p, j, b).start()
        load_w(j).wait()

        def tile(n, carry):
            at = [pl.ds(pl.multiple_of(i * H + n * 256, 256), 256) for i in range(3)]
            gate = dot_nn(R[0, j], W[:, at[0]])
            up = dot_nn(R[0, j], W[:, at[1]])
            grad = dot_nn(R[1, j], W[:, at[2]])
            sig = jax.nn.sigmoid(gate)
            act = gate * sig
            G[:, at[2]] = (act * up).astype(BF16)
            G[:, at[0]] = (grad * up * sig * (1.0 + gate * (1.0 - sig))).astype(BF16)
            G[:, at[1]] = (grad * act).astype(BF16)
            for i in range(3):
                pg_copy(at[i]).start()
            return carry

        lax.fori_loop(0, 3, tile, 0)

    def outputs_part(j, out, route):
        def tile(n, carry):
            at = pl.ds(pl.multiple_of(n * 512, 512), 512)
            out[:, at] = dot_nt(G[:, 2 * H :], W[at, 2 * H :]).astype(BF16)
            route[:, at] = dot_nt(G[:, : 2 * H], W[at, : 2 * H]).astype(BF16)
            return carry

        lax.fori_loop(0, D // 512, tile, 0)

    def weight_block(j, b, dst):
        mine = pl.ds(pl.multiple_of(b * 512 + c * SHARE, SHARE), SHARE)
        theirs = pl.ds(pl.multiple_of(b * SHARE, SHARE), SHARE)

        def tile(p, first, count):
            def body(n, carry):
                at = pl.ds(pl.multiple_of(first + n * H, H), H)
                acc = dot_tn(R[p, j, :, mine], G[:, at])
                acc = acc + dot_tn(PX[p, :, theirs], PG[:, at])
                dst[:, at] = acc.astype(BF16)
                return carry

            lax.fori_loop(0, count, body, 0)

        tile(0, 0, 2)
        tile(1, 2 * H, 1)

    AH = pl.ds(0, SHARE // 2)
    BH = pl.ds(SHARE // 2, SHARE // 2)

    def x_copy(j, own, d, i):
        to = xdev(1 if d == 0 else 3)
        near = own((x + (1 if d == 0 else 3)) % RING)
        far = own((x + 2) % RING)
        early, late = (AH, BH) if d == 0 else (BH, AH)
        fin = (o_left, o_right)[d].at[j]
        if i == 0:
            src, dst = far.at[early], TMP.at[j, d]
        elif i == 1:
            src, dst = near.at[late], fin.at[late]
        else:
            src, dst = near.at[early], fin.at[early]
        return rcopy(src, dst, x_s.at[j, d, i], x_r.at[j, d, i], to)

    def weight_far(j, own):
        for p in (0, 1):
            px_whole(p).wait_recv()
        pg_whole.wait_recv()
        weight_block(j, (x + 2) % RING, own((x + 2) % RING))
        x_copy(j, own, 0, 0).start()
        x_copy(j, own, 1, 0).start()

    def weight_near(j, own, d):
        b = (x + (1 if d == 0 else 3)) % RING
        weight_block(j, b, own(b))
        x_copy(j, own, d, 1).start()

    def weight_own(j, own):
        weight_block(j, x, own(x))

    def partner_sent():
        for p in (0, 1):
            px_whole(p).wait_send()
        pg_whole.wait_send()

    def x_add(j, own):
        for d in (0, 1):
            early = AH if d == 0 else BH
            near = own((x + (1 if d == 0 else 3)) % RING)
            x_copy(j, own, d, 0).wait_recv()
            near[early, :] = (near[early, :].astype(F32) + TMP[j, d].astype(F32)).astype(BF16)
            x_copy(j, own, d, 2).start()

    def x_arrived(j, own):
        for d in (0, 1):
            for i in (1, 2):
                x_copy(j, own, d, i).wait_recv()

    def x_sent(j, own):
        for d in (0, 1):
            for i in range(3):
                x_copy(j, own, d, i).wait_send()

    def own0(b):
        return OWN.at[b]

    def own1(b):
        return W.at[pl.ds(pl.multiple_of(b * SHARE, SHARE), SHARE)]

    OFFS = (2, 1, 3, 0)

    def back(j, i):
        for p in (0, 1):
            a = (a_me[p] + OFFS[i]) % RING
            for k in (1, 2, 3):
                b = (b_me[p] + k) % RING
                rcopy(
                    O.at[p, j, r_rows_of(p, a, b)], SD.at[p, j, a, slots(b_me[p])],
                    rb_s.at[p, j, k], rb_r.at[p, j, i], b_dev[p](k),
                ).start()
            pltpu.make_async_copy(
                O.at[p, j, r_rows(p, a)], SD.at[p, j, a, slots(b_me[p])], loc_b.at[p, j, i]
            ).start()

    def back_arrived(p, j, i):
        rcopy(
            O.at[p, j, pl.ds(0, 3 * S)], SD.at[p, j, 0, pl.ds(0, 3 * S)],
            rb_s.at[p, j, 1], rb_r.at[p, j, i], b_dev[p](1),
        ).wait_recv()
        pltpu.make_async_copy(
            O.at[p, j, pl.ds(0, S)], SD.at[p, j, 0, pl.ds(0, S)], loc_b.at[p, j, i]
        ).wait()

    def back_sent(p, j, k):
        rcopy(
            O.at[p, j, pl.ds(0, T)], SD.at[p, j, 0], rb_s.at[p, j, k], rb_r.at[p, j, 0], b_dev[p](k)
        ).wait_send()

    hidden_part(0)
    weight_far(0, own0)
    outputs_part(0, O.at[0, 0], O.at[1, 0])
    load_w(1).start()
    pl.semaphore_wait(credit.at[0], 6)
    for i in range(RING):
        back(0, i)
    weight_near(0, own0, 0)
    weight_near(0, own0, 1)
    weight_own(0, own0)
    pl.semaphore_signal(pcredit, inc=1, device_id=partner, device_id_type=MESH)
    partner_sent()
    s2_sent(1)
    hidden_part(1)
    x_add(0, own0)
    outputs_part(1, O.at[0, 1], O.at[1, 1])
    pl.semaphore_wait(credit.at[1], 6)
    back(1, 0)
    weight_far(1, own1)
    back(1, 1)
    weight_near(1, own1, 0)
    back(1, 2)
    weight_near(1, own1, 1)
    back(1, 3)
    weight_own(1, own1)
    partner_sent()

    own_out = pltpu.make_async_copy(own1(x), o_own, out_sem.at[1])
    own_out.start()
    pieces = [
        pltpu.make_async_copy(src.at[0], G.at[pl.ds(d * SHARE, SHARE)], w_sem.at[1 + d])
        for d, src in enumerate((o_left, o_right))
    ]
    sum_out = pltpu.make_async_copy(G.at[pl.ds(0, SHARE)], o_sum, out_sem.at[0])

    def fetch_pieces():
        x_arrived(0, own0)
        for piece in pieces:
            piece.start()

    def sum0():
        for piece in pieces:
            piece.wait()
        G[0:SHARE, :] = (
            own0(x)[...].astype(F32)
            + G[0:SHARE, :].astype(F32)
            + G[SHARE : 2 * SHARE, :].astype(F32)
        ).astype(BF16)
        sum_out.start()

    def fn_copy(p, d, i):
        to = a_dev[p](1 if d == 0 else 3)
        near = (a_me[p] + (1 if d == 0 else 3)) % RING
        far = (a_me[p] + 2) % RING
        fin = FL if d == 0 else FR
        early, late = rows(d), rows(1 - d)
        if i == 0:
            src, dst = AG.at[p, far, early], FT.at[p, d]
        elif i == 1:
            src, dst = AG.at[p, near, late], fin.at[p, late]
        else:
            src, dst = AG.at[p, near, early], fin.at[p, early]
        return rcopy(src, dst, fn_s.at[p, d, i], fn_r.at[p, d, i], to)

    def combine(p, a):
        parts = []
        for j in (0, 1):
            hot, share = onehot(p, j, a)
            if p == 0:
                top = share.astype(BF16)
                parts.append((j, top))
                parts.append((j, (share - top.astype(F32)).astype(BF16)))
            else:
                parts.append((j, hot.astype(BF16)))
        for n in range(4):
            cols = pl.ds(n * 512, 512)
            total = jnp.zeros((T, 512), F32)
            for j, weights in parts:
                total = total + dot_tn(weights, SD[p, j, a, :, cols])
            AG[p, a, :, cols] = total.astype(BF16)

    for i in range(RING):
        if i == 3:
            for p in (0, 1):
                for d in (0, 1):
                    near = (a_me[p] + (1 if d == 0 else 3)) % RING
                    early = rows(d)
                    fn_copy(p, d, 0).wait_recv()
                    AG[p, near, early, :] = (
                        AG[p, near, early, :].astype(F32) + FT[p, d].astype(F32)
                    ).astype(BF16)
                    fn_copy(p, d, 2).start()
            x_add(1, own1)
        for p in (0, 1):
            for j in (0, 1):
                back_arrived(p, j, i)
            combine(p, (a_me[p] + OFFS[i]) % RING)
            if i == 0:
                fn_copy(p, 0, 0).start()
                fn_copy(p, 1, 0).start()
            elif i < 3:
                fn_copy(p, i - 1, 1).start()
        if i == 0:
            fetch_pieces()
        if i == 1:
            sum0()

    def fn_arrived(p):
        for d in (0, 1):
            for i in (1, 2):
                fn_copy(p, d, i).wait_recv()

    results = [
        pltpu.make_async_copy(src, dst, out_sem.at[2 + p]) for p, (src, dst) in enumerate(((uh, o_up), (lg, o_lo)))
    ]
    loads[5].wait()
    loads[6].wait()
    low = lh[...].astype(F32)
    scale = lax.rsqrt(jnp.mean(low * low, axis=1, keepdims=True) + NORM_EPS)
    fn_arrived(0)
    mixture = AG[0, y].astype(F32) + FL[0].astype(F32) + FR[0].astype(F32)
    uh[...] = (uh[...].astype(F32) - mixture).astype(BF16)
    results[0].start()
    fn_arrived(1)
    grad_normed = AG[1, z].astype(F32) + FL[1].astype(F32) + FR[1].astype(F32)
    low = lh[...].astype(F32)
    inner = jnp.mean(low * grad_normed, axis=1, keepdims=True)
    lg[...] = (
        lg[...].astype(F32) + scale * grad_normed - low * (scale * scale * scale) * inner
    ).astype(BF16)
    results[1].start()
    x_arrived(1, own1)

    for p in (0, 1):
        for d in (0, 1):
            for i in range(3):
                fn_copy(p, d, i).wait_send()
        for j in (0, 1):
            for k in (1, 2, 3):
                back_sent(p, j, k)
    x_sent(0, own0)
    x_sent(1, own1)
    for copy in results + [own_out, sum_out]:
        copy.wait()


def run(*arrays):
    hbm = pl.BlockSpec(memory_space=pl.ANY)
    dma = pltpu.SemaphoreType.DMA
    half = jax.ShapeDtypeStruct((SHARE, F), BF16)
    both = jax.ShapeDtypeStruct((2, SHARE, F), BF16)
    rows = jax.ShapeDtypeStruct((T, D), BF16)
    return pl.pallas_call(
        kernel,
        out_shape=(rows, rows, half, half, both, both),
        in_specs=[hbm] * 8,
        out_specs=(hbm,) * 6,
        scratch_shapes=[
            pltpu.VMEM((T, D), BF16),
            pltpu.VMEM((T, D), BF16),
            pltpu.VMEM((T, D), BF16),
            pltpu.VMEM((TOPK, T), jnp.int32),
            pltpu.VMEM((TOPK, T), jnp.int32),
            pltpu.VMEM((TOPK, T), jnp.int32),
            pltpu.VMEM((2, RING, T, D), BF16),
            pltpu.VMEM((2, RING, 16, T), jnp.int32),
            pltpu.VMEM((2, 2, RING, T, D), BF16),
            pltpu.VMEM((2, 2, M, D), BF16),
            pltpu.VMEM((2, 2, M, D), BF16),
            pltpu.VMEM((D, F), BF16),
            pltpu.VMEM((M, F), BF16),
            pltpu.VMEM((2, M, 4 * SHARE), BF16),
            pltpu.VMEM((M, F), BF16),
            pltpu.VMEM((RING, SHARE, F), BF16),
            pltpu.VMEM((2, 2, SHARE // 2, F), BF16),
            pltpu.VMEM((2, T, D), BF16),
            pltpu.VMEM((2, T, D), BF16),
            pltpu.VMEM((2, 2, T // 2, D), BF16),
            dma((2, 2, 2)), dma((2, 2, 2)),
            dma((2, 2)), dma((2, 2)),
            dma((2, 4)), dma((2, 4)),
            dma((2, 2, 4)), dma((2, 2, 4)),
            dma((2, 2, 4)), dma((2, 2, 4)),
            dma((2,)), dma((2,)),
            dma, dma,
            dma((2, 2, 3)), dma((2, 2, 3)),
            dma((2, 2, 3)), dma((2, 2, 3)),
            dma((2, 2)),
            dma((2, 2, 4)),
            dma((3,)),
            dma((7,)),
            dma((4,)),
            pltpu.SemaphoreType.REGULAR((2,)),
            pltpu.SemaphoreType.REGULAR,
        ],
        compiler_params=pltpu.CompilerParams(
            collective_id=0, has_side_effects=True, vmem_limit_bytes=63 * 1024 * 1024
        ),
        cost_estimate=pl.CostEstimate(
            flops=29_000_000_000, bytes_accessed=30_000_000, transcendentals=800_000
        ),
    )(*arrays)


def finish_kernel(up, lo, total, own, left, right, o_up, o_lo, o_weight, parts, wide, pass_sem, in_sem, out_sem):
    half = SHARE // 2
    loads = []
    for q in range(4):
        at = pl.ds((q % 2) * half, half)
        srcs = (total.at[at],) if q < 2 else (own.at[at], left.at[1, at], right.at[1, at])
        loads.append([
            pltpu.make_async_copy(src, parts.at[q, i], in_sem.at[q, i]) for i, src in enumerate(srcs)
        ])
    passed = [
        pltpu.make_async_copy(src, dst, pass_sem.at[i]) for i, (src, dst) in enumerate(((up, o_up), (lo, o_lo)))
    ]
    for load in loads[0] + loads[1] + loads[2] + loads[3] + passed:
        load.start()
    stores = []
    for q in range(4):
        for load in loads[q]:
            load.wait()
        value = parts[q, 0].astype(F32)
        if q >= 2:
            value = value + parts[q, 1].astype(F32) + parts[q, 2].astype(F32)
        wide[q] = value
        store = pltpu.make_async_copy(wide.at[q], o_weight.at[q // 2, pl.ds((q % 2) * half, half)], out_sem.at[q])
        store.start()
        stores.append(store)
    for copy in passed + stores:
        copy.wait()


def finish(*arrays):
    hbm = pl.BlockSpec(memory_space=pl.ANY)
    dma = pltpu.SemaphoreType.DMA
    return pl.pallas_call(
        finish_kernel,
        out_shape=(
            jax.ShapeDtypeStruct((T, D), BF16),
            jax.ShapeDtypeStruct((T, D), BF16),
            jax.ShapeDtypeStruct((2, SHARE, F), F32),
        ),
        in_specs=[hbm] * 6,
        out_specs=(hbm,) * 3,
        scratch_shapes=[
            pltpu.VMEM((4, 3, SHARE // 2, F), BF16),
            pltpu.VMEM((4, SHARE // 2, F), F32),
            dma((2,)), dma((4, 3)), dma((4,)),
        ],
        compiler_params=pltpu.CompilerParams(vmem_limit_bytes=60 * 1024 * 1024),
        cost_estimate=pl.CostEstimate(flops=3_000_000, bytes_accessed=11_500_000, transcendentals=0),
    )(*arrays)


def shards(
    upper_half, lower_half, upper_grad, lower_grad, expert_ids, gate_weights, route_slots, expert_weight
):
    return finish(*run(
        upper_half, lower_half, upper_grad, lower_grad,
        expert_ids.T, gate_weights.T, route_slots.T, expert_weight,
    ))


def solution(mesh):
    tok = P(("dp", "expert"), None)
    return jax.shard_map(
        shards,
        mesh=mesh,
        in_specs=(tok,) * 7 + (P("expert", None, None),),
        out_specs=(tok, tok, P("expert", "dp", None)),
        check_vma=False,
    )
```

```python
import functools

import jax
import jax.numpy as jnp
from jax import lax
from jax.experimental import pallas as pl
from jax.experimental.pallas import tpu as pltpu
from jax.sharding import PartitionSpec as P

MESH = pl.DeviceIdType.MESH
F32 = jnp.float32
BF16 = jnp.bfloat16

GATE_DENOM = 1024
NORM_EPS = 1e-06
T = 128
D = 2048
H = 768
F = 3 * H
TOPK = 6
CAP = 30
S = 32
M = 16 * S
RING = 4
SHARE = D // 8


def dot_nt(a, b):
    return lax.dot_general(a, b, (((1,), (1,)), ((), ())), preferred_element_type=F32)


def dot_tn(a, b):
    return lax.dot_general(a, b, (((0,), (0,)), ((), ())), preferred_element_type=F32)


def dot_nn(a, b):
    return lax.dot_general(a, b, (((1,), (0,)), ((), ())), preferred_element_type=F32)


def kernel(
    uh_in, lh_in, ug_in, lg_in, ids_in, gates_in, slots_in, w_hbm,
    o_up, o_lo, o_sum, o_own, o_left, o_right,
    uh, lh, lg, ids, gates, slots_of, AG, RT, SD, R, O, W, G, PX, PG, OWN, TMP, FL, FR, FT,
    ag_s, ag_r, agf_s, agf_r, rt_s, rt_r, s2_s, s2_r, rb_s, rb_r,
    px_s, px_r, pg_s, pg_r, x_s, x_r, fn_s, fn_r, loc, loc_b, w_sem, in_sem, out_sem, credit, pcredit,
):
    dp = lax.axis_index("dp")
    ex = lax.axis_index("expert")
    x, c = dp // 2, dp % 2
    y, z = ex // RING, ex % RING
    a_me = (y, z)
    b_me = (z, y)

    def ydev(k):
        return (dp, ((y + k) % RING) * RING + z)

    def zdev(k):
        return (dp, y * RING + (z + k) % RING)

    def xdev(k):
        return (((x + k) % RING) * 2 + c, ex)

    a_dev = (ydev, zdev)
    b_dev = (zdev, ydev)
    partner = (x * 2 + 1 - c, ex)

    def rcopy(src, dst, ss, rs, dev):
        return pltpu.make_async_remote_copy(
            src_ref=src, dst_ref=dst, send_sem=ss, recv_sem=rs, device_id=dev, device_id_type=MESH
        )

    def load_w(j):
        return pltpu.make_async_copy(w_hbm.at[j], W, w_sem.at[0])

    barrier = pltpu.get_barrier_semaphore()
    peers = [ydev(k) for k in (1, 2, 3)] + [zdev(k) for k in (1, 2, 3)] + [xdev(1), xdev(3), partner]
    for dev in peers:
        pl.semaphore_signal(barrier, inc=1, device_id=dev, device_id_type=MESH)

    pairs = (
        (lh_in, lh), (ug_in, AG.at[1, z]), (ids_in, ids), (gates_in, gates), (slots_in, slots_of),
        (uh_in, uh), (lg_in, lg),
    )
    loads = [pltpu.make_async_copy(src, dst, in_sem.at[i]) for i, (src, dst) in enumerate(pairs)]
    for load in loads:
        load.start()
    load_w(0).start()
    for i in (2, 3, 4):
        loads[i].wait()
    for p in (0, 1):
        RT[p, a_me[p], 0:TOPK, :] = jnp.where(slots_of[...] < CAP, ids[...] * S + slots_of[...], -1)
        RT[p, a_me[p], 8 : 8 + TOPK, :] = gates[...]
    loads[0].wait()
    low = lh[...].astype(F32)
    scale = lax.rsqrt(jnp.mean(low * low, axis=1, keepdims=True) + NORM_EPS)
    AG[0, y] = (low * scale).astype(BF16)
    loads[1].wait()

    pl.semaphore_wait(barrier, len(peers))

    HALF = T // 2

    def rows(h):
        return pl.ds(h * HALF, HALF)

    def rt_copy(p, k):
        me = a_me[p]
        return rcopy(RT.at[p, me], RT.at[p, me], rt_s.at[p, k], rt_r.at[p, k], a_dev[p](k))

    def ag_copy(p, d, h):
        me = a_me[p]
        blk = AG.at[p, me, rows(h)]
        return rcopy(blk, blk, ag_s.at[p, d, h], ag_r.at[p, d, h], a_dev[p](1 if d == 0 else 3))

    def agf_copy(p, d):
        frm = (a_me[p] + (3 if d == 0 else 1)) % RING
        blk = AG.at[p, frm, rows(d)]
        return rcopy(blk, blk, agf_s.at[p, d], agf_r.at[p, d], a_dev[p](1 if d == 0 else 3))

    for p in (1, 0):
        for k in (1, 2, 3):
            rt_copy(p, k).start()
    for p in (1, 0):
        ag_copy(p, 0, 0).start()
        ag_copy(p, 1, 1).start()
    for p in (1, 0):
        ag_copy(p, 0, 1).start()
        ag_copy(p, 1, 0).start()

    row = lax.broadcasted_iota(jnp.int32, (T, T), 0)

    def codes_of(p, j):
        b, s = row >> 5, row & 31
        if p == 0:
            return 64 * (4 * y + b) + 32 * j + s
        return 64 * (4 * b + z) + 32 * j + s

    def onehot(p, j, a):
        val = codes_of(p, j)
        hot = jnp.zeros((T, T), F32)
        share = jnp.zeros((T, T), F32)
        for k in range(TOPK):
            m = RT[p, a, k : k + 1, :] == val
            hot = jnp.where(m, 1.0, hot)
            gate = RT[p, a, 8 + k : 9 + k, :].astype(F32) * (1.0 / GATE_DENOM)
            share = jnp.where(m, gate, share)
        return hot, share

    def gather(p, j, a):
        hot, share = onehot(p, j, a)
        hot = hot.astype(BF16)
        for n in range(4):
            cols = pl.ds(n * 512, 512)
            picked = dot_nn(hot, AG[p, a, :, cols])
            if p == 1:
                picked = picked * jnp.sum(share, axis=1, keepdims=True)
            SD[p, j, a, :, cols] = picked.astype(BF16)

    def r_rows(p, a):
        block = a * RING + z if p == 0 else y * RING + a
        return pl.ds(pl.multiple_of(block * S, S), S)

    def r_rows_of(p, a, b):
        block = a * RING + b if p == 0 else b * RING + a
        return pl.ds(pl.multiple_of(block * S, S), S)

    def slots(b):
        return pl.ds(pl.multiple_of(b * S, S), S)

    def s2_send(p, j, a):
        for k in (1, 2, 3):
            b = (b_me[p] + k) % RING
            rcopy(
                SD.at[p, j, a, slots(b)], R.at[p, j, r_rows(p, a)],
                s2_s.at[p, j, k], s2_r.at[p, j, k], b_dev[p](k),
            ).start()
        pltpu.make_async_copy(
            SD.at[p, j, a, slots(b_me[p])], R.at[p, j, r_rows(p, a)], loc.at[p, j]
        ).start()

    def s2_whole(p, j, k):
        return rcopy(SD.at[p, j, 0], R.at[p, j, pl.ds(0, T)], s2_s.at[p, j, k], s2_r.at[p, j, k], b_dev[p](k))

    def loc_whole(p, j):
        return pltpu.make_async_copy(SD.at[p, j, 0], R.at[p, j, pl.ds(0, T)], loc.at[p, j])

    for p in (1, 0):
        gather(p, 0, a_me[p])
        s2_send(p, 0, a_me[p])
    for p in (1, 0):
        ag_copy(p, 0, 0).wait_recv()
        agf_copy(p, 0).start()
        ag_copy(p, 1, 1).wait_recv()
        agf_copy(p, 1).start()
    for p in (1, 0):
        for k in (1, 2, 3):
            rt_copy(p, k).wait_recv()
    for p in (1, 0):
        ag_copy(p, 0, 1).wait_recv()
        gather(p, 0, (a_me[p] + 3) % RING)
        s2_send(p, 0, (a_me[p] + 3) % RING)
        ag_copy(p, 1, 0).wait_recv()
        gather(p, 0, (a_me[p] + 1) % RING)
        s2_send(p, 0, (a_me[p] + 1) % RING)
    for p in (1, 0):
        agf_copy(p, 0).wait_recv()
        agf_copy(p, 1).wait_recv()
        gather(p, 0, (a_me[p] + 2) % RING)
        s2_send(p, 0, (a_me[p] + 2) % RING)

    def gather_later(a, carry):
        for p in (1, 0):
            gather(p, 1, a)
        return carry

    lax.fori_loop(0, RING, gather_later, 0)
    for p in (1, 0):
        for k in (1, 2, 3):
            rt_copy(p, k).wait_send()
        for d in (0, 1):
            for h in (0, 1):
                ag_copy(p, d, h).wait_send()
            agf_copy(p, d).wait_send()

    def s2_sent(j):
        for p in (0, 1):
            for k in (1, 2, 3):
                s2_whole(p, j, k).wait_send()
            loc_whole(p, j).wait()
        for p in (0, 1):
            for k in (1, 2, 3):
                pl.semaphore_signal(credit.at[j], inc=1, device_id=b_dev[p](k), device_id_type=MESH)

    s2_sent(0)

    def send_later(a, carry):
        for p in (1, 0):
            s2_send(p, 1, a)
        return carry

    lax.fori_loop(0, RING, send_later, 0)

    def px_copy(p, j, b):
        src = R.at[p, j, :, pl.ds(pl.multiple_of(b * 512 + (1 - c) * SHARE, SHARE), SHARE)]
        return rcopy(src, PX.at[p, :, pl.ds(b * SHARE, SHARE)], px_s.at[p], px_r.at[p], partner)

    def px_whole(p):
        half = R.at[p, 0, :, pl.ds(0, 4 * SHARE)]
        return rcopy(half, PX.at[p], px_s.at[p], px_r.at[p], partner)

    def pg_copy(cols):
        return rcopy(G.at[:, cols], PG.at[:, cols], pg_s, pg_r, partner)

    pg_whole = rcopy(G, PG, pg_s, pg_r, partner)

    def hidden_part(j):
        for p in (0, 1):
            for k in (1, 2, 3):
                s2_whole(p, j, k).wait_recv()
        if j == 1:
            pl.semaphore_wait(pcredit, 1)
        for p in (0, 1):
            for b in range(RING):
                px_copy(p, j, b).start()
        load_w(j).wait()

        def tile(n, carry):
            at = [pl.ds(pl.multiple_of(i * H + n * 256, 256), 256) for i in range(3)]
            gate = dot_nn(R[0, j], W[:, at[0]])
            up = dot_nn(R[0, j], W[:, at[1]])
            grad = dot_nn(R[1, j], W[:, at[2]])
            sig = jax.nn.sigmoid(gate)
            act = gate * sig
            G[:, at[2]] = (act * up).astype(BF16)
            G[:, at[0]] = (grad * up * sig * (1.0 + gate * (1.0 - sig))).astype(BF16)
            G[:, at[1]] = (grad * act).astype(BF16)
            for i in range(3):
                pg_copy(at[i]).start()
            return carry

        lax.fori_loop(0, 3, tile, 0)

    def outputs_part(j, out, route):
        def tile(n, carry):
            at = pl.ds(pl.multiple_of(n * 512, 512), 512)
            out[:, at] = dot_nt(G[:, 2 * H :], W[at, 2 * H :]).astype(BF16)
            route[:, at] = dot_nt(G[:, : 2 * H], W[at, : 2 * H]).astype(BF16)
            return carry

        lax.fori_loop(0, D // 512, tile, 0)

    def weight_block(j, b, dst):
        mine = pl.ds(pl.multiple_of(b * 512 + c * SHARE, SHARE), SHARE)
        theirs = pl.ds(pl.multiple_of(b * SHARE, SHARE), SHARE)

        def tile(p, first, count):
            def body(n, carry):
                at = pl.ds(pl.multiple_of(first + n * H, H), H)
                acc = dot_tn(R[p, j, :, mine], G[:, at])
                acc = acc + dot_tn(PX[p, :, theirs], PG[:, at])
                dst[:, at] = acc.astype(BF16)
                return carry

            lax.fori_loop(0, count, body, 0)

        tile(0, 0, 2)
        tile(1, 2 * H, 1)

    AH = pl.ds(0, SHARE // 2)
    BH = pl.ds(SHARE // 2, SHARE // 2)

    def x_copy(j, own, d, i):
        to = xdev(1 if d == 0 else 3)
        near = own((x + (1 if d == 0 else 3)) % RING)
        far = own((x + 2) % RING)
        early, late = (AH, BH) if d == 0 else (BH, AH)
        fin = (o_left, o_right)[d].at[j]
        if i == 0:
            src, dst = far.at[early], TMP.at[j, d]
        elif i == 1:
            src, dst = near.at[late], fin.at[late]
        else:
            src, dst = near.at[early], fin.at[early]
        return rcopy(src, dst, x_s.at[j, d, i], x_r.at[j, d, i], to)

    def weight_far(j, own):
        for p in (0, 1):
            px_whole(p).wait_recv()
        pg_whole.wait_recv()
        weight_block(j, (x + 2) % RING, own((x + 2) % RING))
        x_copy(j, own, 0, 0).start()
        x_copy(j, own, 1, 0).start()

    def weight_near(j, own, d):
        b = (x + (1 if d == 0 else 3)) % RING
        weight_block(j, b, own(b))
        x_copy(j, own, d, 1).start()

    def weight_own(j, own):
        weight_block(j, x, own(x))

    def partner_sent():
        for p in (0, 1):
            px_whole(p).wait_send()
        pg_whole.wait_send()

    def x_add(j, own):
        for d in (0, 1):
            early = AH if d == 0 else BH
            near = own((x + (1 if d == 0 else 3)) % RING)
            x_copy(j, own, d, 0).wait_recv()
            near[early, :] = (near[early, :].astype(F32) + TMP[j, d].astype(F32)).astype(BF16)
            x_copy(j, own, d, 2).start()

    def x_arrived(j, own):
        for d in (0, 1):
            for i in (1, 2):
                x_copy(j, own, d, i).wait_recv()

    def x_sent(j, own):
        for d in (0, 1):
            for i in range(3):
                x_copy(j, own, d, i).wait_send()

    def own0(b):
        return OWN.at[b]

    def own1(b):
        return W.at[pl.ds(pl.multiple_of(b * SHARE, SHARE), SHARE)]

    OFFS = (2, 1, 3, 0)

    def back(j, i):
        for p in (0, 1):
            a = (a_me[p] + OFFS[i]) % RING
            for k in (1, 2, 3):
                b = (b_me[p] + k) % RING
                rcopy(
                    O.at[p, j, r_rows_of(p, a, b)], SD.at[p, j, a, slots(b_me[p])],
                    rb_s.at[p, j, k], rb_r.at[p, j, i], b_dev[p](k),
                ).start()
            pltpu.make_async_copy(
                O.at[p, j, r_rows(p, a)], SD.at[p, j, a, slots(b_me[p])], loc_b.at[p, j, i]
            ).start()

    def back_arrived(p, j, i):
        rcopy(
            O.at[p, j, pl.ds(0, 3 * S)], SD.at[p, j, 0, pl.ds(0, 3 * S)],
            rb_s.at[p, j, 1], rb_r.at[p, j, i], b_dev[p](1),
        ).wait_recv()
        pltpu.make_async_copy(
            O.at[p, j, pl.ds(0, S)], SD.at[p, j, 0, pl.ds(0, S)], loc_b.at[p, j, i]
        ).wait()

    def back_sent(p, j, k):
        rcopy(
            O.at[p, j, pl.ds(0, T)], SD.at[p, j, 0], rb_s.at[p, j, k], rb_r.at[p, j, 0], b_dev[p](k)
        ).wait_send()

    hidden_part(0)
    weight_far(0, own0)
    outputs_part(0, O.at[0, 0], O.at[1, 0])
    load_w(1).start()
    pl.semaphore_wait(credit.at[0], 6)
    for i in range(RING):
        back(0, i)
    weight_near(0, own0, 0)
    weight_near(0, own0, 1)
    weight_own(0, own0)
    pl.semaphore_signal(pcredit, inc=1, device_id=partner, device_id_type=MESH)
    partner_sent()
    s2_sent(1)
    hidden_part(1)
    x_add(0, own0)
    outputs_part(1, O.at[0, 1], O.at[1, 1])
    pl.semaphore_wait(credit.at[1], 6)
    back(1, 0)
    weight_far(1, own1)
    back(1, 1)
    weight_near(1, own1, 0)
    back(1, 2)
    weight_near(1, own1, 1)
    back(1, 3)
    weight_own(1, own1)
    partner_sent()

    own_out = pltpu.make_async_copy(own1(x), o_own, out_sem.at[1])
    own_out.start()
    pieces = [
        pltpu.make_async_copy(src.at[0], G.at[pl.ds(d * SHARE, SHARE)], w_sem.at[1 + d])
        for d, src in enumerate((o_left, o_right))
    ]
    sum_out = pltpu.make_async_copy(G.at[pl.ds(0, SHARE)], o_sum, out_sem.at[0])

    def fetch_pieces():
        x_arrived(0, own0)
        for piece in pieces:
            piece.start()

    def sum0():
        for piece in pieces:
            piece.wait()
        G[0:SHARE, :] = (
            own0(x)[...].astype(F32)
            + G[0:SHARE, :].astype(F32)
            + G[SHARE : 2 * SHARE, :].astype(F32)
        ).astype(BF16)
        sum_out.start()

    def fn_copy(p, d, i):
        to = a_dev[p](1 if d == 0 else 3)
        near = (a_me[p] + (1 if d == 0 else 3)) % RING
        far = (a_me[p] + 2) % RING
        fin = FL if d == 0 else FR
        early, late = rows(d), rows(1 - d)
        if i == 0:
            src, dst = AG.at[p, far, early], FT.at[p, d]
        elif i == 1:
            src, dst = AG.at[p, near, late], fin.at[p, late]
        else:
            src, dst = AG.at[p, near, early], fin.at[p, early]
        return rcopy(src, dst, fn_s.at[p, d, i], fn_r.at[p, d, i], to)

    def combine(p, a):
        parts = []
        for j in (0, 1):
            hot, share = onehot(p, j, a)
            if p == 0:
                top = share.astype(BF16)
                parts.append((j, top))
                parts.append((j, (share - top.astype(F32)).astype(BF16)))
            else:
                parts.append((j, hot.astype(BF16)))
        for n in range(4):
            cols = pl.ds(n * 512, 512)
            total = jnp.zeros((T, 512), F32)
            for j, weights in parts:
                total = total + dot_tn(weights, SD[p, j, a, :, cols])
            AG[p, a, :, cols] = total.astype(BF16)

    for i in range(RING):
        if i == 3:
            for p in (0, 1):
                for d in (0, 1):
                    near = (a_me[p] + (1 if d == 0 else 3)) % RING
                    early = rows(d)
                    fn_copy(p, d, 0).wait_recv()
                    AG[p, near, early, :] = (
                        AG[p, near, early, :].astype(F32) + FT[p, d].astype(F32)
                    ).astype(BF16)
                    fn_copy(p, d, 2).start()
            x_add(1, own1)
        for p in (0, 1):
            for j in (0, 1):
                back_arrived(p, j, i)
            combine(p, (a_me[p] + OFFS[i]) % RING)
            if i == 0:
                fn_copy(p, 0, 0).start()
                fn_copy(p, 1, 0).start()
            elif i < 3:
                fn_copy(p, i - 1, 1).start()
        if i == 0:
            fetch_pieces()
        if i == 1:
            sum0()

    def fn_arrived(p):
        for d in (0, 1):
            for i in (1, 2):
                fn_copy(p, d, i).wait_recv()

    results = [
        pltpu.make_async_copy(src, dst, out_sem.at[2 + p]) for p, (src, dst) in enumerate(((uh, o_up), (lg, o_lo)))
    ]
    loads[5].wait()
    loads[6].wait()
    low = lh[...].astype(F32)
    scale = lax.rsqrt(jnp.mean(low * low, axis=1, keepdims=True) + NORM_EPS)
    fn_arrived(0)
    mixture = AG[0, y].astype(F32) + FL[0].astype(F32) + FR[0].astype(F32)
    uh[...] = (uh[...].astype(F32) - mixture).astype(BF16)
    results[0].start()
    fn_arrived(1)
    grad_normed = AG[1, z].astype(F32) + FL[1].astype(F32) + FR[1].astype(F32)
    low = lh[...].astype(F32)
    inner = jnp.mean(low * grad_normed, axis=1, keepdims=True)
    lg[...] = (
        lg[...].astype(F32) + scale * grad_normed - low * (scale * scale * scale) * inner
    ).astype(BF16)
    results[1].start()
    x_arrived(1, own1)

    for p in (0, 1):
        for d in (0, 1):
            for i in range(3):
                fn_copy(p, d, i).wait_send()
        for j in (0, 1):
            for k in (1, 2, 3):
                back_sent(p, j, k)
    x_sent(0, own0)
    x_sent(1, own1)
    for copy in results + [own_out, sum_out]:
        copy.wait()


def run(*arrays):
    hbm = pl.BlockSpec(memory_space=pl.ANY)
    dma = pltpu.SemaphoreType.DMA
    half = jax.ShapeDtypeStruct((SHARE, F), BF16)
    both = jax.ShapeDtypeStruct((2, SHARE, F), BF16)
    rows = jax.ShapeDtypeStruct((T, D), BF16)
    return pl.pallas_call(
        kernel,
        out_shape=(rows, rows, half, half, both, both),
        in_specs=[hbm] * 8,
        out_specs=(hbm,) * 6,
        scratch_shapes=[
            pltpu.VMEM((T, D), BF16),
            pltpu.VMEM((T, D), BF16),
            pltpu.VMEM((T, D), BF16),
            pltpu.VMEM((TOPK, T), jnp.int32),
            pltpu.VMEM((TOPK, T), jnp.int32),
            pltpu.VMEM((TOPK, T), jnp.int32),
            pltpu.VMEM((2, RING, T, D), BF16),
            pltpu.VMEM((2, RING, 16, T), jnp.int32),
            pltpu.VMEM((2, 2, RING, T, D), BF16),
            pltpu.VMEM((2, 2, M, D), BF16),
            pltpu.VMEM((2, 2, M, D), BF16),
            pltpu.VMEM((D, F), BF16),
            pltpu.VMEM((M, F), BF16),
            pltpu.VMEM((2, M, 4 * SHARE), BF16),
            pltpu.VMEM((M, F), BF16),
            pltpu.VMEM((RING, SHARE, F), BF16),
            pltpu.VMEM((2, 2, SHARE // 2, F), BF16),
            pltpu.VMEM((2, T, D), BF16),
            pltpu.VMEM((2, T, D), BF16),
            pltpu.VMEM((2, 2, T // 2, D), BF16),
            dma((2, 2, 2)), dma((2, 2, 2)),
            dma((2, 2)), dma((2, 2)),
            dma((2, 4)), dma((2, 4)),
            dma((2, 2, 4)), dma((2, 2, 4)),
            dma((2, 2, 4)), dma((2, 2, 4)),
            dma((2,)), dma((2,)),
            dma, dma,
            dma((2, 2, 3)), dma((2, 2, 3)),
            dma((2, 2, 3)), dma((2, 2, 3)),
            dma((2, 2)),
            dma((2, 2, 4)),
            dma((3,)),
            dma((7,)),
            dma((4,)),
            pltpu.SemaphoreType.REGULAR((2,)),
            pltpu.SemaphoreType.REGULAR,
        ],
        compiler_params=pltpu.CompilerParams(
            collective_id=0, has_side_effects=True, vmem_limit_bytes=63 * 1024 * 1024
        ),
        cost_estimate=pl.CostEstimate(
            flops=29_000_000_000, bytes_accessed=30_000_000, transcendentals=800_000
        ),
    )(*arrays)


def finish_kernel(up, lo, total, own, left, right, o_up, o_lo, o_weight, parts, wide, tok, tok_sem, in_sem, out_sem):
    half = SHARE // 2
    loads = []
    for q in range(4):
        at = pl.ds((q % 2) * half, half)
        srcs = (total.at[at],) if q < 2 else (own.at[at], left.at[1, at], right.at[1, at])
        loads.append([
            pltpu.make_async_copy(src, parts.at[q, i], in_sem.at[q, i]) for i, src in enumerate(srcs)
        ])
    fetched = [pltpu.make_async_copy(src, tok.at[i], tok_sem.at[i, 0]) for i, src in enumerate((up, lo))]
    passed = [pltpu.make_async_copy(tok.at[i], dst, tok_sem.at[i, 1]) for i, dst in enumerate((o_up, o_lo))]
    for load in loads[0] + fetched + loads[1] + loads[2] + loads[3]:
        load.start()
    stores = []
    for q in range(4):
        for load in loads[q]:
            load.wait()
        value = parts[q, 0].astype(F32)
        if q >= 2:
            value = value + parts[q, 1].astype(F32) + parts[q, 2].astype(F32)
        wide[q] = value
        store = pltpu.make_async_copy(wide.at[q], o_weight.at[q // 2, pl.ds((q % 2) * half, half)], out_sem.at[q])
        store.start()
        stores.append(store)
        if q < 2:
            fetched[q].wait()
            passed[q].start()
    for copy in passed + stores:
        copy.wait()


def finish(*arrays):
    hbm = pl.BlockSpec(memory_space=pl.ANY)
    dma = pltpu.SemaphoreType.DMA
    return pl.pallas_call(
        finish_kernel,
        out_shape=(
            jax.ShapeDtypeStruct((T, D), BF16),
            jax.ShapeDtypeStruct((T, D), BF16),
            jax.ShapeDtypeStruct((2, SHARE, F), F32),
        ),
        in_specs=[hbm] * 6,
        out_specs=(hbm,) * 3,
        scratch_shapes=[
            pltpu.VMEM((4, 3, SHARE // 2, F), BF16),
            pltpu.VMEM((4, SHARE // 2, F), F32),
            pltpu.VMEM((2, T, D), BF16),
            dma((2, 2)), dma((4, 3)), dma((4,)),
        ],
        compiler_params=pltpu.CompilerParams(vmem_limit_bytes=60 * 1024 * 1024),
        cost_estimate=pl.CostEstimate(flops=3_000_000, bytes_accessed=11_500_000, transcendentals=0),
    )(*arrays)


def shards(
    upper_half, lower_half, upper_grad, lower_grad, expert_ids, gate_weights, route_slots, expert_weight
):
    return finish(*run(
        upper_half, lower_half, upper_grad, lower_grad,
        expert_ids.T, gate_weights.T, route_slots.T, expert_weight,
    ))


def solution(mesh):
    tok = P(("dp", "expert"), None)
    return jax.shard_map(
        shards,
        mesh=mesh,
        in_specs=(tok,) * 7 + (P("expert", None, None),),
        out_specs=(tok, tok, P("expert", "dp", None)),
        check_vma=False,
    )
```

```python
import functools

import jax
import jax.numpy as jnp
from jax import lax
from jax.experimental import pallas as pl
from jax.experimental.pallas import tpu as pltpu
from jax.sharding import PartitionSpec as P

MESH = pl.DeviceIdType.MESH
F32 = jnp.float32
BF16 = jnp.bfloat16

GATE_DENOM = 1024
NORM_EPS = 1e-06
T = 128
D = 2048
H = 768
F = 3 * H
TOPK = 6
CAP = 30
S = 32
EARLY = 2
LATE = 4 * (CAP - EARLY)
M = 16 * S
RING = 4
SHARE = D // 8


def dot_nt(a, b):
    return lax.dot_general(a, b, (((1,), (1,)), ((), ())), preferred_element_type=F32)


def dot_tn(a, b):
    return lax.dot_general(a, b, (((0,), (0,)), ((), ())), preferred_element_type=F32)


def dot_nn(a, b):
    return lax.dot_general(a, b, (((1,), (0,)), ((), ())), preferred_element_type=F32)


def kernel(
    uh_in, lh_in, ug_in, lg_in, ids_in, gates_in, slots_in, w_hbm,
    o_up, o_lo, o_sum, o_own, o_left, o_right,
    uh, lh, lg, ids, gates, slots_of, AG, RT, SD, R, O, W, G, PX, PG, OWN, TMP, FL, FR, FT,
    ag_s, ag_r, agf_s, agf_r, rt_s, rt_r, s2_s, s2_r, rb_s, rb_r,
    px_s, px_r, pg_s, pg_r, x_s, x_r, fn_s, fn_r, loc, loc_b, w_sem, in_sem, out_sem, credit, pcredit,
):
    dp = lax.axis_index("dp")
    ex = lax.axis_index("expert")
    x, c = dp // 2, dp % 2
    y, z = ex // RING, ex % RING
    a_me = (y, z)
    b_me = (z, y)

    def ydev(k):
        return (dp, ((y + k) % RING) * RING + z)

    def zdev(k):
        return (dp, y * RING + (z + k) % RING)

    def xdev(k):
        return (((x + k) % RING) * 2 + c, ex)

    a_dev = (ydev, zdev)
    b_dev = (zdev, ydev)
    partner = (x * 2 + 1 - c, ex)

    def rcopy(src, dst, ss, rs, dev):
        return pltpu.make_async_remote_copy(
            src_ref=src, dst_ref=dst, send_sem=ss, recv_sem=rs, device_id=dev, device_id_type=MESH
        )

    def load_w(j):
        return pltpu.make_async_copy(w_hbm.at[j], W, w_sem.at[0])

    barrier = pltpu.get_barrier_semaphore()
    peers = [ydev(k) for k in (1, 2, 3)] + [zdev(k) for k in (1, 2, 3)] + [xdev(1), xdev(3), partner]
    for dev in peers:
        pl.semaphore_signal(barrier, inc=1, device_id=dev, device_id_type=MESH)

    pairs = (
        (lh_in, lh), (ug_in, AG.at[1, z]), (ids_in, ids), (gates_in, gates), (slots_in, slots_of),
        (uh_in, uh), (lg_in, lg),
    )
    loads = [pltpu.make_async_copy(src, dst, in_sem.at[i]) for i, (src, dst) in enumerate(pairs)]
    for load in loads:
        load.start()
    load_w(0).start()
    for i in (2, 3, 4):
        loads[i].wait()
    for p in (0, 1):
        RT[p, a_me[p], 0:TOPK, :] = jnp.where(slots_of[...] < CAP, ids[...] * S + slots_of[...], -1)
        RT[p, a_me[p], 8 : 8 + TOPK, :] = gates[...]
    loads[0].wait()
    low = lh[...].astype(F32)
    scale = lax.rsqrt(jnp.mean(low * low, axis=1, keepdims=True) + NORM_EPS)
    AG[0, y] = (low * scale).astype(BF16)
    loads[1].wait()

    for p in (0, 1):
        for line in range(RING):
            O[p, 1, line * T + LATE : (line + 1) * T, :] = jnp.zeros((T - LATE, D), BF16)

    pl.semaphore_wait(barrier, len(peers))

    HALF = T // 2

    def rows(h):
        return pl.ds(h * HALF, HALF)

    def rt_copy(p, k):
        me = a_me[p]
        return rcopy(RT.at[p, me], RT.at[p, me], rt_s.at[p, k], rt_r.at[p, k], a_dev[p](k))

    def ag_copy(p, d, h):
        me = a_me[p]
        blk = AG.at[p, me, rows(h)]
        return rcopy(blk, blk, ag_s.at[p, d, h], ag_r.at[p, d, h], a_dev[p](1 if d == 0 else 3))

    def agf_copy(p, d):
        frm = (a_me[p] + (3 if d == 0 else 1)) % RING
        blk = AG.at[p, frm, rows(d)]
        return rcopy(blk, blk, agf_s.at[p, d], agf_r.at[p, d], a_dev[p](1 if d == 0 else 3))

    for p in (1, 0):
        for k in (1, 2, 3):
            rt_copy(p, k).start()
    for p in (1, 0):
        ag_copy(p, 0, 0).start()
        ag_copy(p, 1, 1).start()
    for p in (1, 0):
        ag_copy(p, 0, 1).start()
        ag_copy(p, 1, 0).start()

    row = lax.broadcasted_iota(jnp.int32, (T, T), 0)

    def codes_of(p, j, filled=False):
        b, s = row >> 5, row & 31
        if filled:
            s = jnp.where(s < CAP, s, s + S - EARLY)
        if p == 0:
            return 64 * (4 * y + b) + 32 * j + s
        return 64 * (4 * b + z) + 32 * j + s

    def onehot(p, j, a, filled=False):
        val = codes_of(p, j, filled)
        hot = jnp.zeros((T, T), F32)
        share = jnp.zeros((T, T), F32)
        for k in range(TOPK):
            m = RT[p, a, k : k + 1, :] == val
            hot = jnp.where(m, 1.0, hot)
            gate = RT[p, a, 8 + k : 9 + k, :].astype(F32) * (1.0 / GATE_DENOM)
            share = jnp.where(m, gate, share)
        return hot, share

    def gather(p, j, a):
        hot, share = onehot(p, j, a, True)
        hot = hot.astype(BF16)
        for n in range(4):
            cols = pl.ds(n * 512, 512)
            picked = dot_nn(hot, AG[p, a, :, cols])
            if p == 1:
                picked = picked * jnp.sum(share, axis=1, keepdims=True)
            SD[p, j, a, :, cols] = picked.astype(BF16)

    def r_rows(p, a):
        block = a * RING + z if p == 0 else y * RING + a
        return pl.ds(pl.multiple_of(block * S, S), S)

    def r_rows_of(p, a, b):
        block = a * RING + b if p == 0 else b * RING + a
        return pl.ds(pl.multiple_of(block * S, S), S)

    def slots(b):
        return pl.ds(pl.multiple_of(b * S, S), S)

    def s2_send(p, j, a):
        for k in (1, 2, 3):
            b = (b_me[p] + k) % RING
            rcopy(
                SD.at[p, j, a, slots(b)], R.at[p, j, r_rows(p, a)],
                s2_s.at[p, j, k], s2_r.at[p, j, k], b_dev[p](k),
            ).start()
        pltpu.make_async_copy(
            SD.at[p, j, a, slots(b_me[p])], R.at[p, j, r_rows(p, a)], loc.at[p, j]
        ).start()

    def raw(p, line):
        return O.at[p, 1, pl.ds(pl.multiple_of(line * T, T), LATE)]

    def s2_whole(p, j, k):
        if j == 0:
            src, dst = SD.at[p, j, 0], R.at[p, j, pl.ds(0, T)]
        else:
            src, dst = SD.at[p, j, (b_me[p] + k) % RING, pl.ds(0, LATE)], raw(p, b_me[p])
        return rcopy(src, dst, s2_s.at[p, j, k], s2_r.at[p, j, k], b_dev[p](k))

    def loc_whole(p, j):
        if j == 0:
            src, dst = SD.at[p, j, 0], R.at[p, j, pl.ds(0, T)]
        else:
            src, dst = SD.at[p, j, b_me[p], pl.ds(0, LATE)], raw(p, b_me[p])
        return pltpu.make_async_copy(src, dst, loc.at[p, j])

    def gather_late(p):
        shape = (RING * LATE, T)
        r = lax.broadcasted_iota(jnp.int32, shape, 0)

        def over(v, step):
            return sum((v >= step * i).astype(jnp.int32) for i in (1, 2, 3))

        b = over(r, LATE)
        r = r - LATE * b
        owner = over(r, CAP - EARLY)
        s = r - (CAP - EARLY) * owner
        val = 64 * (4 * y + b if p == 0 else 4 * b + z) + S + s
        share = jnp.zeros(shape, F32)
        hots = []
        for a in range(RING):
            mine = jnp.where(owner == a, val, -2)
            hot = jnp.zeros(shape, F32)
            for k in range(TOPK):
                m = RT[p, a, k : k + 1, :] == mine
                hot = jnp.where(m, 1.0, hot)
                if p == 1:
                    gate = RT[p, a, 8 + k : 9 + k, :].astype(F32) * (1.0 / GATE_DENOM)
                    share = jnp.where(m, gate, share)
            hots.append(hot.astype(BF16))
        for n in range(4):
            cols = pl.ds(n * 512, 512)
            picked = jnp.zeros((RING * LATE, 512), F32)
            for a in range(RING):
                picked = picked + dot_nn(hots[a], AG[p, a, :, cols])
            if p == 1:
                picked = picked * jnp.sum(share, axis=1, keepdims=True)
            for b in range(RING):
                SD[p, 1, b, 0:LATE, cols] = picked[b * LATE : (b + 1) * LATE].astype(BF16)

    def unpack():
        r = lax.broadcasted_iota(jnp.int32, (T, T), 0)
        q = lax.broadcasted_iota(jnp.int32, (T, T), 1)
        s = r & 31
        sent = (s < CAP - EARLY) & (q == (r >> 5) * (CAP - EARLY) + s)
        early = (s >= CAP - EARLY) & (s < CAP) & (q == r + EARLY)
        sent = jnp.where(sent, 1.0, 0.0).astype(BF16)
        early = jnp.where(early, 1.0, 0.0).astype(BF16)
        for p in (0, 1):
            for line in range(RING):
                blocks = [(a * RING + line if p == 0 else line * RING + a) * S for a in range(RING)]
                for n in range(4):
                    cols = pl.ds(n * 512, 512)
                    first = jnp.concatenate([R[p, 0, i : i + S, cols] for i in blocks], axis=0)
                    value = dot_nn(sent, O[p, 1, line * T : (line + 1) * T, cols]) + dot_nn(early, first)
                    value = value.astype(BF16)
                    for a, i in enumerate(blocks):
                        R[p, 1, i : i + S, cols] = value[a * S : (a + 1) * S]

    for p in (1, 0):
        gather(p, 0, a_me[p])
        s2_send(p, 0, a_me[p])
    for p in (1, 0):
        ag_copy(p, 0, 0).wait_recv()
        agf_copy(p, 0).start()
        ag_copy(p, 1, 1).wait_recv()
        agf_copy(p, 1).start()
    for p in (1, 0):
        for k in (1, 2, 3):
            rt_copy(p, k).wait_recv()
    for p in (1, 0):
        ag_copy(p, 0, 1).wait_recv()
        gather(p, 0, (a_me[p] + 3) % RING)
        s2_send(p, 0, (a_me[p] + 3) % RING)
        ag_copy(p, 1, 0).wait_recv()
        gather(p, 0, (a_me[p] + 1) % RING)
        s2_send(p, 0, (a_me[p] + 1) % RING)
    for p in (1, 0):
        agf_copy(p, 0).wait_recv()
        agf_copy(p, 1).wait_recv()
        gather(p, 0, (a_me[p] + 2) % RING)
        s2_send(p, 0, (a_me[p] + 2) % RING)

    for p in (1, 0):
        gather_late(p)
    for p in (1, 0):
        for k in (1, 2, 3):
            rt_copy(p, k).wait_send()
        for d in (0, 1):
            for h in (0, 1):
                ag_copy(p, d, h).wait_send()
            agf_copy(p, d).wait_send()

    def s2_sent(j):
        for p in (0, 1):
            for k in (1, 2, 3):
                s2_whole(p, j, k).wait_send()
            loc_whole(p, j).wait()
        for p in (0, 1):
            for k in (1, 2, 3):
                pl.semaphore_signal(credit.at[j], inc=1, device_id=b_dev[p](k), device_id_type=MESH)

    s2_sent(0)

    for p in (1, 0):
        for k in (1, 2, 3):
            s2_whole(p, 1, k).start()
        loc_whole(p, 1).start()

    def px_copy(p, j, b):
        src = R.at[p, j, :, pl.ds(pl.multiple_of(b * 512 + (1 - c) * SHARE, SHARE), SHARE)]
        return rcopy(src, PX.at[p, :, pl.ds(b * SHARE, SHARE)], px_s.at[p], px_r.at[p], partner)

    def px_whole(p):
        half = R.at[p, 0, :, pl.ds(0, 4 * SHARE)]
        return rcopy(half, PX.at[p], px_s.at[p], px_r.at[p], partner)

    def pg_copy(cols):
        return rcopy(G.at[:, cols], PG.at[:, cols], pg_s, pg_r, partner)

    pg_whole = rcopy(G, PG, pg_s, pg_r, partner)

    def hidden_part(j):
        for p in (0, 1):
            for k in (1, 2, 3):
                s2_whole(p, j, k).wait_recv()
        if j == 1:
            unpack()
            pl.semaphore_wait(pcredit, 1)
        for p in (0, 1):
            for b in range(RING):
                px_copy(p, j, b).start()
        load_w(j).wait()

        def tile(n, carry):
            at = [pl.ds(pl.multiple_of(i * H + n * 256, 256), 256) for i in range(3)]
            gate = dot_nn(R[0, j], W[:, at[0]])
            up = dot_nn(R[0, j], W[:, at[1]])
            grad = dot_nn(R[1, j], W[:, at[2]])
            sig = jax.nn.sigmoid(gate)
            act = gate * sig
            parts = (grad * up * sig * (1.0 + gate * (1.0 - sig)), grad * act, act * up)
            if j == 0:
                live = (lax.broadcasted_iota(jnp.int32, (M, 256), 0) & 31) < CAP
                parts = [jnp.where(live, part, 0.0) for part in parts]
            for i in range(3):
                G[:, at[i]] = parts[i].astype(BF16)
            for i in range(3):
                pg_copy(at[i]).start()
            return carry

        lax.fori_loop(0, 3, tile, 0)

    def outputs_part(j, out, route):
        def tile(n, carry):
            at = pl.ds(pl.multiple_of(n * 512, 512), 512)
            out[:, at] = dot_nt(G[:, 2 * H :], W[at, 2 * H :]).astype(BF16)
            route[:, at] = dot_nt(G[:, : 2 * H], W[at, : 2 * H]).astype(BF16)
            return carry

        lax.fori_loop(0, D // 512, tile, 0)

    def weight_block(j, b, dst):
        mine = pl.ds(pl.multiple_of(b * 512 + c * SHARE, SHARE), SHARE)
        theirs = pl.ds(pl.multiple_of(b * SHARE, SHARE), SHARE)

        def tile(p, first, count):
            def body(n, carry):
                at = pl.ds(pl.multiple_of(first + n * H, H), H)
                acc = dot_tn(R[p, j, :, mine], G[:, at])
                acc = acc + dot_tn(PX[p, :, theirs], PG[:, at])
                dst[:, at] = acc.astype(BF16)
                return carry

            lax.fori_loop(0, count, body, 0)

        tile(0, 0, 2)
        tile(1, 2 * H, 1)

    AH = pl.ds(0, SHARE // 2)
    BH = pl.ds(SHARE // 2, SHARE // 2)

    def x_copy(j, own, d, i):
        to = xdev(1 if d == 0 else 3)
        near = own((x + (1 if d == 0 else 3)) % RING)
        far = own((x + 2) % RING)
        early, late = (AH, BH) if d == 0 else (BH, AH)
        fin = (o_left, o_right)[d].at[j]
        if i == 0:
            src, dst = far.at[early], TMP.at[j, d]
        elif i == 1:
            src, dst = near.at[late], fin.at[late]
        else:
            src, dst = near.at[early], fin.at[early]
        return rcopy(src, dst, x_s.at[j, d, i], x_r.at[j, d, i], to)

    def weight_far(j, own):
        for p in (0, 1):
            px_whole(p).wait_recv()
        pg_whole.wait_recv()
        weight_block(j, (x + 2) % RING, own((x + 2) % RING))
        x_copy(j, own, 0, 0).start()
        x_copy(j, own, 1, 0).start()

    def weight_near(j, own, d):
        b = (x + (1 if d == 0 else 3)) % RING
        weight_block(j, b, own(b))
        x_copy(j, own, d, 1).start()

    def weight_own(j, own):
        weight_block(j, x, own(x))

    def partner_sent():
        for p in (0, 1):
            px_whole(p).wait_send()
        pg_whole.wait_send()

    def x_add(j, own):
        for d in (0, 1):
            early = AH if d == 0 else BH
            near = own((x + (1 if d == 0 else 3)) % RING)
            x_copy(j, own, d, 0).wait_recv()
            near[early, :] = (near[early, :].astype(F32) + TMP[j, d].astype(F32)).astype(BF16)
            x_copy(j, own, d, 2).start()

    def x_arrived(j, own):
        for d in (0, 1):
            for i in (1, 2):
                x_copy(j, own, d, i).wait_recv()

    def x_sent(j, own):
        for d in (0, 1):
            for i in range(3):
                x_copy(j, own, d, i).wait_send()

    def own0(b):
        return OWN.at[b]

    def own1(b):
        return W.at[pl.ds(pl.multiple_of(b * SHARE, SHARE), SHARE)]

    OFFS = (2, 1, 3, 0)

    def back(j, i):
        for p in (0, 1):
            a = (a_me[p] + OFFS[i]) % RING
            for k in (1, 2, 3):
                b = (b_me[p] + k) % RING
                rcopy(
                    O.at[p, j, r_rows_of(p, a, b)], SD.at[p, j, a, slots(b_me[p])],
                    rb_s.at[p, j, k], rb_r.at[p, j, i], b_dev[p](k),
                ).start()
            pltpu.make_async_copy(
                O.at[p, j, r_rows(p, a)], SD.at[p, j, a, slots(b_me[p])], loc_b.at[p, j, i]
            ).start()

    def back_arrived(p, j, i):
        rcopy(
            O.at[p, j, pl.ds(0, 3 * S)], SD.at[p, j, 0, pl.ds(0, 3 * S)],
            rb_s.at[p, j, 1], rb_r.at[p, j, i], b_dev[p](1),
        ).wait_recv()
        pltpu.make_async_copy(
            O.at[p, j, pl.ds(0, S)], SD.at[p, j, 0, pl.ds(0, S)], loc_b.at[p, j, i]
        ).wait()

    def back_sent(p, j, k):
        rcopy(
            O.at[p, j, pl.ds(0, T)], SD.at[p, j, 0], rb_s.at[p, j, k], rb_r.at[p, j, 0], b_dev[p](k)
        ).wait_send()

    hidden_part(0)
    weight_far(0, own0)
    outputs_part(0, O.at[0, 0], O.at[1, 0])
    load_w(1).start()
    pl.semaphore_wait(credit.at[0], 6)
    for i in range(RING):
        back(0, i)
    weight_near(0, own0, 0)
    weight_near(0, own0, 1)
    weight_own(0, own0)
    pl.semaphore_signal(pcredit, inc=1, device_id=partner, device_id_type=MESH)
    partner_sent()
    s2_sent(1)
    hidden_part(1)
    x_add(0, own0)
    outputs_part(1, O.at[0, 1], O.at[1, 1])
    pl.semaphore_wait(credit.at[1], 6)
    back(1, 0)
    weight_far(1, own1)
    back(1, 1)
    weight_near(1, own1, 0)
    back(1, 2)
    weight_near(1, own1, 1)
    back(1, 3)
    weight_own(1, own1)
    partner_sent()

    own_out = pltpu.make_async_copy(own1(x), o_own, out_sem.at[1])
    own_out.start()
    pieces = [
        pltpu.make_async_copy(src.at[0], G.at[pl.ds(d * SHARE, SHARE)], w_sem.at[1 + d])
        for d, src in enumerate((o_left, o_right))
    ]
    sum_out = pltpu.make_async_copy(G.at[pl.ds(0, SHARE)], o_sum, out_sem.at[0])

    def fetch_pieces():
        x_arrived(0, own0)
        for piece in pieces:
            piece.start()

    def sum0():
        for piece in pieces:
            piece.wait()
        G[0:SHARE, :] = (
            own0(x)[...].astype(F32)
            + G[0:SHARE, :].astype(F32)
            + G[SHARE : 2 * SHARE, :].astype(F32)
        ).astype(BF16)
        sum_out.start()

    def fn_copy(p, d, i):
        to = a_dev[p](1 if d == 0 else 3)
        near = (a_me[p] + (1 if d == 0 else 3)) % RING
        far = (a_me[p] + 2) % RING
        fin = FL if d == 0 else FR
        early, late = rows(d), rows(1 - d)
        if i == 0:
            src, dst = AG.at[p, far, early], FT.at[p, d]
        elif i == 1:
            src, dst = AG.at[p, near, late], fin.at[p, late]
        else:
            src, dst = AG.at[p, near, early], fin.at[p, early]
        return rcopy(src, dst, fn_s.at[p, d, i], fn_r.at[p, d, i], to)

    def combine(p, a):
        parts = []
        for j in (0, 1):
            hot, share = onehot(p, j, a)
            if p == 0:
                top = share.astype(BF16)
                parts.append((j, top))
                parts.append((j, (share - top.astype(F32)).astype(BF16)))
            else:
                parts.append((j, hot.astype(BF16)))
        for n in range(4):
            cols = pl.ds(n * 512, 512)
            total = jnp.zeros((T, 512), F32)
            for j, weights in parts:
                total = total + dot_tn(weights, SD[p, j, a, :, cols])
            AG[p, a, :, cols] = total.astype(BF16)

    for i in range(RING):
        if i == 3:
            for p in (0, 1):
                for d in (0, 1):
                    near = (a_me[p] + (1 if d == 0 else 3)) % RING
                    early = rows(d)
                    fn_copy(p, d, 0).wait_recv()
                    AG[p, near, early, :] = (
                        AG[p, near, early, :].astype(F32) + FT[p, d].astype(F32)
                    ).astype(BF16)
                    fn_copy(p, d, 2).start()
            x_add(1, own1)
        for p in (0, 1):
            for j in (0, 1):
                back_arrived(p, j, i)
            combine(p, (a_me[p] + OFFS[i]) % RING)
            if i == 0:
                fn_copy(p, 0, 0).start()
                fn_copy(p, 1, 0).start()
            elif i < 3:
                fn_copy(p, i - 1, 1).start()
        if i == 0:
            fetch_pieces()
        if i == 1:
            sum0()

    def fn_arrived(p):
        for d in (0, 1):
            for i in (1, 2):
                fn_copy(p, d, i).wait_recv()

    results = [
        pltpu.make_async_copy(src, dst, out_sem.at[2 + p]) for p, (src, dst) in enumerate(((uh, o_up), (lg, o_lo)))
    ]
    loads[5].wait()
    loads[6].wait()
    low = lh[...].astype(F32)
    scale = lax.rsqrt(jnp.mean(low * low, axis=1, keepdims=True) + NORM_EPS)
    fn_arrived(0)
    mixture = AG[0, y].astype(F32) + FL[0].astype(F32) + FR[0].astype(F32)
    uh[...] = (uh[...].astype(F32) - mixture).astype(BF16)
    results[0].start()
    fn_arrived(1)
    grad_normed = AG[1, z].astype(F32) + FL[1].astype(F32) + FR[1].astype(F32)
    low = lh[...].astype(F32)
    inner = jnp.mean(low * grad_normed, axis=1, keepdims=True)
    lg[...] = (
        lg[...].astype(F32) + scale * grad_normed - low * (scale * scale * scale) * inner
    ).astype(BF16)
    results[1].start()
    x_arrived(1, own1)

    for p in (0, 1):
        for d in (0, 1):
            for i in range(3):
                fn_copy(p, d, i).wait_send()
        for j in (0, 1):
            for k in (1, 2, 3):
                back_sent(p, j, k)
    x_sent(0, own0)
    x_sent(1, own1)
    for copy in results + [own_out, sum_out]:
        copy.wait()


def run(*arrays):
    hbm = pl.BlockSpec(memory_space=pl.ANY)
    dma = pltpu.SemaphoreType.DMA
    half = jax.ShapeDtypeStruct((SHARE, F), BF16)
    both = jax.ShapeDtypeStruct((2, SHARE, F), BF16)
    rows = jax.ShapeDtypeStruct((T, D), BF16)
    return pl.pallas_call(
        kernel,
        out_shape=(rows, rows, half, half, both, both),
        in_specs=[hbm] * 8,
        out_specs=(hbm,) * 6,
        scratch_shapes=[
            pltpu.VMEM((T, D), BF16),
            pltpu.VMEM((T, D), BF16),
            pltpu.VMEM((T, D), BF16),
            pltpu.VMEM((TOPK, T), jnp.int32),
            pltpu.VMEM((TOPK, T), jnp.int32),
            pltpu.VMEM((TOPK, T), jnp.int32),
            pltpu.VMEM((2, RING, T, D), BF16),
            pltpu.VMEM((2, RING, 16, T), jnp.int32),
            pltpu.VMEM((2, 2, RING, T, D), BF16),
            pltpu.VMEM((2, 2, M, D), BF16),
            pltpu.VMEM((2, 2, M, D), BF16),
            pltpu.VMEM((D, F), BF16),
            pltpu.VMEM((M, F), BF16),
            pltpu.VMEM((2, M, 4 * SHARE), BF16),
            pltpu.VMEM((M, F), BF16),
            pltpu.VMEM((RING, SHARE, F), BF16),
            pltpu.VMEM((2, 2, SHARE // 2, F), BF16),
            pltpu.VMEM((2, T, D), BF16),
            pltpu.VMEM((2, T, D), BF16),
            pltpu.VMEM((2, 2, T // 2, D), BF16),
            dma((2, 2, 2)), dma((2, 2, 2)),
            dma((2, 2)), dma((2, 2)),
            dma((2, 4)), dma((2, 4)),
            dma((2, 2, 4)), dma((2, 2, 4)),
            dma((2, 2, 4)), dma((2, 2, 4)),
            dma((2,)), dma((2,)),
            dma, dma,
            dma((2, 2, 3)), dma((2, 2, 3)),
            dma((2, 2, 3)), dma((2, 2, 3)),
            dma((2, 2)),
            dma((2, 2, 4)),
            dma((3,)),
            dma((7,)),
            dma((4,)),
            pltpu.SemaphoreType.REGULAR((2,)),
            pltpu.SemaphoreType.REGULAR,
        ],
        compiler_params=pltpu.CompilerParams(
            collective_id=0, has_side_effects=True, vmem_limit_bytes=63 * 1024 * 1024
        ),
        cost_estimate=pl.CostEstimate(
            flops=29_000_000_000, bytes_accessed=30_000_000, transcendentals=800_000
        ),
    )(*arrays)


def finish_kernel(up, lo, total, own, left, right, o_up, o_lo, o_weight, parts, wide, tok, tok_sem, in_sem, out_sem):
    half = SHARE // 2
    loads = []
    for q in range(4):
        at = pl.ds((q % 2) * half, half)
        srcs = (total.at[at],) if q < 2 else (own.at[at], left.at[1, at], right.at[1, at])
        loads.append([
            pltpu.make_async_copy(src, parts.at[q, i], in_sem.at[q, i]) for i, src in enumerate(srcs)
        ])
    fetched = [pltpu.make_async_copy(src, tok.at[i], tok_sem.at[i, 0]) for i, src in enumerate((up, lo))]
    passed = [pltpu.make_async_copy(tok.at[i], dst, tok_sem.at[i, 1]) for i, dst in enumerate((o_up, o_lo))]
    for load in loads[0] + fetched + loads[1] + loads[2] + loads[3]:
        load.start()
    stores = []
    for q in range(4):
        for load in loads[q]:
            load.wait()
        value = parts[q, 0].astype(F32)
        if q >= 2:
            value = value + parts[q, 1].astype(F32) + parts[q, 2].astype(F32)
        wide[q] = value
        store = pltpu.make_async_copy(wide.at[q], o_weight.at[q // 2, pl.ds((q % 2) * half, half)], out_sem.at[q])
        store.start()
        stores.append(store)
        if q < 2:
            fetched[q].wait()
            passed[q].start()
    for copy in passed + stores:
        copy.wait()


def finish(*arrays):
    hbm = pl.BlockSpec(memory_space=pl.ANY)
    dma = pltpu.SemaphoreType.DMA
    return pl.pallas_call(
        finish_kernel,
        out_shape=(
            jax.ShapeDtypeStruct((T, D), BF16),
            jax.ShapeDtypeStruct((T, D), BF16),
            jax.ShapeDtypeStruct((2, SHARE, F), F32),
        ),
        in_specs=[hbm] * 6,
        out_specs=(hbm,) * 3,
        scratch_shapes=[
            pltpu.VMEM((4, 3, SHARE // 2, F), BF16),
            pltpu.VMEM((4, SHARE // 2, F), F32),
            pltpu.VMEM((2, T, D), BF16),
            dma((2, 2)), dma((4, 3)), dma((4,)),
        ],
        compiler_params=pltpu.CompilerParams(vmem_limit_bytes=60 * 1024 * 1024),
        cost_estimate=pl.CostEstimate(flops=3_000_000, bytes_accessed=11_500_000, transcendentals=0),
    )(*arrays)


def shards(
    upper_half, lower_half, upper_grad, lower_grad, expert_ids, gate_weights, route_slots, expert_weight
):
    return finish(*run(
        upper_half, lower_half, upper_grad, lower_grad,
        expert_ids.T, gate_weights.T, route_slots.T, expert_weight,
    ))


def solution(mesh):
    tok = P(("dp", "expert"), None)
    return jax.shard_map(
        shards,
        mesh=mesh,
        in_specs=(tok,) * 7 + (P("expert", None, None),),
        out_specs=(tok, tok, P("expert", "dp", None)),
        check_vma=False,
    )
```

```python
import functools

import jax
import jax.numpy as jnp
from jax import lax
from jax.experimental import pallas as pl
from jax.experimental.pallas import tpu as pltpu
from jax.sharding import PartitionSpec as P

MESH = pl.DeviceIdType.MESH
F32 = jnp.float32
BF16 = jnp.bfloat16

GATE_DENOM = 1024
NORM_EPS = 1e-06
T = 128
D = 2048
H = 768
F = 3 * H
TOPK = 6
CAP = 30
S = 32
M = 16 * S
RING = 4
SHARE = D // 8


def dot_nt(a, b):
    return lax.dot_general(a, b, (((1,), (1,)), ((), ())), preferred_element_type=F32)


def dot_tn(a, b):
    return lax.dot_general(a, b, (((0,), (0,)), ((), ())), preferred_element_type=F32)


def dot_nn(a, b):
    return lax.dot_general(a, b, (((1,), (0,)), ((), ())), preferred_element_type=F32)


def kernel(
    uh_in, lh_in, ug_in, lg_in, ids_in, gates_in, slots_in, w_hbm,
    o_up, o_lo, o_sum, o_own, o_left, o_right,
    uh, lh, lg, ids, gates, slots_of, AG, RT, SD, R, O, W, G, PX, PG, OWN, TMP, FL, FR, FT,
    ag_s, ag_r, agf_s, agf_r, rt_s, rt_r, s2_s, s2_r, rb_s, rb_r,
    px_s, px_r, pg_s, pg_r, x_s, x_r, fn_s, fn_r, loc, loc_b, w_sem, in_sem, out_sem, credit, pcredit,
):
    dp = lax.axis_index("dp")
    ex = lax.axis_index("expert")
    x, c = dp // 2, dp % 2
    y, z = ex // RING, ex % RING
    a_me = (y, z)
    b_me = (z, y)

    def ydev(k):
        return (dp, ((y + k) % RING) * RING + z)

    def zdev(k):
        return (dp, y * RING + (z + k) % RING)

    def xdev(k):
        return (((x + k) % RING) * 2 + c, ex)

    a_dev = (ydev, zdev)
    b_dev = (zdev, ydev)
    partner = (x * 2 + 1 - c, ex)

    def rcopy(src, dst, ss, rs, dev):
        return pltpu.make_async_remote_copy(
            src_ref=src, dst_ref=dst, send_sem=ss, recv_sem=rs, device_id=dev, device_id_type=MESH
        )

    def load_w(j):
        return pltpu.make_async_copy(w_hbm.at[j], W, w_sem.at[0])

    barrier = pltpu.get_barrier_semaphore()
    peers = [ydev(k) for k in (1, 2, 3)] + [zdev(k) for k in (1, 2, 3)] + [xdev(1), xdev(3), partner]
    for dev in peers:
        pl.semaphore_signal(barrier, inc=1, device_id=dev, device_id_type=MESH)

    pairs = (
        (lh_in, lh), (ug_in, AG.at[1, z]), (ids_in, ids), (gates_in, gates), (slots_in, slots_of),
        (uh_in, uh), (lg_in, lg),
    )
    loads = [pltpu.make_async_copy(src, dst, in_sem.at[i]) for i, (src, dst) in enumerate(pairs)]
    for load in loads[:5]:
        load.start()
    for i in (2, 3, 4):
        loads[i].wait()
    for p in (0, 1):
        RT[p, a_me[p], 0:TOPK, :] = jnp.where(slots_of[...] < CAP, ids[...] * S + slots_of[...], -1)
        RT[p, a_me[p], 8 : 8 + TOPK, :] = gates[...]
    loads[0].wait()
    low = lh[...].astype(F32)
    scale = lax.rsqrt(jnp.mean(low * low, axis=1, keepdims=True) + NORM_EPS)
    AG[0, y] = (low * scale).astype(BF16)
    loads[1].wait()

    pl.semaphore_wait(barrier, len(peers))

    HALF = T // 2

    def rows(h):
        return pl.ds(h * HALF, HALF)

    def rt_copy(p, k):
        me = a_me[p]
        return rcopy(RT.at[p, me], RT.at[p, me], rt_s.at[p, k], rt_r.at[p, k], a_dev[p](k))

    def ag_copy(p, d, h):
        me = a_me[p]
        blk = AG.at[p, me, rows(h)]
        return rcopy(blk, blk, ag_s.at[p, d, h], ag_r.at[p, d, h], a_dev[p](1 if d == 0 else 3))

    def agf_copy(p, d):
        frm = (a_me[p] + (3 if d == 0 else 1)) % RING
        blk = AG.at[p, frm, rows(d)]
        return rcopy(blk, blk, agf_s.at[p, d], agf_r.at[p, d], a_dev[p](1 if d == 0 else 3))

    for p in (1, 0):
        for k in (1, 2, 3):
            rt_copy(p, k).start()
    for p in (1, 0):
        ag_copy(p, 0, 0).start()
        ag_copy(p, 1, 1).start()
    for p in (1, 0):
        ag_copy(p, 0, 1).start()
        ag_copy(p, 1, 0).start()
    for load in loads[5:]:
        load.start()
    load_w(0).start()

    row = lax.broadcasted_iota(jnp.int32, (T, T), 0)

    def codes_of(p, j):
        b, s = row >> 5, row & 31
        if p == 0:
            return 64 * (4 * y + b) + 32 * j + s
        return 64 * (4 * b + z) + 32 * j + s

    def onehot(p, j, a):
        val = codes_of(p, j)
        hot = jnp.zeros((T, T), F32)
        share = jnp.zeros((T, T), F32)
        for k in range(TOPK):
            m = RT[p, a, k : k + 1, :] == val
            hot = jnp.where(m, 1.0, hot)
            gate = RT[p, a, 8 + k : 9 + k, :].astype(F32) * (1.0 / GATE_DENOM)
            share = jnp.where(m, gate, share)
        return hot, share

    def gather(p, j, a):
        hot, share = onehot(p, j, a)
        hot = hot.astype(BF16)
        for n in range(4):
            cols = pl.ds(n * 512, 512)
            picked = dot_nn(hot, AG[p, a, :, cols])
            if p == 1:
                picked = picked * jnp.sum(share, axis=1, keepdims=True)
            SD[p, j, a, :, cols] = picked.astype(BF16)

    def r_rows(p, a):
        block = a * RING + z if p == 0 else y * RING + a
        return pl.ds(pl.multiple_of(block * S, S), S)

    def r_rows_of(p, a, b):
        block = a * RING + b if p == 0 else b * RING + a
        return pl.ds(pl.multiple_of(block * S, S), S)

    def slots(b):
        return pl.ds(pl.multiple_of(b * S, S), S)

    def s2_send(p, j, a):
        for k in (1, 2, 3):
            b = (b_me[p] + k) % RING
            rcopy(
                SD.at[p, j, a, slots(b)], R.at[p, j, r_rows(p, a)],
                s2_s.at[p, j, k], s2_r.at[p, j, k], b_dev[p](k),
            ).start()
        pltpu.make_async_copy(
            SD.at[p, j, a, slots(b_me[p])], R.at[p, j, r_rows(p, a)], loc.at[p, j]
        ).start()

    def s2_whole(p, j, k):
        return rcopy(SD.at[p, j, 0], R.at[p, j, pl.ds(0, T)], s2_s.at[p, j, k], s2_r.at[p, j, k], b_dev[p](k))

    def loc_whole(p, j):
        return pltpu.make_async_copy(SD.at[p, j, 0], R.at[p, j, pl.ds(0, T)], loc.at[p, j])

    for p in (1, 0):
        gather(p, 0, a_me[p])
        s2_send(p, 0, a_me[p])
    for p in (1, 0):
        ag_copy(p, 0, 0).wait_recv()
        agf_copy(p, 0).start()
        ag_copy(p, 1, 1).wait_recv()
        agf_copy(p, 1).start()
    for p in (1, 0):
        for k in (1, 2, 3):
            rt_copy(p, k).wait_recv()
    for p in (1, 0):
        ag_copy(p, 0, 1).wait_recv()
        gather(p, 0, (a_me[p] + 3) % RING)
        s2_send(p, 0, (a_me[p] + 3) % RING)
        ag_copy(p, 1, 0).wait_recv()
        gather(p, 0, (a_me[p] + 1) % RING)
        s2_send(p, 0, (a_me[p] + 1) % RING)
    for p in (1, 0):
        agf_copy(p, 0).wait_recv()
        agf_copy(p, 1).wait_recv()
        gather(p, 0, (a_me[p] + 2) % RING)
        s2_send(p, 0, (a_me[p] + 2) % RING)

    def gather_later(a, carry):
        for p in (1, 0):
            gather(p, 1, a)
        return carry

    lax.fori_loop(0, RING, gather_later, 0)
    for p in (1, 0):
        for k in (1, 2, 3):
            rt_copy(p, k).wait_send()
        for d in (0, 1):
            for h in (0, 1):
                ag_copy(p, d, h).wait_send()
            agf_copy(p, d).wait_send()

    def s2_sent(j):
        for p in (0, 1):
            for k in (1, 2, 3):
                s2_whole(p, j, k).wait_send()
            loc_whole(p, j).wait()
        for p in (0, 1):
            for k in (1, 2, 3):
                pl.semaphore_signal(credit.at[j], inc=1, device_id=b_dev[p](k), device_id_type=MESH)

    s2_sent(0)

    def send_later(a, carry):
        for p in (1, 0):
            s2_send(p, 1, a)
        return carry

    lax.fori_loop(0, RING, send_later, 0)

    def px_copy(p, j, b):
        src = R.at[p, j, :, pl.ds(pl.multiple_of(b * 512 + (1 - c) * SHARE, SHARE), SHARE)]
        return rcopy(src, PX.at[p, :, pl.ds(b * SHARE, SHARE)], px_s.at[p], px_r.at[p], partner)

    def px_whole(p):
        half = R.at[p, 0, :, pl.ds(0, 4 * SHARE)]
        return rcopy(half, PX.at[p], px_s.at[p], px_r.at[p], partner)

    def pg_copy(cols):
        return rcopy(G.at[:, cols], PG.at[:, cols], pg_s, pg_r, partner)

    pg_whole = rcopy(G, PG, pg_s, pg_r, partner)

    def hidden_part(j):
        for p in (0, 1):
            for k in (1, 2, 3):
                s2_whole(p, j, k).wait_recv()
        if j == 1:
            pl.semaphore_wait(pcredit, 1)
        for p in (0, 1):
            for b in range(RING):
                px_copy(p, j, b).start()
        load_w(j).wait()

        def tile(n, carry):
            at = [pl.ds(pl.multiple_of(i * H + n * 256, 256), 256) for i in range(3)]
            gate = dot_nn(R[0, j], W[:, at[0]])
            up = dot_nn(R[0, j], W[:, at[1]])
            grad = dot_nn(R[1, j], W[:, at[2]])
            sig = jax.nn.sigmoid(gate)
            act = gate * sig
            G[:, at[2]] = (act * up).astype(BF16)
            G[:, at[0]] = (grad * up * sig * (1.0 + gate * (1.0 - sig))).astype(BF16)
            G[:, at[1]] = (grad * act).astype(BF16)
            for i in range(3):
                pg_copy(at[i]).start()
            return carry

        lax.fori_loop(0, 3, tile, 0)

    def outputs_part(j, out, route):
        def tile(n, carry):
            at = pl.ds(pl.multiple_of(n * 512, 512), 512)
            out[:, at] = dot_nt(G[:, 2 * H :], W[at, 2 * H :]).astype(BF16)
            route[:, at] = dot_nt(G[:, : 2 * H], W[at, : 2 * H]).astype(BF16)
            return carry

        lax.fori_loop(0, D // 512, tile, 0)

    def weight_block(j, b, dst):
        mine = pl.ds(pl.multiple_of(b * 512 + c * SHARE, SHARE), SHARE)
        theirs = pl.ds(pl.multiple_of(b * SHARE, SHARE), SHARE)

        def tile(p, first, count):
            def body(n, carry):
                at = pl.ds(pl.multiple_of(first + n * H, H), H)
                acc = dot_tn(R[p, j, :, mine], G[:, at])
                acc = acc + dot_tn(PX[p, :, theirs], PG[:, at])
                dst[:, at] = acc.astype(BF16)
                return carry

            lax.fori_loop(0, count, body, 0)

        tile(0, 0, 2)
        tile(1, 2 * H, 1)

    AH = pl.ds(0, SHARE // 2)
    BH = pl.ds(SHARE // 2, SHARE // 2)

    def x_copy(j, own, d, i):
        to = xdev(1 if d == 0 else 3)
        near = own((x + (1 if d == 0 else 3)) % RING)
        far = own((x + 2) % RING)
        early, late = (AH, BH) if d == 0 else (BH, AH)
        fin = (o_left, o_right)[d].at[j]
        if i == 0:
            src, dst = far.at[early], TMP.at[j, d]
        elif i == 1:
            src, dst = near.at[late], fin.at[late]
        else:
            src, dst = near.at[early], fin.at[early]
        return rcopy(src, dst, x_s.at[j, d, i], x_r.at[j, d, i], to)

    def weight_far(j, own):
        for p in (0, 1):
            px_whole(p).wait_recv()
        pg_whole.wait_recv()
        weight_block(j, (x + 2) % RING, own((x + 2) % RING))
        x_copy(j, own, 0, 0).start()
        x_copy(j, own, 1, 0).start()

    def weight_near(j, own, d):
        b = (x + (1 if d == 0 else 3)) % RING
        weight_block(j, b, own(b))
        x_copy(j, own, d, 1).start()

    def weight_own(j, own):
        weight_block(j, x, own(x))

    def partner_sent():
        for p in (0, 1):
            px_whole(p).wait_send()
        pg_whole.wait_send()

    def x_add(j, own):
        for d in (0, 1):
            early = AH if d == 0 else BH
            near = own((x + (1 if d == 0 else 3)) % RING)
            x_copy(j, own, d, 0).wait_recv()
            near[early, :] = (near[early, :].astype(F32) + TMP[j, d].astype(F32)).astype(BF16)
            x_copy(j, own, d, 2).start()

    def x_arrived(j, own):
        for d in (0, 1):
            for i in (1, 2):
                x_copy(j, own, d, i).wait_recv()

    def x_sent(j, own):
        for d in (0, 1):
            for i in range(3):
                x_copy(j, own, d, i).wait_send()

    def own0(b):
        return OWN.at[b]

    def own1(b):
        return W.at[pl.ds(pl.multiple_of(b * SHARE, SHARE), SHARE)]

    OFFS = (2, 1, 3, 0)

    def back(j, i):
        for p in (0, 1):
            a = (a_me[p] + OFFS[i]) % RING
            for k in (1, 2, 3):
                b = (b_me[p] + k) % RING
                rcopy(
                    O.at[p, j, r_rows_of(p, a, b)], SD.at[p, j, a, slots(b_me[p])],
                    rb_s.at[p, j, k], rb_r.at[p, j, i], b_dev[p](k),
                ).start()
            pltpu.make_async_copy(
                O.at[p, j, r_rows(p, a)], SD.at[p, j, a, slots(b_me[p])], loc_b.at[p, j, i]
            ).start()

    def back_arrived(p, j, i):
        rcopy(
            O.at[p, j, pl.ds(0, 3 * S)], SD.at[p, j, 0, pl.ds(0, 3 * S)],
            rb_s.at[p, j, 1], rb_r.at[p, j, i], b_dev[p](1),
        ).wait_recv()
        pltpu.make_async_copy(
            O.at[p, j, pl.ds(0, S)], SD.at[p, j, 0, pl.ds(0, S)], loc_b.at[p, j, i]
        ).wait()

    def back_sent(p, j, k):
        rcopy(
            O.at[p, j, pl.ds(0, T)], SD.at[p, j, 0], rb_s.at[p, j, k], rb_r.at[p, j, 0], b_dev[p](k)
        ).wait_send()

    hidden_part(0)
    weight_far(0, own0)
    outputs_part(0, O.at[0, 0], O.at[1, 0])
    load_w(1).start()
    pl.semaphore_wait(credit.at[0], 6)
    for i in range(RING):
        back(0, i)
    weight_near(0, own0, 0)
    weight_near(0, own0, 1)
    weight_own(0, own0)
    pl.semaphore_signal(pcredit, inc=1, device_id=partner, device_id_type=MESH)
    partner_sent()
    s2_sent(1)
    hidden_part(1)
    x_add(0, own0)
    outputs_part(1, O.at[0, 1], O.at[1, 1])
    pl.semaphore_wait(credit.at[1], 6)
    back(1, 0)
    weight_far(1, own1)
    back(1, 1)
    weight_near(1, own1, 0)
    back(1, 2)
    weight_near(1, own1, 1)
    back(1, 3)
    weight_own(1, own1)
    partner_sent()

    own_out = pltpu.make_async_copy(own1(x), o_own, out_sem.at[1])
    own_out.start()
    pieces = [
        pltpu.make_async_copy(src.at[0], G.at[pl.ds(d * SHARE, SHARE)], w_sem.at[1 + d])
        for d, src in enumerate((o_left, o_right))
    ]
    sum_out = pltpu.make_async_copy(G.at[pl.ds(0, SHARE)], o_sum, out_sem.at[0])

    def fetch_pieces():
        x_arrived(0, own0)
        for piece in pieces:
            piece.start()

    def sum0():
        for piece in pieces:
            piece.wait()
        G[0:SHARE, :] = (
            own0(x)[...].astype(F32)
            + G[0:SHARE, :].astype(F32)
            + G[SHARE : 2 * SHARE, :].astype(F32)
        ).astype(BF16)
        sum_out.start()

    def fn_copy(p, d, i):
        to = a_dev[p](1 if d == 0 else 3)
        near = (a_me[p] + (1 if d == 0 else 3)) % RING
        far = (a_me[p] + 2) % RING
        fin = FL if d == 0 else FR
        early, late = rows(d), rows(1 - d)
        if i == 0:
            src, dst = AG.at[p, far, early], FT.at[p, d]
        elif i == 1:
            src, dst = AG.at[p, near, late], fin.at[p, late]
        else:
            src, dst = AG.at[p, near, early], fin.at[p, early]
        return rcopy(src, dst, fn_s.at[p, d, i], fn_r.at[p, d, i], to)

    def combine(p, a):
        parts = []
        for j in (0, 1):
            hot, share = onehot(p, j, a)
            if p == 0:
                top = share.astype(BF16)
                parts.append((j, top))
                parts.append((j, (share - top.astype(F32)).astype(BF16)))
            else:
                parts.append((j, hot.astype(BF16)))
        for n in range(4):
            cols = pl.ds(n * 512, 512)
            total = jnp.zeros((T, 512), F32)
            for j, weights in parts:
                total = total + dot_tn(weights, SD[p, j, a, :, cols])
            AG[p, a, :, cols] = total.astype(BF16)

    for i in range(RING):
        if i == 3:
            for p in (0, 1):
                for d in (0, 1):
                    near = (a_me[p] + (1 if d == 0 else 3)) % RING
                    early = rows(d)
                    fn_copy(p, d, 0).wait_recv()
                    AG[p, near, early, :] = (
                        AG[p, near, early, :].astype(F32) + FT[p, d].astype(F32)
                    ).astype(BF16)
                    fn_copy(p, d, 2).start()
            x_add(1, own1)
        for p in (0, 1):
            for j in (0, 1):
                back_arrived(p, j, i)
            combine(p, (a_me[p] + OFFS[i]) % RING)
            if i == 0:
                fn_copy(p, 0, 0).start()
                fn_copy(p, 1, 0).start()
            elif i < 3:
                fn_copy(p, i - 1, 1).start()
        if i == 0:
            fetch_pieces()
        if i == 1:
            sum0()

    def fn_arrived(p):
        for d in (0, 1):
            for i in (1, 2):
                fn_copy(p, d, i).wait_recv()

    results = [
        pltpu.make_async_copy(src, dst, out_sem.at[2 + p]) for p, (src, dst) in enumerate(((uh, o_up), (lg, o_lo)))
    ]
    loads[5].wait()
    loads[6].wait()
    low = lh[...].astype(F32)
    scale = lax.rsqrt(jnp.mean(low * low, axis=1, keepdims=True) + NORM_EPS)
    fn_arrived(0)
    mixture = AG[0, y].astype(F32) + FL[0].astype(F32) + FR[0].astype(F32)
    uh[...] = (uh[...].astype(F32) - mixture).astype(BF16)
    results[0].start()
    fn_arrived(1)
    grad_normed = AG[1, z].astype(F32) + FL[1].astype(F32) + FR[1].astype(F32)
    low = lh[...].astype(F32)
    inner = jnp.mean(low * grad_normed, axis=1, keepdims=True)
    lg[...] = (
        lg[...].astype(F32) + scale * grad_normed - low * (scale * scale * scale) * inner
    ).astype(BF16)
    results[1].start()
    x_arrived(1, own1)

    for p in (0, 1):
        for d in (0, 1):
            for i in range(3):
                fn_copy(p, d, i).wait_send()
        for j in (0, 1):
            for k in (1, 2, 3):
                back_sent(p, j, k)
    x_sent(0, own0)
    x_sent(1, own1)
    for copy in results + [own_out, sum_out]:
        copy.wait()


def run(*arrays):
    hbm = pl.BlockSpec(memory_space=pl.ANY)
    dma = pltpu.SemaphoreType.DMA
    half = jax.ShapeDtypeStruct((SHARE, F), BF16)
    both = jax.ShapeDtypeStruct((2, SHARE, F), BF16)
    rows = jax.ShapeDtypeStruct((T, D), BF16)
    return pl.pallas_call(
        kernel,
        out_shape=(rows, rows, half, half, both, both),
        in_specs=[hbm] * 8,
        out_specs=(hbm,) * 6,
        scratch_shapes=[
            pltpu.VMEM((T, D), BF16),
            pltpu.VMEM((T, D), BF16),
            pltpu.VMEM((T, D), BF16),
            pltpu.VMEM((TOPK, T), jnp.int32),
            pltpu.VMEM((TOPK, T), jnp.int32),
            pltpu.VMEM((TOPK, T), jnp.int32),
            pltpu.VMEM((2, RING, T, D), BF16),
            pltpu.VMEM((2, RING, 16, T), jnp.int32),
            pltpu.VMEM((2, 2, RING, T, D), BF16),
            pltpu.VMEM((2, 2, M, D), BF16),
            pltpu.VMEM((2, 2, M, D), BF16),
            pltpu.VMEM((D, F), BF16),
            pltpu.VMEM((M, F), BF16),
            pltpu.VMEM((2, M, 4 * SHARE), BF16),
            pltpu.VMEM((M, F), BF16),
            pltpu.VMEM((RING, SHARE, F), BF16),
            pltpu.VMEM((2, 2, SHARE // 2, F), BF16),
            pltpu.VMEM((2, T, D), BF16),
            pltpu.VMEM((2, T, D), BF16),
            pltpu.VMEM((2, 2, T // 2, D), BF16),
            dma((2, 2, 2)), dma((2, 2, 2)),
            dma((2, 2)), dma((2, 2)),
            dma((2, 4)), dma((2, 4)),
            dma((2, 2, 4)), dma((2, 2, 4)),
            dma((2, 2, 4)), dma((2, 2, 4)),
            dma((2,)), dma((2,)),
            dma, dma,
            dma((2, 2, 3)), dma((2, 2, 3)),
            dma((2, 2, 3)), dma((2, 2, 3)),
            dma((2, 2)),
            dma((2, 2, 4)),
            dma((3,)),
            dma((7,)),
            dma((4,)),
            pltpu.SemaphoreType.REGULAR((2,)),
            pltpu.SemaphoreType.REGULAR,
        ],
        compiler_params=pltpu.CompilerParams(
            collective_id=0, has_side_effects=True, vmem_limit_bytes=63 * 1024 * 1024
        ),
        cost_estimate=pl.CostEstimate(
            flops=29_000_000_000, bytes_accessed=30_000_000, transcendentals=800_000
        ),
    )(*arrays)


PIECES = 8


def finish_kernel(up, lo, total, own, left, right, o_up, o_lo, o_weight, parts, wide, tok, tok_sem, in_sem, out_sem):
    per = PIECES // 2
    tall = SHARE // per
    loads = []
    for q in range(PIECES):
        at = pl.ds((q % per) * tall, tall)
        srcs = (total.at[at],) if q < per else (own.at[at], left.at[1, at], right.at[1, at])
        loads.append([
            pltpu.make_async_copy(src, parts.at[q, i], in_sem.at[q, i]) for i, src in enumerate(srcs)
        ])
    fetched = [pltpu.make_async_copy(src, tok.at[i], tok_sem.at[i, 0]) for i, src in enumerate((up, lo))]
    passed = [pltpu.make_async_copy(tok.at[i], dst, tok_sem.at[i, 1]) for i, dst in enumerate((o_up, o_lo))]
    for load in loads[0] + fetched + sum(loads[1:], []):
        load.start()
    stores = []
    for q in range(PIECES):
        for load in loads[q]:
            load.wait()
        value = parts[q, 0].astype(F32)
        if q >= per:
            value = value + parts[q, 1].astype(F32) + parts[q, 2].astype(F32)
        wide[q] = value
        store = pltpu.make_async_copy(wide.at[q], o_weight.at[q // per, pl.ds((q % per) * tall, tall)], out_sem.at[q])
        store.start()
        stores.append(store)
        if q < 2:
            fetched[q].wait()
            passed[q].start()
    for copy in passed + stores:
        copy.wait()


def finish(*arrays):
    hbm = pl.BlockSpec(memory_space=pl.ANY)
    dma = pltpu.SemaphoreType.DMA
    return pl.pallas_call(
        finish_kernel,
        out_shape=(
            jax.ShapeDtypeStruct((T, D), BF16),
            jax.ShapeDtypeStruct((T, D), BF16),
            jax.ShapeDtypeStruct((2, SHARE, F), F32),
        ),
        in_specs=[hbm] * 6,
        out_specs=(hbm,) * 3,
        scratch_shapes=[
            pltpu.VMEM((PIECES, 3, 2 * SHARE // PIECES, F), BF16),
            pltpu.VMEM((PIECES, 2 * SHARE // PIECES, F), F32),
            pltpu.VMEM((2, T, D), BF16),
            dma((2, 2)), dma((PIECES, 3)), dma((PIECES,)),
        ],
        compiler_params=pltpu.CompilerParams(vmem_limit_bytes=60 * 1024 * 1024),
        cost_estimate=pl.CostEstimate(flops=3_000_000, bytes_accessed=11_500_000, transcendentals=0),
    )(*arrays)


def shards(
    upper_half, lower_half, upper_grad, lower_grad, expert_ids, gate_weights, route_slots, expert_weight
):
    return finish(*run(
        upper_half, lower_half, upper_grad, lower_grad,
        expert_ids.T, gate_weights.T, route_slots.T, expert_weight,
    ))


def solution(mesh):
    tok = P(("dp", "expert"), None)
    return jax.shard_map(
        shards,
        mesh=mesh,
        in_specs=(tok,) * 7 + (P("expert", None, None),),
        out_specs=(tok, tok, P("expert", "dp", None)),
        check_vma=False,
    )
```
